32 devices in a mesh: grp: 2 (over x), lat: 16 (over z, y, core).
Axes of the slice: x: 2, y: 2, z: 4, core: 2. Of those that a mesh axis runs over, the one named last changes fastest.
Arguments:
- noisy_state: bfloat16 [160, 128, 1024], P('grp', 'lat'), parts along dimension 0, may hold values from -6 to 6
- w_first: bfloat16 [3, 3, 80, 80], replicated, may hold values from -0.21875 to 0.21875
- w_second: bfloat16 [3, 3, 80, 80], replicated, may hold values from -0.21875 to 0.21875
- prior_weight: float32 [80], replicated, may hold values from 0.5 to 2
- obs_weight: float32 [80], replicated, may hold values from 0.5 to 2
- block_route: int32 [32, 9], P(('grp', 'lat')), parts along dimension 0, may hold values from 0 to 31
- counts: int32 [32, 9], P(('grp', 'lat')), parts along dimension 0, may hold values from 0 to 128, as said below
- tile_weights: bfloat16 [32, 9, 128, 256], P(('grp', 'lat')), parts along dimension 0, may hold values from -0.375 to 0.375
- observations: bfloat16 [32, 9, 80, 128], P(('grp', 'lat')), parts along dimension 0, may hold values from -6 to 6
Outputs:
- posterior_score: bfloat16 [160, 128, 1024], P('grp', 'lat'), parts along dimension 0
The draws below stay inside these ranges and needn't reach their ends.
There are 2 independent parts, one for each index of `grp`. The reference program is written for one: setup_inputs(seed, part) draws one part's arguments, and reference() takes and returns one part's arrays. A program takes and returns all parts, laid end to end along the dimension named above; an argument that names none is the same for every part. Nothing has to cross between parts.
Inputs may be any that keep to these rules, and one draw needn't show every extreme that they name: counts[o, k] tells how many of tile k's first retrievals are live; it is 0 where band o - k + 4 lies outside the grid; owners carry uneven numbers of live tiles.
All inputs are finite; a program needn't handle non-finite values.
Results may differ from the reference program's by a relative error of at most 0.0058.
Values may be sent and summed in bfloat16 or wider, within the bound.
No kernel may reach another device: no remote copies, remote signals or barrier semaphores. Data moves between devices by JAX's collectives and lax.ppermute only.
A program may use at most 64 MiB of HBM per device.

```python
import math
import jax
import jax.numpy as jnp
from jax import lax

C = 80
LAT_DEV = 8
NLON = 1024
BLK_LAT = 2
BLK_LON = 128
TOBS = 128
SPAN = 4
NOFF = 9
NBLK = 32
NLAT = 128
N_LAT = 16


def draw_counts(key, part):
    key = jax.random.fold_in(key, 11)
    key_one, key_two, key_three, key_four = jax.random.split(key, 4)
    owners = jnp.arange(N_LAT, dtype=jnp.int32)[:, None]
    offsets = jnp.arange(NOFF, dtype=jnp.int32)[None, :]
    source = owners - offsets + SPAN
    inside = (source >= 0) & (source < N_LAT)
    busyness = jax.random.randint(key_one, (N_LAT, 1), 0, 4)
    chance = jax.random.randint(key_two, (N_LAT, NOFF), 0, 4)
    amount = jax.random.randint(key_three, (N_LAT, NOFF), 1, TOBS + 1)
    result = jnp.where(inside & (chance <= busyness), amount, 0)
    chosen_owner = jax.random.randint(key_four, (), 0, N_LAT)
    result = jnp.where((owners == chosen_owner) & (offsets == SPAN), TOBS, result)
    return result.astype(jnp.int32)


def set_ends(values, rng, least, top_value):
    longest = values.shape.index(max(values.shape))
    spots = []
    for shift in (0, 1):
        where = [jax.random.randint(jax.random.fold_in(rng, axis), (), 0, length) for axis, length in enumerate(values.shape)]
        where[longest] = (where[longest] + shift) % values.shape[longest]
        spots.append(tuple(where))
    return values.at[spots[0]].set(least).at[spots[1]].set(top_value)


def block_levels(stream_key, extent, pieces, smallest, largest):
    gain = 1.0
    for position, parts in pieces:
        steps = jax.random.uniform(jax.random.fold_in(jax.random.fold_in(stream_key, 6), position), (parts,), jnp.float32, smallest / len(pieces), largest / len(pieces))
        gain = gain * jnp.repeat(jnp.exp(steps), extent[position] // parts).reshape((-1,) + (1,) * (len(extent) - 1 - position))
    return gain


def bell_draw(own_key, extent, deviation, bound, cuts=(), kind=jnp.bfloat16):
    loudness = block_levels(own_key, extent, cuts, -0.22, 0.18) if cuts else 1.0
    values = jax.random.normal(own_key, extent, jnp.float32) * deviation * loudness
    return jnp.minimum(jnp.maximum(values, -bound), bound).astype(kind)


def setup_inputs(seed: int = 0, part: int = 0) -> dict:
    key_of = jax.random.split(jax.random.key(seed), 10)
    own_keys = jax.random.split(jax.random.fold_in(key_of[9], part), 10)
    return {
        "noisy_state": bell_draw(own_keys[0], (C, NLAT, NLON), 1.0, 6.0, ((1, 16),)),
        "w_first": bell_draw(key_of[1], (3, 3, C, C), (9 * C) ** -0.5, 0.21875),
        "w_second": bell_draw(key_of[2], (3, 3, C, C), (9 * C) ** -0.5, 0.21875),
        "prior_weight": jnp.clip(jnp.exp(jax.random.uniform(key_of[3], (C,), jnp.float32, math.log(0.5), math.log(2.0))), 0.5, 2.0),
        "obs_weight": jnp.clip(jnp.exp(jax.random.uniform(key_of[4], (C,), jnp.float32, math.log(0.5), math.log(2.0))), 0.5, 2.0),
        "block_route": set_ends(jax.random.randint(own_keys[5], (N_LAT, NOFF), 0, NBLK), jax.random.fold_in(own_keys[5], 1), 0, NBLK - 1).astype(jnp.int32),
        "counts": draw_counts(jax.random.fold_in(jax.random.fold_in(key_of[9], part), 71), part),
        "tile_weights": bell_draw(own_keys[7], (N_LAT, NOFF, TOBS, BLK_LAT * BLK_LON), (BLK_LAT * BLK_LON) ** -0.5, 0.375, ((0, 16),)),
        "observations": bell_draw(own_keys[8], (N_LAT, NOFF, C, TOBS), 1.0, 6.0, ((0, 16),)),
    }


def pad_rows(grid_field):
    return jnp.pad(grid_field, ((0, 0), (1, 1), (0, 0)))


def conv_rows(weights, padded):
    height = padded.shape[1] - 2
    accumulated = jnp.zeros((weights.shape[2], height, padded.shape[2]), jnp.float32)
    for row_step in range(3):
        stripe = padded[:, row_step:row_step + height, :].astype(jnp.float32)
        for col_step in range(3):
            shifted = jnp.roll(stripe, 1 - col_step, axis=2)
            accumulated = accumulated + jnp.einsum("oc,crl->orl", weights[row_step, col_step].astype(jnp.float32), shifted)
    return accumulated


def conv_back(weights, padded):
    height = padded.shape[1] - 2
    accumulated = jnp.zeros((weights.shape[3], height, padded.shape[2]), jnp.float32)
    for row_step in range(3):
        stripe = padded[:, 2 - row_step:2 - row_step + height, :].astype(jnp.float32)
        for col_step in range(3):
            shifted = jnp.roll(stripe, col_step - 1, axis=2)
            accumulated = accumulated + jnp.einsum("oc,orl->crl", weights[row_step, col_step].astype(jnp.float32), shifted)
    return accumulated


def to_blocks(grid_field):
    shaped = grid_field.reshape(C, N_LAT, LAT_DEV // BLK_LAT, BLK_LAT, NLON // BLK_LON, BLK_LON)
    return shaped.transpose(1, 2, 4, 0, 3, 5).reshape(N_LAT * NBLK, C, BLK_LAT * BLK_LON)


def from_blocks(blocks):
    shaped = blocks.reshape(N_LAT, LAT_DEV // BLK_LAT, NLON // BLK_LON, C, BLK_LAT, BLK_LON)
    return shaped.transpose(3, 0, 1, 4, 2, 5).reshape(C, NLAT, NLON)


def reference(noisy_state, w_first, w_second, prior_weight, obs_weight, block_route, counts, tile_weights, observations):
    activation = conv_rows(w_first, pad_rows(noisy_state))
    hidden = jax.nn.silu(activation).astype(jnp.bfloat16)
    residual_branch = conv_rows(w_second, pad_rows(hidden))
    denoised = (noisy_state.astype(jnp.float32) + residual_branch).astype(jnp.bfloat16)
    blocks = to_blocks(denoised)
    owners = jnp.arange(N_LAT, dtype=jnp.int32)[:, None]
    offsets = jnp.arange(NOFF, dtype=jnp.int32)[None, :]
    source = jnp.clip(owners - offsets + SPAN, 0, N_LAT - 1).astype(jnp.int32)
    block_ids = (source * NBLK + block_route[source, offsets]).astype(jnp.int32)
    slot_index = jnp.arange(TOBS, dtype=jnp.int32)

    def per_owner(member):
        tile_ids, weights, values, tile_counts = member
        picked = blocks[tile_ids].astype(jnp.float32)
        weights_wide = weights.astype(jnp.float32)
        predicted = jnp.einsum("tcb,tob->tco", picked, weights_wide)
        live_mask = slot_index[None, None, :] < tile_counts[:, None, None]
        misfit = jnp.where(live_mask, (values.astype(jnp.float32) - predicted) * obs_weight[None, :, None], 0.0).astype(jnp.bfloat16)
        return jnp.einsum("tco,tob->tcb", misfit.astype(jnp.float32), weights_wide).astype(jnp.bfloat16)

    tile_terms = lax.map(per_owner, (block_ids, tile_weights, observations, counts))
    block_sums = jnp.zeros((N_LAT * NBLK, C, BLK_LAT * BLK_LON), jnp.float32)
    block_sums = block_sums.at[block_ids.reshape(-1)].add(tile_terms.reshape(-1, C, BLK_LAT * BLK_LON).astype(jnp.float32))
    guidance = from_blocks(block_sums)
    guide_low = guidance.astype(jnp.bfloat16)
    sigmoid_value = jax.nn.sigmoid(activation)
    derivative = sigmoid_value * (1.0 + activation * (1.0 - sigmoid_value))
    adjoint_hidden = (derivative * conv_back(w_second, pad_rows(guide_low))).astype(jnp.bfloat16)
    back_first = conv_back(w_first, pad_rows(adjoint_hidden))
    posterior_score = prior_weight[:, None, None] * residual_branch + guidance + back_first
    return posterior_score.astype(jnp.bfloat16)
```

```python
import functools

import jax
import jax.numpy as jnp
from jax import lax
from jax.experimental import pallas as pl
from jax.experimental.pallas import tpu as pltpu
from jax.sharding import PartitionSpec as P

BLK_LAT = 2
BLK_LON = 128
HALO = 2
F32 = jnp.float32
BF16 = jnp.bfloat16

VM = pl.BlockSpec(memory_space=pltpu.VMEM)
SM = pl.BlockSpec(memory_space=pltpu.SMEM)


def params(mib=40):
    return pltpu.CompilerParams(vmem_limit_bytes=mib << 20)


def rows(index, count, channels):
    return pl.ds(pl.multiple_of(index * channels, 16), count * channels)


def permutation(height, group):
    n = height * group
    out = lax.broadcasted_iota(jnp.int32, (n, n), 0)
    src = lax.broadcasted_iota(jnp.int32, (n, n), 1)
    want = (out % group) * height + out // group
    return jnp.where(src == want, 1.0, 0.0).astype(BF16)


def back_permutation(height, group):
    n = height * group
    out = lax.broadcasted_iota(jnp.int32, (n, n), 0)
    src = lax.broadcasted_iota(jnp.int32, (n, n), 1)
    want = (out % height) * group + out // height
    return jnp.where(src == want, 1.0, 0.0).astype(BF16)


def channel_groups(channels):
    groups, start = [], 0
    while start < channels:
        size = min(32, channels - start)
        groups.append((start, size))
        start += size
    return groups


def pack_tile(k, dst, w_ref, obs_ref, count_ref, slots, channels):
    live = lax.broadcasted_iota(jnp.int32, (slots, BLK_LON), 0) < count_ref[k]
    zero = jnp.zeros((slots, BLK_LON), BF16)
    for i in range(BLK_LAT):
        half = w_ref[k, :, i * BLK_LON : (i + 1) * BLK_LON]
        dst[i * slots : (i + 1) * slots, :] = jnp.where(live, half, zero)
    dst[BLK_LAT * slots : BLK_LAT * slots + channels, :] = obs_ref[k]


def prepare_kernel(
    channels, height, span,
    where_ref, count_ref, x_ref, w_ref, obs_ref,
    xt_ref, ha_ref, hb_ref, za_ref, zb_ref, own_ref,
):
    for start, size in channel_groups(channels):
        n = size * height
        moved = jnp.dot(
            permutation(height, size),
            x_ref[start * height : start * height + n, :],
            preferred_element_type=F32,
        ).astype(BF16)
        for r in range(height):
            xt_ref[r * channels + start : r * channels + start + size, :] = (
                moved[r * size : (r + 1) * size, :]
            )
    odd = where_ref[0] % 2
    last = height - HALO
    ha_ref[...] = xt_ref[rows(last * (1 - odd), HALO, channels), :]
    hb_ref[...] = xt_ref[rows(last * odd, HALO, channels), :]
    slots = w_ref.shape[1]
    p = where_ref[0] % span
    z_odd = (where_ref[0] // span) % 2
    pack = functools.partial(
        pack_tile, w_ref=w_ref, obs_ref=obs_ref, count_ref=count_ref, slots=slots, channels=channels
    )
    for j in range(span):
        up = jnp.maximum(p - j, 0)
        down = jnp.minimum(2 * span + p - j, 2 * span)
        pack(jnp.where(z_odd == 1, down, up), za_ref.at[j])
        pack(jnp.where(z_odd == 1, up, down), zb_ref.at[j])
        if j == 0:
            pack(span, own_ref.at[0])
        else:
            pack(span + p - lax.bitwise_xor(p, j), own_ref.at[j])


def relay_kernel(span, where_ref, za_ref, zb_ref, own_ref, *outs):
    p = where_ref[0] % span
    z_odd = (where_ref[0] // span) % 2
    for m in range(1, span):
        to = lax.bitwise_xor(p, m)
        below = jnp.where(to < p, 1, 0)
        outs[m - 1][0] = own_ref[m]

        @pl.when(below == z_odd)
        def _():
            outs[m - 1][1] = za_ref[to]

        @pl.when(below != z_odd)
        def _():
            outs[m - 1][1] = zb_ref[to]


def conv_row(w_ref, src_ref, index, channels):
    depth = w_ref.shape[1]
    window = src_ref[pl.ds(pl.multiple_of(index * channels, 16), depth), :]
    taps = jnp.dot(w_ref[...], window, preferred_element_type=F32)
    width = taps.shape[1]
    return (
        pltpu.roll(taps[0:channels], 1, 1)
        + taps[channels : 2 * channels]
        + pltpu.roll(taps[2 * channels : 3 * channels], width - 1, 1)
    )


def fill(ext, mid, a_ref, b_ref, where_ref, channels, height):
    odd = where_ref[0] % 2
    ext[HALO * channels : (HALO + height) * channels, :] = mid
    top = jnp.where(odd == 1, 0, HALO + height)
    ext[rows(top, HALO, channels), :] = a_ref[...]
    ext[rows(HALO + height - top, HALO, channels), :] = b_ref[...]
    tail = (2 * HALO + height) * channels
    if ext.shape[0] > tail:
        ext[tail:, :] = jnp.zeros((ext.shape[0] - tail, ext.shape[1]), BF16)


def forward_kernel(
    channels, height,
    where_ref, xt_ref, a_ref, b_ref, w1_ref, w2_ref,
    res_ref, slope_ref,
    ext, hid,
):
    fill(ext, xt_ref[...], a_ref, b_ref, where_ref, channels, height)
    me, count = where_ref[0], where_ref[1]
    tail = (height + 2) * channels
    hid[tail:, :] = jnp.zeros((hid.shape[0] - tail, hid.shape[1]), BF16)

    def first(e, _):
        act = conv_row(w1_ref, ext, e, channels)
        off = ((e == 0) & (me == 0)) | ((e == height + 1) & (me == count - 1))
        keep = jnp.where(off, 0.0, 1.0)
        gate = keep / (1.0 + jnp.exp(-act))
        hid[rows(e, 1, channels), :] = (act * gate).astype(BF16)
        slope_ref[rows(e, 1, channels), :] = gate * (1.0 + act * (1.0 - gate))
        return 0

    lax.fori_loop(0, height + 2, first, 0)

    def second(r, _):
        res_ref[rows(r, 1, channels), :] = conv_row(w2_ref, hid, r, channels)
        return 0

    lax.fori_loop(0, height, second, 0)


def tile_kernel(
    channels, height, columns, span,
    where_ref, route_ref, xt_ref, res_ref, ow_ref, own_ref, za_ref, zb_ref, p1_ref, p2_ref, p3_ref,
    guide_ref, ga_ref, gb_ref,
):
    slots = BLK_LON
    across = columns // BLK_LON
    p = where_ref[0] % span
    z_odd = (where_ref[0] // span) % 2
    odd = where_ref[0] % 2
    guide_ref[...] = jnp.zeros_like(guide_ref)
    jobs = [
        (span, own_ref.at[0]),
        (jnp.where(z_odd == 1, 0, 2 * span), za_ref.at[p]),
        (jnp.where(z_odd == 1, 2 * span, 0), zb_ref.at[p]),
    ]
    for m, ref in ((1, p1_ref), (2, p2_ref), (3, p3_ref)):
        other = lax.bitwise_xor(p, m)
        step = other - p
        jobs.append((span + step, ref.at[0]))
        jobs.append((jnp.where(step > 0, step, 2 * span + step), ref.at[1]))
    obs_weight = ow_ref[...]
    places = []
    terms = []
    for k, ref in jobs:
        n = route_ref[k]
        r, q = n // across, n % across
        place = [
            (rows(r * BLK_LAT + i, 1, channels), pl.ds(pl.multiple_of(q * BLK_LON, BLK_LON), BLK_LON))
            for i in range(BLK_LAT)
        ]
        predicted = jnp.zeros((channels, slots), F32)
        for i in range(BLK_LAT):
            block = (xt_ref[place[i]].astype(F32) + res_ref[place[i]]).astype(BF16)
            predicted += lax.dot_general(
                block,
                ref[i * slots : (i + 1) * slots, :],
                (((1,), (1,)), ((), ())),
                preferred_element_type=F32,
            )
        obs = ref[BLK_LAT * slots : BLK_LAT * slots + channels, :].astype(F32)
        misfit = ((obs - predicted) * obs_weight).astype(BF16)
        places.append(place)
        terms.append(
            [
                jnp.dot(misfit, ref[i * slots : (i + 1) * slots, :], preferred_element_type=F32)
                .astype(BF16)
                .astype(F32)
                for i in range(BLK_LAT)
            ]
        )
    for place, term in zip(places, terms):
        for i in range(BLK_LAT):
            guide_ref[place[i]] += term[i]
    last = height - HALO
    ga_ref[...] = guide_ref[rows(last * (1 - odd), HALO, channels), :].astype(BF16)
    gb_ref[...] = guide_ref[rows(last * odd, HALO, channels), :].astype(BF16)


def backward_kernel(
    channels, height,
    where_ref, guide_ref, a_ref, b_ref, slope_ref, res_ref, prior_ref, w2_ref, w1_ref,
    out_ref,
    ext, adj, score,
):
    fill(ext, guide_ref[...].astype(BF16), a_ref, b_ref, where_ref, channels, height)
    tail = (height + 2) * channels
    adj[tail:, :] = jnp.zeros((adj.shape[0] - tail, adj.shape[1]), BF16)

    def first(e, _):
        back = conv_row(w2_ref, ext, e, channels)
        adj[rows(e, 1, channels), :] = (slope_ref[rows(e, 1, channels), :] * back).astype(BF16)
        return 0

    lax.fori_loop(0, height + 2, first, 0)

    def second(r, _):
        here = rows(r, 1, channels)
        back = conv_row(w1_ref, adj, r, channels)
        score[here, :] = (prior_ref[...] * res_ref[here, :] + guide_ref[here, :] + back).astype(BF16)
        return 0

    lax.fori_loop(0, height, second, 0)
    for start, size in channel_groups(channels):
        n = size * height
        picked = jnp.concatenate(
            [score[r * channels + start : r * channels + start + size, :] for r in range(height)], axis=0
        )
        out_ref[start * height : start * height + n, :] = jnp.dot(
            back_permutation(height, size), picked, preferred_element_type=F32
        ).astype(BF16)


def stacked(weights, flip):
    if flip:
        weights = weights[::-1, ::-1].transpose(1, 3, 0, 2)
    else:
        weights = weights.transpose(1, 2, 0, 3)
    taps, outs, row_taps, ins = weights.shape
    matrix = weights.reshape(taps * outs, row_taps * ins)
    depth = matrix.shape[1]
    return jnp.pad(matrix, ((0, 0), (0, -depth % 256)))


def pairs(count, step, parity):
    found = []
    for i in range(count):
        other = i + step if (i // step) % 2 == parity else i - step
        if 0 <= other < count:
            found.append((i, other))
    return found


def local(
    noisy_state, w_first, w_second, prior_weight, obs_weight, block_route, counts, tile_weights, observations
):
    channels, height, columns = noisy_state.shape
    tile_total = block_route.shape[1]
    span = tile_total // 2
    slots = tile_weights.shape[2]
    count = lax.axis_size("lat")
    where = jnp.stack([lax.axis_index("lat"), jnp.int32(count)]).astype(jnp.int32)
    pack_rows = BLK_LAT * slots + channels
    field = (height * channels, columns)

    def swap(x, step, parity):
        return lax.ppermute(x, "lat", pairs(count, step, parity))

    def shape(dims, dtype=BF16):
        return jax.ShapeDtypeStruct(dims, dtype)

    xt, ha, hb, za, zb, own = pl.pallas_call(
        functools.partial(prepare_kernel, channels, height, span),
        out_shape=(
            shape(field),
            shape((HALO * channels, columns)),
            shape((HALO * channels, columns)),
            shape((span, pack_rows, BLK_LON)),
            shape((span, pack_rows, BLK_LON)),
            shape((span, pack_rows, BLK_LON)),
        ),
        in_specs=[SM, SM, VM, VM, VM],
        out_specs=[VM] * 6,
        compiler_params=params(),
    )(where, counts[0], noisy_state.reshape(channels * height, columns), tile_weights[0], observations[0])
    ha, hb = swap(ha, 1, 0), swap(hb, 1, 1)
    za, zb = swap(za, span, 0), swap(zb, span, 1)
    relayed = pl.pallas_call(
        functools.partial(relay_kernel, span),
        out_shape=tuple(shape((2, pack_rows, BLK_LON)) for _ in range(span - 1)),
        in_specs=[SM, VM, VM, VM],
        out_specs=[VM] * (span - 1),
        compiler_params=params(),
    )(where, za, zb, own)
    arrived = [
        lax.ppermute(relayed[m - 1], "lat", [(i, i ^ m) for i in range(count)]) for m in range(1, span)
    ]
    w1, w2 = stacked(w_first, False), stacked(w_second, False)
    w1t, w2t = stacked(w_first, True), stacked(w_second, True)
    pad = w1.shape[1] - 3 * channels
    ext_rows = (height + 2 * HALO) * channels + pad
    mid_rows = (height + 2) * channels + pad
    res, slope = pl.pallas_call(
        functools.partial(forward_kernel, channels, height),
        out_shape=(shape(field, F32), shape(((height + 2) * channels, columns), F32)),
        in_specs=[SM] + [VM] * 5,
        out_specs=[VM] * 2,
        scratch_shapes=[pltpu.VMEM((ext_rows, columns), BF16), pltpu.VMEM((mid_rows, columns), BF16)],
        compiler_params=params(),
    )(where, xt, ha, hb, w1, w2)
    guide, ga, gb = pl.pallas_call(
        functools.partial(tile_kernel, channels, height, columns, span),
        out_shape=(
            shape(field, F32),
            shape((HALO * channels, columns)),
            shape((HALO * channels, columns)),
        ),
        in_specs=[SM, SM] + [VM] * 9,
        out_specs=[VM] * 3,
        compiler_params=params(),
    )(where, block_route[0], xt, res, obs_weight[:, None], own, za, zb, *arrived)
    ga, gb = swap(ga, 1, 0), swap(gb, 1, 1)
    out = pl.pallas_call(
        functools.partial(backward_kernel, channels, height),
        out_shape=shape(field),
        in_specs=[SM] + [VM] * 8,
        out_specs=VM,
        scratch_shapes=[
            pltpu.VMEM((ext_rows, columns), BF16),
            pltpu.VMEM((mid_rows, columns), BF16),
            pltpu.VMEM(field, BF16),
        ],
        compiler_params=params(),
    )(where, guide, ga, gb, slope, res, prior_weight[:, None], w2t, w1t)
    return out.reshape(channels, height, columns)


def solution(mesh):
    in_specs = (
        P("grp", "lat", None),
        P(),
        P(),
        P(),
        P(),
        P(("grp", "lat"), None),
        P(("grp", "lat"), None),
        P(("grp", "lat"), None, None, None),
        P(("grp", "lat"), None, None, None),
    )
    out_specs = P("grp", "lat", None)
    return jax.shard_map(local, mesh=mesh, in_specs=in_specs, out_specs=out_specs, check_vma=False)
```

```python
import functools

import jax
import jax.numpy as jnp
from jax import lax
from jax.experimental import pallas as pl
from jax.experimental.pallas import tpu as pltpu
from jax.sharding import PartitionSpec as P

BLK_LAT = 2
BLK_LON = 128
HALO = 2
F32 = jnp.float32
BF16 = jnp.bfloat16

VM = pl.BlockSpec(memory_space=pltpu.VMEM)
SM = pl.BlockSpec(memory_space=pltpu.SMEM)
HB = pl.BlockSpec(memory_space=pltpu.HBM)


def params(mib=16):
    return pltpu.CompilerParams(vmem_limit_bytes=mib << 20)


def shape(dims, dtype=BF16):
    return jax.ShapeDtypeStruct(dims, dtype)


def rows(index, count, channels):
    start = index * channels
    if not isinstance(start, int):
        start = pl.multiple_of(start, 16)
    return pl.ds(start, count * channels)


def permutation(height, group, back):
    n = height * group
    out = lax.broadcasted_iota(jnp.int32, (n, n), 0)
    src = lax.broadcasted_iota(jnp.int32, (n, n), 1)
    if back:
        want = (out % height) * group + out // height
    else:
        want = (out % group) * height + out // group
    return jnp.where(src == want, 1.0, 0.0).astype(BF16)


def channel_groups(channels):
    return [(start, min(32, channels - start)) for start in range(0, channels, 32)]


def as_column(row):
    n = row.shape[1]
    here = lax.broadcasted_iota(jnp.int32, (n, n), 0) == lax.broadcasted_iota(jnp.int32, (n, n), 1)
    return jnp.sum(jnp.where(here, jnp.broadcast_to(row, (n, n)), 0.0), axis=1, keepdims=True)


def place_in_plane(span):
    me = lax.axis_index("lat")
    return me % span, (me // span) % 2, me % 2


def pack_tile(k, dst, w_ref, obs_ref, count_ref, slots, channels):
    live = lax.broadcasted_iota(jnp.int32, (slots, BLK_LON), 0) < count_ref[0, k]
    zero = jnp.zeros((slots, BLK_LON), BF16)
    for i in range(BLK_LAT):
        half = w_ref[k, :, i * BLK_LON : (i + 1) * BLK_LON]
        dst[i * slots : (i + 1) * slots, :] = jnp.where(live, half, zero)
    dst[BLK_LAT * slots : BLK_LAT * slots + channels, :] = obs_ref[k]


def prepare_kernel(
    channels, height, span,
    count_ref, x_hbm, w_hbm, obs_hbm,
    xt_ref, ha_ref, hb_ref, za_ref, zb_ref, own_ref,
    x_ref, w_ref, obs_ref, sems,
):
    copies = []
    for index, (start, size) in enumerate(channel_groups(channels)):
        part = pl.ds(start * height, size * height)
        copies.append(pltpu.make_async_copy(x_hbm.at[part], x_ref.at[part], sems.at[index]))
    copies.append(pltpu.make_async_copy(w_hbm.at[0], w_ref, sems.at[len(copies)]))
    copies.append(pltpu.make_async_copy(obs_hbm.at[0], obs_ref, sems.at[len(copies)]))
    for copy in copies:
        copy.start()
    p, z_odd, odd = place_in_plane(span)
    for index, (start, size) in enumerate(channel_groups(channels)):
        copies[index].wait()
        n = size * height
        moved = jnp.dot(
            permutation(height, size, False),
            x_ref[start * height : start * height + n, :],
            preferred_element_type=F32,
        ).astype(BF16)
        for r in range(height):
            xt_ref[r * channels + start : r * channels + start + size, :] = (
                moved[r * size : (r + 1) * size, :]
            )
    last = height - HALO
    ha_ref[...] = xt_ref[rows(last * (1 - odd), HALO, channels), :]
    hb_ref[...] = xt_ref[rows(last * odd, HALO, channels), :]
    copies[-2].wait()
    copies[-1].wait()
    slots = w_ref.shape[1]
    pack = functools.partial(
        pack_tile, w_ref=w_ref, obs_ref=obs_ref, count_ref=count_ref, slots=slots, channels=channels
    )
    for j in range(span):
        up = jnp.maximum(p - j, 0)
        down = jnp.minimum(2 * span + p - j, 2 * span)
        pack(jnp.where(z_odd == 1, down, up), za_ref.at[j])
        pack(jnp.where(z_odd == 1, up, down), zb_ref.at[j])
        if j == 0:
            pack(span, own_ref.at[0])
        else:
            pack(span + p - lax.bitwise_xor(p, j), own_ref.at[j])


def relay_kernel(span, za_ref, zb_ref, own_ref, *outs):
    p, z_odd, _ = place_in_plane(span)
    for m in range(1, span):
        to = lax.bitwise_xor(p, m)
        below = jnp.where(to < p, 1, 0)
        outs[m - 1][0] = own_ref[m]

        @pl.when(below == z_odd)
        def _():
            outs[m - 1][1] = za_ref[to]

        @pl.when(below != z_odd)
        def _():
            outs[m - 1][1] = zb_ref[to]


def stack_forward(raw_ref, dst):
    taps, _, outs, ins = raw_ref.shape
    total = jnp.zeros(dst.shape, F32)
    for a in range(taps):
        block = raw_ref[a].reshape(taps * outs, ins)
        to = lax.broadcasted_iota(jnp.int32, (ins, taps * ins), 1)
        pick = jnp.where(to == lax.broadcasted_iota(jnp.int32, to.shape, 0) + a * ins, 1.0, 0.0)
        total += jnp.dot(block, pick.astype(BF16), preferred_element_type=F32)
    dst[...] = total.astype(BF16)


def stack_backward(raw_ref, dst):
    taps, _, outs, ins = raw_ref.shape
    n = taps * outs
    here = lax.broadcasted_iota(jnp.int32, (n, n), 0) == lax.broadcasted_iota(jnp.int32, (n, n), 1)
    same = jnp.where(here, 1.0, 0.0).astype(BF16)
    for b in range(taps):
        block = jnp.concatenate([raw_ref[taps - 1 - a, taps - 1 - b] for a in range(taps)], axis=0)
        dst[b * ins : (b + 1) * ins, :] = lax.dot_general(
            block, same, (((0,), (0,)), ((), ())), preferred_element_type=F32
        ).astype(BF16)


def conv_row(w_ref, src_ref, index, channels):
    window = src_ref[rows(index, 3, channels), :]
    taps = jnp.dot(w_ref[...], window, preferred_element_type=F32)
    width = taps.shape[1]
    return (
        pltpu.roll(taps[0:channels], 1, 1)
        + taps[channels : 2 * channels]
        + pltpu.roll(taps[2 * channels : 3 * channels], width - 1, 1)
    )


def silu_and_slope(act, keep=None):
    gate = 0.5 * jnp.tanh(0.5 * act) + 0.5
    if keep is not None:
        gate = gate * keep
    hidden = act * gate
    return hidden.astype(BF16), gate * (1.0 + act - hidden)


def ext_edges(channels, height, mid_ref, a_ref, b_ref, top, bottom, odd):
    edge = HALO * channels
    top[edge : 2 * edge, :] = mid_ref[0:edge, :]
    bottom[0:edge, :] = mid_ref[(height - HALO) * channels : height * channels, :]

    @pl.when(odd == 1)
    def _():
        top[0:edge, :] = a_ref[...]
        bottom[edge : 2 * edge, :] = b_ref[...]

    @pl.when(odd == 0)
    def _():
        top[0:edge, :] = b_ref[...]
        bottom[edge : 2 * edge, :] = a_ref[...]


def forward_inner_kernel(
    channels, height,
    xt_ref, raw1_ref, raw2_ref,
    hid_ref, slope_ref, res_ref, w1_ref, w2_ref, w1t_ref, w2t_ref,
):
    stack_forward(raw1_ref, w1_ref)
    stack_forward(raw2_ref, w2_ref)
    for i in range(height - 2):
        act = conv_row(w1_ref, xt_ref, i, channels)
        hid_ref[rows(i, 1, channels), :], slope_ref[rows(i, 1, channels), :] = silu_and_slope(act)
    for i in range(height - 4):
        res_ref[rows(i, 1, channels), :] = conv_row(w2_ref, hid_ref, i, channels)
    stack_backward(raw1_ref, w1t_ref)
    stack_backward(raw2_ref, w2t_ref)


def on_grid():
    me = lax.axis_index("lat")
    count = lax.axis_size("lat")
    return jnp.where(me == 0, 0.0, 1.0), jnp.where(me == count - 1, 0.0, 1.0)


def forward_edge_kernel(
    channels, height,
    xt_ref, a_ref, b_ref, hid_ref, w1_ref, w2_ref,
    slope_ref, res_ref,
    top, bottom, hid_top, hid_bottom,
):
    odd = lax.axis_index("lat") % 2
    ext_edges(channels, height, xt_ref, a_ref, b_ref, top, bottom, odd)
    has_above, has_below = on_grid()
    inner = (height - 2 - HALO) * channels
    hid_top[2 * channels : 4 * channels, :] = hid_ref[0 : 2 * channels, :]
    hid_bottom[0 : 2 * channels, :] = hid_ref[inner : inner + 2 * channels, :]
    for i, keep in ((0, has_above), (1, None)):
        act = conv_row(w1_ref, top, i, channels)
        hid_top[rows(i, 1, channels), :], slope_ref[rows(i, 1, channels), :] = silu_and_slope(act, keep)
    for i, keep in ((0, None), (1, has_below)):
        act = conv_row(w1_ref, bottom, i, channels)
        hid_bottom[rows(2 + i, 1, channels), :], slope_ref[rows(2 + i, 1, channels), :] = (
            silu_and_slope(act, keep)
        )
    for i in range(2):
        res_ref[rows(i, 1, channels), :] = conv_row(w2_ref, hid_top, i, channels)
        res_ref[rows(2 + i, 1, channels), :] = conv_row(w2_ref, hid_bottom, i, channels)


def tile_kernel(
    channels, height, columns, span,
    route_ref, xt_ref, inner_ref, edge_ref, ow_ref, own_ref, za_ref, zb_ref, *refs,
):
    near_refs, (guide_ref, low_ref, ga_ref, gb_ref) = refs[: span - 1], refs[span - 1 :]
    slots = BLK_LON
    across = columns // BLK_LON
    p, z_odd, odd = place_in_plane(span)
    guide_ref[...] = jnp.zeros_like(guide_ref)
    jobs = [
        (span, own_ref.at[0]),
        (jnp.where(z_odd == 1, 0, 2 * span), za_ref.at[p]),
        (jnp.where(z_odd == 1, 2 * span, 0), zb_ref.at[p]),
    ]
    for m in range(1, span):
        step = lax.bitwise_xor(p, m) - p
        jobs.append((span + step, near_refs[m - 1].at[0]))
        jobs.append((jnp.where(step > 0, step, 2 * span + step), near_refs[m - 1].at[1]))
    obs_weight = as_column(ow_ref[...])
    down = height // BLK_LAT
    places, blocks = [], []
    for k, ref in jobs:
        n = route_ref[0, k]
        r, q = n // across, n % across
        inside = (r > 0) & (r < down - 1)
        place, block = [], []
        for i in range(BLK_LAT):
            lanes = pl.ds(pl.multiple_of(q * BLK_LON, BLK_LON), BLK_LON)
            here = (rows(r * BLK_LAT + i, 1, channels), lanes)
            row_in = jnp.clip(r * BLK_LAT + i - HALO, 0, height - 2 * HALO - 1)
            row_edge = jnp.where(r == 0, i, HALO + i)
            res = jnp.where(
                inside,
                inner_ref[rows(row_in, 1, channels), lanes],
                edge_ref[rows(row_edge, 1, channels), lanes],
            )
            place.append(here)
            block.append((xt_ref[here].astype(F32) + res).astype(BF16))
        places.append(place)
        blocks.append(block)
    misfits = []
    for (k, ref), block in zip(jobs, blocks):
        predicted = jnp.zeros((channels, slots), F32)
        for i in range(BLK_LAT):
            predicted += lax.dot_general(
                block[i],
                ref[i * slots : (i + 1) * slots, :],
                (((1,), (1,)), ((), ())),
                preferred_element_type=F32,
            )
        obs = ref[BLK_LAT * slots : BLK_LAT * slots + channels, :].astype(F32)
        misfits.append(((obs - predicted) * obs_weight).astype(BF16))
    terms = [
        [
            jnp.dot(misfit, ref[i * slots : (i + 1) * slots, :], preferred_element_type=F32)
            .astype(BF16)
            .astype(F32)
            for i in range(BLK_LAT)
        ]
        for (k, ref), misfit in zip(jobs, misfits)
    ]
    for place, term in zip(places, terms):
        for i in range(BLK_LAT):
            guide_ref[place[i]] += term[i]
    last = height - HALO
    low_ref[...] = guide_ref[...].astype(BF16)
    ga_ref[...] = low_ref[rows(last * (1 - odd), HALO, channels), :]
    gb_ref[...] = low_ref[rows(last * odd, HALO, channels), :]


def backward_inner_kernel(
    channels, height,
    guide_ref, low_ref, slope_ref, res_ref, prior_ref, w2_ref, w1_ref,
    adj_ref, score_ref,
):
    for i in range(height - 2):
        here = rows(i, 1, channels)
        adj_ref[here, :] = (slope_ref[here, :] * conv_row(w2_ref, low_ref, i, channels)).astype(BF16)
    prior = as_column(prior_ref[...])
    for i in range(height - 4):
        here = rows(i, 1, channels)
        back = conv_row(w1_ref, adj_ref, i, channels)
        guide = guide_ref[rows(i + HALO, 1, channels), :]
        score_ref[here, :] = (prior * res_ref[here, :] + guide + back).astype(BF16)


def backward_edge_kernel(
    channels, height,
    guide_ref, low_ref, a_ref, b_ref, slope_ref, res_ref, prior_ref, adj_ref, score_ref, w2_ref, w1_ref,
    out_ref,
    top, bottom, adj_top, adj_bottom, edge_ref,
):
    odd = lax.axis_index("lat") % 2
    ext_edges(channels, height, low_ref, a_ref, b_ref, top, bottom, odd)
    inner = (height - 2 - HALO) * channels
    adj_top[2 * channels : 4 * channels, :] = adj_ref[0 : 2 * channels, :]
    adj_bottom[0 : 2 * channels, :] = adj_ref[inner : inner + 2 * channels, :]
    for i in range(2):
        adj_top[rows(i, 1, channels), :] = (
            slope_ref[rows(i, 1, channels), :] * conv_row(w2_ref, top, i, channels)
        ).astype(BF16)
        adj_bottom[rows(2 + i, 1, channels), :] = (
            slope_ref[rows(2 + i, 1, channels), :] * conv_row(w2_ref, bottom, i, channels)
        ).astype(BF16)
    prior = as_column(prior_ref[...])
    for i in range(2):
        for src, at, row in ((adj_top, i, i), (adj_bottom, HALO + i, height - HALO + i)):
            here = rows(at, 1, channels)
            back = conv_row(w1_ref, src, i, channels)
            edge_ref[here, :] = (
                prior * res_ref[here, :] + guide_ref[rows(row, 1, channels), :] + back
            ).astype(BF16)
    for start, size in channel_groups(channels):
        n = size * height
        picked = []
        for r in range(height):
            if r < HALO:
                src, at = edge_ref, r
            elif r < height - HALO:
                src, at = score_ref, r - HALO
            else:
                src, at = edge_ref, r - height + 2 * HALO
            picked.append(src[at * channels + start : at * channels + start + size, :])
        out_ref[start * height : start * height + n, :] = jnp.dot(
            permutation(height, size, True), jnp.concatenate(picked, axis=0), preferred_element_type=F32
        ).astype(BF16)


def pairs(count, step, parity):
    found = []
    for i in range(count):
        other = i + step if (i // step) % 2 == parity else i - step
        if 0 <= other < count:
            found.append((i, other))
    return found


def local(
    noisy_state, w_first, w_second, prior_weight, obs_weight, block_route, counts, tile_weights, observations
):
    channels, height, columns = noisy_state.shape
    tile_total = block_route.shape[1]
    span = tile_total // 2
    slots = tile_weights.shape[2]
    count = lax.axis_size("lat")
    pack_rows = BLK_LAT * slots + channels
    taps = w_first.shape[0]

    def field(n, dtype=BF16):
        return shape((n * channels, columns), dtype)

    def buffer(n, dtype=BF16):
        return pltpu.VMEM((n * channels, columns), dtype)

    def swap(x, step, parity):
        return lax.ppermute(x, "lat", pairs(count, step, parity))

    packed = shape((span, pack_rows, BLK_LON))
    xt, ha, hb, za, zb, own = pl.pallas_call(
        functools.partial(prepare_kernel, channels, height, span),
        out_shape=(field(height), field(HALO), field(HALO), packed, packed, packed),
        in_specs=[SM, HB, HB, HB],
        out_specs=[VM] * 6,
        scratch_shapes=[
            pltpu.VMEM((channels * height, columns), BF16),
            pltpu.VMEM(tile_weights.shape[1:], BF16),
            pltpu.VMEM(observations.shape[1:], BF16),
            pltpu.SemaphoreType.DMA((len(channel_groups(channels)) + 2,)),
        ],
        compiler_params=params(),
    )(counts, noisy_state.reshape(channels * height, columns), tile_weights, observations)
    ha, hb = swap(ha, 1, 0), swap(hb, 1, 1)
    za, zb = swap(za, span, 0), swap(zb, span, 1)

    weight = shape((taps * channels, taps * channels))
    hid, slope_in, res_in, w1, w2, w1t, w2t = pl.pallas_call(
        functools.partial(forward_inner_kernel, channels, height),
        out_shape=(field(height - 2), field(height - 2, F32), field(height - 4, F32)) + (weight,) * 4,
        in_specs=[VM] * 3,
        out_specs=[VM] * 7,
        compiler_params=params(),
    )(xt, w_first, w_second)

    relayed = pl.pallas_call(
        functools.partial(relay_kernel, span),
        out_shape=tuple(shape((2, pack_rows, BLK_LON)) for _ in range(span - 1)),
        in_specs=[VM] * 3,
        out_specs=[VM] * (span - 1),
        compiler_params=params(),
    )(za, zb, own)
    arrived = [
        lax.ppermute(relayed[m - 1], "lat", [(i, i ^ m) for i in range(count)]) for m in range(1, span)
    ]

    slope_ed, res_ed = pl.pallas_call(
        functools.partial(forward_edge_kernel, channels, height),
        out_shape=(field(2 * HALO, F32), field(2 * HALO, F32)),
        in_specs=[VM] * 6,
        out_specs=[VM] * 2,
        scratch_shapes=[buffer(2 * HALO)] * 4,
        compiler_params=params(),
    )(xt, ha, hb, hid, w1, w2)

    guide, low, ga, gb = pl.pallas_call(
        functools.partial(tile_kernel, channels, height, columns, span),
        out_shape=(field(height, F32), field(height), field(HALO), field(HALO)),
        in_specs=[SM] + [VM] * (7 + span - 1),
        out_specs=[VM] * 4,
        compiler_params=params(),
    )(block_route, xt, res_in, res_ed, obs_weight[None, :], own, za, zb, *arrived)
    ga, gb = swap(ga, 1, 0), swap(gb, 1, 1)

    prior = prior_weight[None, :]
    adj, score = pl.pallas_call(
        functools.partial(backward_inner_kernel, channels, height),
        out_shape=(field(height - 2), field(height - 4)),
        in_specs=[VM] * 7,
        out_specs=[VM] * 2,
        compiler_params=params(),
    )(guide, low, slope_in, res_in, prior, w2t, w1t)

    out = pl.pallas_call(
        functools.partial(backward_edge_kernel, channels, height),
        out_shape=shape((channels * height, columns)),
        in_specs=[VM] * 11,
        out_specs=VM,
        scratch_shapes=[buffer(2 * HALO)] * 5,
        compiler_params=params(),
    )(guide, low, ga, gb, slope_ed, res_ed, prior, adj, score, w2t, w1t)
    return out.reshape(channels, height, columns)


def solution(mesh):
    in_specs = (
        P("grp", "lat", None),
        P(),
        P(),
        P(),
        P(),
        P(("grp", "lat"), None),
        P(("grp", "lat"), None),
        P(("grp", "lat"), None, None, None),
        P(("grp", "lat"), None, None, None),
    )
    out_specs = P("grp", "lat", None)
    return jax.shard_map(local, mesh=mesh, in_specs=in_specs, out_specs=out_specs, check_vma=False)
```

```python
import functools

import jax
import jax.numpy as jnp
from jax import lax
from jax.experimental import pallas as pl
from jax.experimental.pallas import tpu as pltpu
from jax.sharding import PartitionSpec as P

BLK_LAT = 2
BLK_LON = 128
HALO = 2
F32 = jnp.float32
BF16 = jnp.bfloat16

VM = pl.BlockSpec(memory_space=pltpu.VMEM)
SM = pl.BlockSpec(memory_space=pltpu.SMEM)
HB = pl.BlockSpec(memory_space=pltpu.HBM)
AN = pl.BlockSpec(memory_space=pl.ANY)


def params(mib=16):
    return pltpu.CompilerParams(vmem_limit_bytes=mib << 20)


def shape(dims, dtype=BF16):
    return jax.ShapeDtypeStruct(dims, dtype)


def rows(index, count, channels):
    start = index * channels
    if not isinstance(start, int):
        start = pl.multiple_of(start, 16)
    return pl.ds(start, count * channels)


def permutation(height, group, back):
    n = height * group
    out = lax.broadcasted_iota(jnp.int32, (n, n), 0)
    src = lax.broadcasted_iota(jnp.int32, (n, n), 1)
    if back:
        want = (out % height) * group + out // height
    else:
        want = (out % group) * height + out // group
    return jnp.where(src == want, 1.0, 0.0).astype(BF16)


def channel_groups(channels):
    return [(start, min(32, channels - start)) for start in range(0, channels, 32)]


def as_column(row):
    n = row.shape[1]
    here = lax.broadcasted_iota(jnp.int32, (n, n), 0) == lax.broadcasted_iota(jnp.int32, (n, n), 1)
    return jnp.sum(jnp.where(here, jnp.broadcast_to(row, (n, n)), 0.0), axis=1, keepdims=True)


def place_in_plane(span):
    me = lax.axis_index("lat")
    return me % span, (me // span) % 2, me % 2


def pack_tile(k, dst, w_ref, obs_ref, count_ref, slots, channels):
    live = lax.broadcasted_iota(jnp.int32, (slots, BLK_LON), 0) < count_ref[0, k]
    zero = jnp.zeros((slots, BLK_LON), BF16)
    for i in range(BLK_LAT):
        half = w_ref[k, :, i * BLK_LON : (i + 1) * BLK_LON]
        dst[i * slots : (i + 1) * slots, :] = jnp.where(live, half, zero)
    dst[BLK_LAT * slots : BLK_LAT * slots + channels, :] = obs_ref[k]


def prepare_kernel(channels, height, x_hbm, xt_ref, ha_ref, hb_ref, x_ref, sems):
    copies = []
    for index, (start, size) in enumerate(channel_groups(channels)):
        part = pl.ds(start * height, size * height)
        copies.append(pltpu.make_async_copy(x_hbm.at[part], x_ref.at[part], sems.at[index]))
        copies[-1].start()
    odd = lax.axis_index("lat") % 2
    for index, (start, size) in enumerate(channel_groups(channels)):
        moving = permutation(height, size, False)
        copies[index].wait()
        n = size * height
        moved = jnp.dot(
            moving, x_ref[start * height : start * height + n, :], preferred_element_type=F32
        ).astype(BF16)
        for r in range(height):
            xt_ref[r * channels + start : r * channels + start + size, :] = (
                moved[r * size : (r + 1) * size, :]
            )
    last = height - HALO
    ha_ref[...] = xt_ref[rows(last * (1 - odd), HALO, channels), :]
    hb_ref[...] = xt_ref[rows(last * odd, HALO, channels), :]


def pack_kernel(
    channels, span,
    count_ref, w_hbm, obs_hbm, after_ref,
    za_ref, zb_ref, own_ref,
    w_ref, obs_ref, sems,
):
    copies = [
        pltpu.make_async_copy(w_hbm.at[0], w_ref, sems.at[0]),
        pltpu.make_async_copy(obs_hbm.at[0], obs_ref, sems.at[1]),
    ]
    for copy in copies:
        copy.start()
    for copy in copies:
        copy.wait()
    p, z_odd, _ = place_in_plane(span)
    slots = w_ref.shape[1]
    pack = functools.partial(
        pack_tile, w_ref=w_ref, obs_ref=obs_ref, count_ref=count_ref, slots=slots, channels=channels
    )
    for j in range(span):
        up = jnp.maximum(p - j, 0)
        down = jnp.minimum(2 * span + p - j, 2 * span)
        pack(jnp.where(z_odd == 1, down, up), za_ref.at[j])
        pack(jnp.where(z_odd == 1, up, down), zb_ref.at[j])
        if j == 0:
            pack(span, own_ref.at[0])
        else:
            pack(span + p - lax.bitwise_xor(p, j), own_ref.at[j])


def relay_kernel(span, after_ref, za_ref, zb_ref, own_ref, *outs):
    p, z_odd, _ = place_in_plane(span)
    for m in range(1, span):
        to = lax.bitwise_xor(p, m)
        below = jnp.where(to < p, 1, 0)
        outs[m - 1][0] = own_ref[m]

        @pl.when(below == z_odd)
        def _():
            outs[m - 1][1] = za_ref[to]

        @pl.when(below != z_odd)
        def _():
            outs[m - 1][1] = zb_ref[to]


def stack_forward(raw_ref, dst):
    taps, _, outs, ins = raw_ref.shape
    total = jnp.zeros(dst.shape, F32)
    for a in range(taps):
        block = raw_ref[a].reshape(taps * outs, ins)
        to = lax.broadcasted_iota(jnp.int32, (ins, taps * ins), 1)
        pick = jnp.where(to == lax.broadcasted_iota(jnp.int32, to.shape, 0) + a * ins, 1.0, 0.0)
        total += jnp.dot(block, pick.astype(BF16), preferred_element_type=F32)
    dst[...] = total.astype(BF16)


def stack_backward(raw_ref, dst):
    taps, _, outs, ins = raw_ref.shape
    n = taps * outs
    here = lax.broadcasted_iota(jnp.int32, (n, n), 0) == lax.broadcasted_iota(jnp.int32, (n, n), 1)
    same = jnp.where(here, 1.0, 0.0).astype(BF16)
    for b in range(taps):
        block = jnp.concatenate([raw_ref[taps - 1 - a, taps - 1 - b] for a in range(taps)], axis=0)
        dst[b * ins : (b + 1) * ins, :] = lax.dot_general(
            block, same, (((0,), (0,)), ((), ())), preferred_element_type=F32
        ).astype(BF16)


def conv_row(w_ref, src_ref, index, channels):
    window = src_ref[rows(index, 3, channels), :]
    taps = jnp.dot(w_ref[...], window, preferred_element_type=F32)
    width = taps.shape[1]
    return (
        pltpu.roll(taps[0:channels], 1, 1)
        + taps[channels : 2 * channels]
        + pltpu.roll(taps[2 * channels : 3 * channels], width - 1, 1)
    )


def silu_and_slope(act, keep=None):
    gate = 0.5 * jnp.tanh(0.5 * act) + 0.5
    if keep is not None:
        gate = gate * keep
    hidden = act * gate
    return hidden.astype(BF16), gate * (1.0 + act - hidden)


def ext_edges(channels, height, mid_ref, a_ref, b_ref, top, bottom, odd):
    edge = HALO * channels
    top[edge : 2 * edge, :] = mid_ref[0:edge, :]
    bottom[0:edge, :] = mid_ref[(height - HALO) * channels : height * channels, :]

    @pl.when(odd == 1)
    def _():
        top[0:edge, :] = a_ref[...]
        bottom[edge : 2 * edge, :] = b_ref[...]

    @pl.when(odd == 0)
    def _():
        top[0:edge, :] = b_ref[...]
        bottom[edge : 2 * edge, :] = a_ref[...]


def forward_inner_kernel(
    channels, height,
    xt_ref, raw1_ref, raw2_ref,
    hid_ref, slope_ref, res_ref, w1_ref, w2_ref, w1t_ref, w2t_ref,
):
    stack_forward(raw1_ref, w1_ref)
    stack_forward(raw2_ref, w2_ref)
    for i in range(height - 2):
        act = conv_row(w1_ref, xt_ref, i, channels)
        hid_ref[rows(i, 1, channels), :], slope_ref[rows(i, 1, channels), :] = silu_and_slope(act)
    for i in range(height - 4):
        res_ref[rows(i, 1, channels), :] = conv_row(w2_ref, hid_ref, i, channels)
    stack_backward(raw1_ref, w1t_ref)
    stack_backward(raw2_ref, w2t_ref)


def on_grid():
    me = lax.axis_index("lat")
    count = lax.axis_size("lat")
    return jnp.where(me == 0, 0.0, 1.0), jnp.where(me == count - 1, 0.0, 1.0)


def forward_edge_kernel(
    channels, height,
    xt_ref, a_ref, b_ref, hid_ref, w1_ref, w2_ref,
    slope_ref, res_ref,
    top, bottom, hid_top, hid_bottom,
):
    odd = lax.axis_index("lat") % 2
    ext_edges(channels, height, xt_ref, a_ref, b_ref, top, bottom, odd)
    has_above, has_below = on_grid()
    inner = (height - 2 - HALO) * channels
    hid_top[2 * channels : 4 * channels, :] = hid_ref[0 : 2 * channels, :]
    hid_bottom[0 : 2 * channels, :] = hid_ref[inner : inner + 2 * channels, :]
    for i, keep in ((0, has_above), (1, None)):
        act = conv_row(w1_ref, top, i, channels)
        hid_top[rows(i, 1, channels), :], slope_ref[rows(i, 1, channels), :] = silu_and_slope(act, keep)
    for i, keep in ((0, None), (1, has_below)):
        act = conv_row(w1_ref, bottom, i, channels)
        hid_bottom[rows(2 + i, 1, channels), :], slope_ref[rows(2 + i, 1, channels), :] = (
            silu_and_slope(act, keep)
        )
    for i in range(2):
        res_ref[rows(i, 1, channels), :] = conv_row(w2_ref, hid_top, i, channels)
        res_ref[rows(2 + i, 1, channels), :] = conv_row(w2_ref, hid_bottom, i, channels)


def tile_kernel(
    channels, height, columns, span,
    route_ref, xt_ref, inner_ref, edge_ref, ow_ref, own_ref, za_ref, zb_ref, *refs,
):
    near_refs, (guide_ref, low_ref, ga_ref, gb_ref) = refs[: span - 1], refs[span - 1 :]
    slots = BLK_LON
    across = columns // BLK_LON
    p, z_odd, odd = place_in_plane(span)
    guide_ref[...] = jnp.zeros_like(guide_ref)
    jobs = [
        (span, own_ref.at[0]),
        (jnp.where(z_odd == 1, 0, 2 * span), za_ref.at[p]),
        (jnp.where(z_odd == 1, 2 * span, 0), zb_ref.at[p]),
    ]
    for m in range(1, span):
        step = lax.bitwise_xor(p, m) - p
        jobs.append((span + step, near_refs[m - 1].at[0]))
        jobs.append((jnp.where(step > 0, step, 2 * span + step), near_refs[m - 1].at[1]))
    obs_weight = as_column(ow_ref[...])
    down = height // BLK_LAT
    places, blocks = [], []
    for k, ref in jobs:
        n = route_ref[0, k]
        r, q = n // across, n % across
        inside = (r > 0) & (r < down - 1)
        place, block = [], []
        for i in range(BLK_LAT):
            lanes = pl.ds(pl.multiple_of(q * BLK_LON, BLK_LON), BLK_LON)
            here = (rows(r * BLK_LAT + i, 1, channels), lanes)
            row_in = jnp.clip(r * BLK_LAT + i - HALO, 0, height - 2 * HALO - 1)
            row_edge = jnp.where(r == 0, i, HALO + i)
            res = jnp.where(
                inside,
                inner_ref[rows(row_in, 1, channels), lanes],
                edge_ref[rows(row_edge, 1, channels), lanes],
            )
            place.append(here)
            block.append((xt_ref[here].astype(F32) + res).astype(BF16))
        places.append(place)
        blocks.append(block)
    misfits = []
    for (k, ref), block in zip(jobs, blocks):
        predicted = jnp.zeros((channels, slots), F32)
        for i in range(BLK_LAT):
            predicted += lax.dot_general(
                block[i],
                ref[i * slots : (i + 1) * slots, :],
                (((1,), (1,)), ((), ())),
                preferred_element_type=F32,
            )
        obs = ref[BLK_LAT * slots : BLK_LAT * slots + channels, :].astype(F32)
        misfits.append(((obs - predicted) * obs_weight).astype(BF16))
    terms = [
        [
            jnp.dot(misfit, ref[i * slots : (i + 1) * slots, :], preferred_element_type=F32)
            .astype(BF16)
            .astype(F32)
            for i in range(BLK_LAT)
        ]
        for (k, ref), misfit in zip(jobs, misfits)
    ]
    for place, term in zip(places, terms):
        for i in range(BLK_LAT):
            guide_ref[place[i]] += term[i]
    last = height - HALO
    low_ref[...] = guide_ref[...].astype(BF16)
    ga_ref[...] = low_ref[rows(last * (1 - odd), HALO, channels), :]
    gb_ref[...] = low_ref[rows(last * odd, HALO, channels), :]


def backward_inner_kernel(
    channels, height,
    guide_ref, low_ref, slope_ref, res_ref, prior_ref, w2_ref, w1_ref,
    adj_ref, score_ref,
):
    for i in range(height - 2):
        here = rows(i, 1, channels)
        adj_ref[here, :] = (slope_ref[here, :] * conv_row(w2_ref, low_ref, i, channels)).astype(BF16)
    prior = as_column(prior_ref[...])
    for i in range(height - 4):
        here = rows(i, 1, channels)
        back = conv_row(w1_ref, adj_ref, i, channels)
        guide = guide_ref[rows(i + HALO, 1, channels), :]
        score_ref[here, :] = (prior * res_ref[here, :] + guide + back).astype(BF16)


def backward_edge_kernel(
    channels, height,
    guide_ref, low_ref, a_ref, b_ref, slope_ref, res_ref, prior_ref, adj_ref, score_ref, w2_ref, w1_ref,
    out_ref,
    top, bottom, adj_top, adj_bottom, edge_ref,
):
    odd = lax.axis_index("lat") % 2
    ext_edges(channels, height, low_ref, a_ref, b_ref, top, bottom, odd)
    inner = (height - 2 - HALO) * channels
    adj_top[2 * channels : 4 * channels, :] = adj_ref[0 : 2 * channels, :]
    adj_bottom[0 : 2 * channels, :] = adj_ref[inner : inner + 2 * channels, :]
    for i in range(2):
        adj_top[rows(i, 1, channels), :] = (
            slope_ref[rows(i, 1, channels), :] * conv_row(w2_ref, top, i, channels)
        ).astype(BF16)
        adj_bottom[rows(2 + i, 1, channels), :] = (
            slope_ref[rows(2 + i, 1, channels), :] * conv_row(w2_ref, bottom, i, channels)
        ).astype(BF16)
    prior = as_column(prior_ref[...])
    for i in range(2):
        for src, at, row in ((adj_top, i, i), (adj_bottom, HALO + i, height - HALO + i)):
            here = rows(at, 1, channels)
            back = conv_row(w1_ref, src, i, channels)
            edge_ref[here, :] = (
                prior * res_ref[here, :] + guide_ref[rows(row, 1, channels), :] + back
            ).astype(BF16)
    for start, size in channel_groups(channels):
        n = size * height
        picked = []
        for r in range(height):
            if r < HALO:
                src, at = edge_ref, r
            elif r < height - HALO:
                src, at = score_ref, r - HALO
            else:
                src, at = edge_ref, r - height + 2 * HALO
            picked.append(src[at * channels + start : at * channels + start + size, :])
        out_ref[start * height : start * height + n, :] = jnp.dot(
            permutation(height, size, True), jnp.concatenate(picked, axis=0), preferred_element_type=F32
        ).astype(BF16)


def pairs(count, step, parity):
    found = []
    for i in range(count):
        other = i + step if (i // step) % 2 == parity else i - step
        if 0 <= other < count:
            found.append((i, other))
    return found


def local(
    noisy_state, w_first, w_second, prior_weight, obs_weight, block_route, counts, tile_weights, observations
):
    channels, height, columns = noisy_state.shape
    tile_total = block_route.shape[1]
    span = tile_total // 2
    slots = tile_weights.shape[2]
    count = lax.axis_size("lat")
    pack_rows = BLK_LAT * slots + channels
    taps = w_first.shape[0]

    def field(n, dtype=BF16):
        return shape((n * channels, columns), dtype)

    def buffer(n, dtype=BF16):
        return pltpu.VMEM((n * channels, columns), dtype)

    def swap(x, step, parity):
        return lax.ppermute(x, "lat", pairs(count, step, parity))

    packed = shape((span, pack_rows, BLK_LON))
    def in_hbm(x):
        return pltpu.with_memory_space_constraint(x, pltpu.HBM)

    xt, ha, hb = pl.pallas_call(
        functools.partial(prepare_kernel, channels, height),
        out_shape=(field(height), field(HALO), field(HALO)),
        in_specs=[HB],
        out_specs=[VM] * 3,
        scratch_shapes=[
            pltpu.VMEM((channels * height, columns), BF16),
            pltpu.SemaphoreType.DMA((len(channel_groups(channels)),)),
        ],
        compiler_params=params(),
    )(in_hbm(noisy_state.reshape(channels * height, columns)))
    ha, hb = swap(ha, 1, 0), swap(hb, 1, 1)
    za, zb, own = pl.pallas_call(
        functools.partial(pack_kernel, channels, span),
        out_shape=(packed, packed, packed),
        in_specs=[SM, HB, HB, AN],
        out_specs=[VM] * 3,
        scratch_shapes=[
            pltpu.VMEM(tile_weights.shape[1:], BF16),
            pltpu.VMEM(observations.shape[1:], BF16),
            pltpu.SemaphoreType.DMA((2,)),
        ],
        compiler_params=params(),
    )(counts, in_hbm(tile_weights), in_hbm(observations), xt)
    za, zb = swap(za, span, 0), swap(zb, span, 1)

    weight = shape((taps * channels, taps * channels))
    hid, slope_in, res_in, w1, w2, w1t, w2t = pl.pallas_call(
        functools.partial(forward_inner_kernel, channels, height),
        out_shape=(field(height - 2), field(height - 2, F32), field(height - 4, F32)) + (weight,) * 4,
        in_specs=[VM] * 3,
        out_specs=[VM] * 7,
        compiler_params=params(),
    )(xt, w_first, w_second)

    relayed = pl.pallas_call(
        functools.partial(relay_kernel, span),
        out_shape=tuple(shape((2, pack_rows, BLK_LON)) for _ in range(span - 1)),
        in_specs=[AN] + [VM] * 3,
        out_specs=[VM] * (span - 1),
        compiler_params=params(),
    )(w1, za, zb, own)
    arrived = [
        lax.ppermute(relayed[m - 1], "lat", [(i, i ^ m) for i in range(count)]) for m in range(1, span)
    ]

    slope_ed, res_ed = pl.pallas_call(
        functools.partial(forward_edge_kernel, channels, height),
        out_shape=(field(2 * HALO, F32), field(2 * HALO, F32)),
        in_specs=[VM] * 6,
        out_specs=[VM] * 2,
        scratch_shapes=[buffer(2 * HALO)] * 4,
        compiler_params=params(),
    )(xt, ha, hb, hid, w1, w2)

    guide, low, ga, gb = pl.pallas_call(
        functools.partial(tile_kernel, channels, height, columns, span),
        out_shape=(field(height, F32), field(height), field(HALO), field(HALO)),
        in_specs=[SM] + [VM] * (7 + span - 1),
        out_specs=[VM] * 4,
        compiler_params=params(),
    )(block_route, xt, res_in, res_ed, obs_weight[None, :], own, za, zb, *arrived)
    ga, gb = swap(ga, 1, 0), swap(gb, 1, 1)

    prior = prior_weight[None, :]
    adj, score = pl.pallas_call(
        functools.partial(backward_inner_kernel, channels, height),
        out_shape=(field(height - 2), field(height - 4)),
        in_specs=[VM] * 7,
        out_specs=[VM] * 2,
        compiler_params=params(),
    )(guide, low, slope_in, res_in, prior, w2t, w1t)

    out = pl.pallas_call(
        functools.partial(backward_edge_kernel, channels, height),
        out_shape=shape((channels * height, columns)),
        in_specs=[VM] * 11,
        out_specs=VM,
        scratch_shapes=[buffer(2 * HALO)] * 5,
        compiler_params=params(),
    )(guide, low, ga, gb, slope_ed, res_ed, prior, adj, score, w2t, w1t)
    return out.reshape(channels, height, columns)


def solution(mesh):
    in_specs = (
        P("grp", "lat", None),
        P(),
        P(),
        P(),
        P(),
        P(("grp", "lat"), None),
        P(("grp", "lat"), None),
        P(("grp", "lat"), None, None, None),
        P(("grp", "lat"), None, None, None),
    )
    out_specs = P("grp", "lat", None)
    return jax.shard_map(local, mesh=mesh, in_specs=in_specs, out_specs=out_specs, check_vma=False)
```

```python
import functools

import jax
import jax.numpy as jnp
from jax import lax
from jax.experimental import pallas as pl
from jax.experimental.pallas import tpu as pltpu
from jax.sharding import PartitionSpec as P

BLK_LAT = 2
BLK_LON = 128
HALO = 2
F32 = jnp.float32
BF16 = jnp.bfloat16

VM = pl.BlockSpec(memory_space=pltpu.VMEM)
SM = pl.BlockSpec(memory_space=pltpu.SMEM)
HB = pl.BlockSpec(memory_space=pltpu.HBM)
AN = pl.BlockSpec(memory_space=pl.ANY)


def params(mib=16):
    return pltpu.CompilerParams(vmem_limit_bytes=mib << 20)


def shape(dims, dtype=BF16):
    return jax.ShapeDtypeStruct(dims, dtype)


def rows(index, count, channels):
    start = index * channels
    if not isinstance(start, int):
        start = pl.multiple_of(start, 16)
    return pl.ds(start, count * channels)


def permutation(height, group, back):
    n = height * group
    out = lax.broadcasted_iota(jnp.int32, (n, n), 0)
    src = lax.broadcasted_iota(jnp.int32, (n, n), 1)
    if back:
        want = (out % height) * group + out // height
    else:
        want = (out % group) * height + out // group
    return jnp.where(src == want, 1.0, 0.0).astype(BF16)


def channel_groups(channels):
    return [(start, min(32, channels - start)) for start in range(0, channels, 32)]


def as_column(row):
    n = row.shape[1]
    here = lax.broadcasted_iota(jnp.int32, (n, n), 0) == lax.broadcasted_iota(jnp.int32, (n, n), 1)
    return jnp.sum(jnp.where(here, jnp.broadcast_to(row, (n, n)), 0.0), axis=1, keepdims=True)


def place_in_plane(span):
    me = lax.axis_index("lat")
    return me % span, (me // span) % 2, me % 2


def pack_tile(k, dst, w_ref, obs_ref, count_ref, slots, channels):
    live = lax.broadcasted_iota(jnp.int32, (slots, BLK_LON), 0) < count_ref[0, k]
    zero = jnp.zeros((slots, BLK_LON), BF16)
    for i in range(BLK_LAT):
        half = w_ref[k, :, i * BLK_LON : (i + 1) * BLK_LON]
        dst[i * slots : (i + 1) * slots, :] = jnp.where(live, half, zero)
    dst[BLK_LAT * slots : BLK_LAT * slots + channels, :] = obs_ref[k]


def edge_pair(src_ref, ha_ref, hb_ref, height, channels):
    me, odd = lax.axis_index("lat"), lax.axis_index("lat") % 2
    last = height - HALO
    ha_ref[...] = src_ref[rows(last * (1 - odd), HALO, channels), :]
    alone = (me == 0) | (me == lax.axis_size("lat") - 1)

    @pl.when(alone)
    def _():
        hb_ref[...] = jnp.zeros_like(hb_ref)

    @pl.when(jnp.logical_not(alone))
    def _():
        hb_ref[...] = src_ref[rows(last * odd, HALO, channels), :]


def prepare_kernel(
    channels, height, span,
    count_ref, x_hbm, w_hbm, obs_hbm,
    xt_ref, ha_ref, hb_ref, za_ref, zb_ref, own_ref,
    x_ref, w_ref, obs_ref, sems,
):
    copies = []
    for start, size in channel_groups(channels):
        part = pl.ds(start * height, size * height)
        copies.append(pltpu.make_async_copy(x_hbm.at[part], x_ref.at[part], sems.at[len(copies)]))
    copies.append(pltpu.make_async_copy(w_hbm.at[0], w_ref, sems.at[len(copies)]))
    copies.append(pltpu.make_async_copy(obs_hbm.at[0], obs_ref, sems.at[len(copies)]))
    for copy in copies:
        copy.start()
    for index, (start, size) in enumerate(channel_groups(channels)):
        moving = permutation(height, size, False)
        copies[index].wait()
        n = size * height
        moved = jnp.dot(
            moving, x_ref[start * height : start * height + n, :], preferred_element_type=F32
        ).astype(BF16)
        for r in range(height):
            xt_ref[r * channels + start : r * channels + start + size, :] = (
                moved[r * size : (r + 1) * size, :]
            )
    edge_pair(xt_ref, ha_ref, hb_ref, height, channels)
    copies[-2].wait()
    copies[-1].wait()
    p, z_odd, _ = place_in_plane(span)
    slots = w_ref.shape[1]
    pack = functools.partial(
        pack_tile, w_ref=w_ref, obs_ref=obs_ref, count_ref=count_ref, slots=slots, channels=channels
    )
    for j in range(span):
        up = jnp.maximum(p - j, 0)
        down = jnp.minimum(2 * span + p - j, 2 * span)
        pack(jnp.where(z_odd == 1, down, up), za_ref.at[j])
        pack(jnp.where(z_odd == 1, up, down), zb_ref.at[j])
        if j == 0:
            pack(span, own_ref.at[0])
        else:
            pack(span + p - lax.bitwise_xor(p, j), own_ref.at[j])


def relay_kernel(span, after_ref, za_ref, zb_ref, own_ref, *outs):
    p, z_odd, _ = place_in_plane(span)
    for m in range(1, span):
        to = lax.bitwise_xor(p, m)
        below = jnp.where(to < p, 1, 0)
        outs[m - 1][0] = own_ref[m]

        @pl.when(below == z_odd)
        def _():
            outs[m - 1][1] = za_ref[to]

        @pl.when(below != z_odd)
        def _():
            outs[m - 1][1] = zb_ref[to]


def stack_forward(raw_ref, dst):
    taps, _, outs, ins = raw_ref.shape
    total = jnp.zeros(dst.shape, F32)
    for a in range(taps):
        block = raw_ref[a].reshape(taps * outs, ins)
        to = lax.broadcasted_iota(jnp.int32, (ins, taps * ins), 1)
        pick = jnp.where(to == lax.broadcasted_iota(jnp.int32, to.shape, 0) + a * ins, 1.0, 0.0)
        total += jnp.dot(block, pick.astype(BF16), preferred_element_type=F32)
    dst[...] = total.astype(BF16)


def stack_backward(raw_ref, dst):
    taps, _, outs, ins = raw_ref.shape
    n = taps * outs
    here = lax.broadcasted_iota(jnp.int32, (n, n), 0) == lax.broadcasted_iota(jnp.int32, (n, n), 1)
    same = jnp.where(here, 1.0, 0.0).astype(BF16)
    for b in range(taps):
        block = jnp.concatenate([raw_ref[taps - 1 - a, taps - 1 - b] for a in range(taps)], axis=0)
        dst[b * ins : (b + 1) * ins, :] = lax.dot_general(
            block, same, (((0,), (0,)), ((), ())), preferred_element_type=F32
        ).astype(BF16)


def conv_row(w_ref, src_ref, index, channels):
    window = src_ref[rows(index, 3, channels), :]
    taps = jnp.dot(w_ref[...], window, preferred_element_type=F32)
    width = taps.shape[1]
    return (
        pltpu.roll(taps[0:channels], 1, 1)
        + taps[channels : 2 * channels]
        + pltpu.roll(taps[2 * channels : 3 * channels], width - 1, 1)
    )


def silu_and_slope(act, keep=None):
    gate = 0.5 * jnp.tanh(0.5 * act) + 0.5
    if keep is not None:
        gate = gate * keep
    hidden = act * gate
    return hidden.astype(BF16), gate * (1.0 + act - hidden)


def ext_edges(channels, height, mid_ref, a_ref, b_ref, top, bottom, odd):
    edge = HALO * channels
    top[edge : 2 * edge, :] = mid_ref[0:edge, :]
    bottom[0:edge, :] = mid_ref[(height - HALO) * channels : height * channels, :]

    @pl.when(odd == 1)
    def _():
        top[0:edge, :] = a_ref[...]
        bottom[edge : 2 * edge, :] = b_ref[...]

    @pl.when(odd == 0)
    def _():
        top[0:edge, :] = b_ref[...]
        bottom[edge : 2 * edge, :] = a_ref[...]


def forward_inner_kernel(
    channels, height,
    xt_ref, raw1_ref, raw2_ref,
    hid_ref, slope_ref, res_ref, w1_ref, w2_ref, w1t_ref, w2t_ref,
):
    stack_forward(raw1_ref, w1_ref)
    stack_forward(raw2_ref, w2_ref)
    for i in range(height - 2):
        act = conv_row(w1_ref, xt_ref, i, channels)
        hid_ref[rows(i, 1, channels), :], slope_ref[rows(i, 1, channels), :] = silu_and_slope(act)
    for i in range(height - 4):
        res_ref[rows(i, 1, channels), :] = conv_row(w2_ref, hid_ref, i, channels)
    stack_backward(raw1_ref, w1t_ref)
    stack_backward(raw2_ref, w2t_ref)


def on_grid():
    me = lax.axis_index("lat")
    count = lax.axis_size("lat")
    return jnp.where(me == 0, 0.0, 1.0), jnp.where(me == count - 1, 0.0, 1.0)


def forward_edge_kernel(
    channels, height,
    xt_ref, a_ref, b_ref, hid_ref, w1_ref, w2_ref,
    slope_ref, res_ref,
    top, bottom, hid_top, hid_bottom,
):
    odd = lax.axis_index("lat") % 2
    ext_edges(channels, height, xt_ref, a_ref, b_ref, top, bottom, odd)
    has_above, has_below = on_grid()
    inner = (height - 2 - HALO) * channels
    hid_top[2 * channels : 4 * channels, :] = hid_ref[0 : 2 * channels, :]
    hid_bottom[0 : 2 * channels, :] = hid_ref[inner : inner + 2 * channels, :]
    for i, keep in ((0, has_above), (1, None)):
        act = conv_row(w1_ref, top, i, channels)
        hid_top[rows(i, 1, channels), :], slope_ref[rows(i, 1, channels), :] = silu_and_slope(act, keep)
    for i, keep in ((0, None), (1, has_below)):
        act = conv_row(w1_ref, bottom, i, channels)
        hid_bottom[rows(2 + i, 1, channels), :], slope_ref[rows(2 + i, 1, channels), :] = (
            silu_and_slope(act, keep)
        )
    for i in range(2):
        res_ref[rows(i, 1, channels), :] = conv_row(w2_ref, hid_top, i, channels)
        res_ref[rows(2 + i, 1, channels), :] = conv_row(w2_ref, hid_bottom, i, channels)


def tile_kernel(
    channels, height, columns, span,
    route_ref, xt_ref, inner_ref, edge_ref, ow_ref, own_ref, za_ref, zb_ref, *refs,
):
    near_refs, (guide_ref, low_ref, ga_ref, gb_ref) = refs[: span - 1], refs[span - 1 :]
    slots = BLK_LON
    across = columns // BLK_LON
    p, z_odd, _ = place_in_plane(span)
    guide_ref[...] = jnp.zeros_like(guide_ref)
    jobs = [
        (span, own_ref.at[0]),
        (jnp.where(z_odd == 1, 0, 2 * span), za_ref.at[p]),
        (jnp.where(z_odd == 1, 2 * span, 0), zb_ref.at[p]),
    ]
    for m in range(1, span):
        step = lax.bitwise_xor(p, m) - p
        jobs.append((span + step, near_refs[m - 1].at[0]))
        jobs.append((jnp.where(step > 0, step, 2 * span + step), near_refs[m - 1].at[1]))
    obs_weight = as_column(ow_ref[...])
    down = height // BLK_LAT
    places, blocks = [], []
    for k, ref in jobs:
        n = route_ref[0, k]
        r, q = n // across, n % across
        inside = (r > 0) & (r < down - 1)
        place, block = [], []
        for i in range(BLK_LAT):
            lanes = pl.ds(pl.multiple_of(q * BLK_LON, BLK_LON), BLK_LON)
            here = (rows(r * BLK_LAT + i, 1, channels), lanes)
            row_in = jnp.clip(r * BLK_LAT + i - HALO, 0, height - 2 * HALO - 1)
            row_edge = jnp.where(r == 0, i, HALO + i)
            res = jnp.where(
                inside,
                inner_ref[rows(row_in, 1, channels), lanes],
                edge_ref[rows(row_edge, 1, channels), lanes],
            )
            place.append(here)
            block.append((xt_ref[here].astype(F32) + res).astype(BF16))
        places.append(place)
        blocks.append(block)
    misfits = []
    for (k, ref), block in zip(jobs, blocks):
        predicted = jnp.zeros((channels, slots), F32)
        for i in range(BLK_LAT):
            predicted += lax.dot_general(
                block[i],
                ref[i * slots : (i + 1) * slots, :],
                (((1,), (1,)), ((), ())),
                preferred_element_type=F32,
            )
        obs = ref[BLK_LAT * slots : BLK_LAT * slots + channels, :].astype(F32)
        misfits.append(((obs - predicted) * obs_weight).astype(BF16))
    terms = [
        [
            jnp.dot(misfit, ref[i * slots : (i + 1) * slots, :], preferred_element_type=F32)
            .astype(BF16)
            .astype(F32)
            for i in range(BLK_LAT)
        ]
        for (k, ref), misfit in zip(jobs, misfits)
    ]
    for place, term in zip(places, terms):
        for i in range(BLK_LAT):
            guide_ref[place[i]] += term[i]
    low_ref[...] = guide_ref[...].astype(BF16)
    edge_pair(low_ref, ga_ref, gb_ref, height, channels)


def backward_inner_kernel(
    channels, height,
    guide_ref, low_ref, slope_ref, res_ref, prior_ref, w2_ref, w1_ref,
    adj_ref, score_ref,
):
    for i in range(height - 2):
        here = rows(i, 1, channels)
        adj_ref[here, :] = (slope_ref[here, :] * conv_row(w2_ref, low_ref, i, channels)).astype(BF16)
    prior = as_column(prior_ref[...])
    for i in range(height - 4):
        here = rows(i, 1, channels)
        back = conv_row(w1_ref, adj_ref, i, channels)
        guide = guide_ref[rows(i + HALO, 1, channels), :]
        score_ref[here, :] = (prior * res_ref[here, :] + guide + back).astype(BF16)


def backward_edge_kernel(
    channels, height,
    guide_ref, low_ref, a_ref, b_ref, slope_ref, res_ref, prior_ref, adj_ref, score_ref, w2_ref, w1_ref,
    out_ref,
    top, bottom, adj_top, adj_bottom, edge_ref,
):
    odd = lax.axis_index("lat") % 2
    ext_edges(channels, height, low_ref, a_ref, b_ref, top, bottom, odd)
    inner = (height - 2 - HALO) * channels
    adj_top[2 * channels : 4 * channels, :] = adj_ref[0 : 2 * channels, :]
    adj_bottom[0 : 2 * channels, :] = adj_ref[inner : inner + 2 * channels, :]
    for i in range(2):
        adj_top[rows(i, 1, channels), :] = (
            slope_ref[rows(i, 1, channels), :] * conv_row(w2_ref, top, i, channels)
        ).astype(BF16)
        adj_bottom[rows(2 + i, 1, channels), :] = (
            slope_ref[rows(2 + i, 1, channels), :] * conv_row(w2_ref, bottom, i, channels)
        ).astype(BF16)
    prior = as_column(prior_ref[...])
    for i in range(2):
        for src, at, row in ((adj_top, i, i), (adj_bottom, HALO + i, height - HALO + i)):
            here = rows(at, 1, channels)
            back = conv_row(w1_ref, src, i, channels)
            edge_ref[here, :] = (
                prior * res_ref[here, :] + guide_ref[rows(row, 1, channels), :] + back
            ).astype(BF16)
    for start, size in channel_groups(channels):
        n = size * height
        picked = []
        for r in range(height):
            if r < HALO:
                src, at = edge_ref, r
            elif r < height - HALO:
                src, at = score_ref, r - HALO
            else:
                src, at = edge_ref, r - height + 2 * HALO
            picked.append(src[at * channels + start : at * channels + start + size, :])
        out_ref[start * height : start * height + n, :] = jnp.dot(
            permutation(height, size, True), jnp.concatenate(picked, axis=0), preferred_element_type=F32
        ).astype(BF16)


def pairs(groups, count, partner):
    found = []
    for g in range(groups):
        for i in range(count):
            other = partner(i)
            if 0 <= other < count:
                found.append((g * count + i, g * count + other))
            elif groups % 2 == 0:
                found.append((g * count + i, (g ^ 1) * count + i))
    return found


def local(
    noisy_state, w_first, w_second, prior_weight, obs_weight, block_route, counts, tile_weights, observations
):
    channels, height, columns = noisy_state.shape
    tile_total = block_route.shape[1]
    span = tile_total // 2
    slots = tile_weights.shape[2]
    count = lax.axis_size("lat")
    pack_rows = BLK_LAT * slots + channels
    taps = w_first.shape[0]

    def field(n, dtype=BF16):
        return shape((n * channels, columns), dtype)

    def buffer(n, dtype=BF16):
        return pltpu.VMEM((n * channels, columns), dtype)

    def exchange(x, partner):
        return lax.ppermute(x, ("grp", "lat"), pairs(lax.axis_size("grp"), count, partner))

    def swap(x, step, parity):
        return exchange(x, lambda i: i + step if (i // step) % 2 == parity else i - step)

    packed = shape((span, pack_rows, BLK_LON))
    def in_hbm(x):
        return pltpu.with_memory_space_constraint(x, pltpu.HBM)

    xt, ha, hb, za, zb, own = pl.pallas_call(
        functools.partial(prepare_kernel, channels, height, span),
        out_shape=(field(height), field(HALO), field(HALO), packed, packed, packed),
        in_specs=[SM, HB, HB, HB],
        out_specs=[VM] * 6,
        scratch_shapes=[
            pltpu.VMEM((channels * height, columns), BF16),
            pltpu.VMEM(tile_weights.shape[1:], BF16),
            pltpu.VMEM(observations.shape[1:], BF16),
            pltpu.SemaphoreType.DMA((len(channel_groups(channels)) + 2,)),
        ],
        compiler_params=params(),
    )(
        counts,
        in_hbm(noisy_state.reshape(channels * height, columns)),
        in_hbm(tile_weights),
        in_hbm(observations),
    )
    ha, hb = swap(ha, 1, 0), swap(hb, 1, 1)
    za, zb = swap(za, span, 0), swap(zb, span, 1)

    weight = shape((taps * channels, taps * channels))
    hid, slope_in, res_in, w1, w2, w1t, w2t = pl.pallas_call(
        functools.partial(forward_inner_kernel, channels, height),
        out_shape=(field(height - 2), field(height - 2, F32), field(height - 4, F32)) + (weight,) * 4,
        in_specs=[VM] * 3,
        out_specs=[VM] * 7,
        compiler_params=params(),
    )(xt, w_first, w_second)

    relayed = pl.pallas_call(
        functools.partial(relay_kernel, span),
        out_shape=tuple(shape((2, pack_rows, BLK_LON)) for _ in range(span - 1)),
        in_specs=[AN] + [VM] * 3,
        out_specs=[VM] * (span - 1),
        compiler_params=params(),
    )(w1, za, zb, own)
    arrived = [exchange(relayed[m - 1], lambda i, m=m: i ^ m) for m in range(1, span)]

    slope_ed, res_ed = pl.pallas_call(
        functools.partial(forward_edge_kernel, channels, height),
        out_shape=(field(2 * HALO, F32), field(2 * HALO, F32)),
        in_specs=[VM] * 6,
        out_specs=[VM] * 2,
        scratch_shapes=[buffer(2 * HALO)] * 4,
        compiler_params=params(),
    )(xt, ha, hb, hid, w1, w2)

    guide, low, ga, gb = pl.pallas_call(
        functools.partial(tile_kernel, channels, height, columns, span),
        out_shape=(field(height, F32), field(height), field(HALO), field(HALO)),
        in_specs=[SM] + [VM] * (7 + span - 1),
        out_specs=[VM] * 4,
        compiler_params=params(),
    )(block_route, xt, res_in, res_ed, obs_weight[None, :], own, za, zb, *arrived)
    ga, gb = swap(ga, 1, 0), swap(gb, 1, 1)

    prior = prior_weight[None, :]
    adj, score = pl.pallas_call(
        functools.partial(backward_inner_kernel, channels, height),
        out_shape=(field(height - 2), field(height - 4)),
        in_specs=[VM] * 7,
        out_specs=[VM] * 2,
        compiler_params=params(),
    )(guide, low, slope_in, res_in, prior, w2t, w1t)

    out = pl.pallas_call(
        functools.partial(backward_edge_kernel, channels, height),
        out_shape=shape((channels * height, columns)),
        in_specs=[VM] * 11,
        out_specs=VM,
        scratch_shapes=[buffer(2 * HALO)] * 5,
        compiler_params=params(),
    )(guide, low, ga, gb, slope_ed, res_ed, prior, adj, score, w2t, w1t)
    return out.reshape(channels, height, columns)


def solution(mesh):
    in_specs = (
        P("grp", "lat", None),
        P(),
        P(),
        P(),
        P(),
        P(("grp", "lat"), None),
        P(("grp", "lat"), None),
        P(("grp", "lat"), None, None, None),
        P(("grp", "lat"), None, None, None),
    )
    out_specs = P("grp", "lat", None)
    return jax.shard_map(local, mesh=mesh, in_specs=in_specs, out_specs=out_specs, check_vma=False)
```

```python
import functools

import jax
import jax.numpy as jnp
from jax import lax
from jax.experimental import pallas as pl
from jax.experimental.pallas import tpu as pltpu
from jax.sharding import PartitionSpec as P

BLK_LAT = 2
BLK_LON = 128
HALO = 2
F32 = jnp.float32
BF16 = jnp.bfloat16

VM = pl.BlockSpec(memory_space=pltpu.VMEM)
SM = pl.BlockSpec(memory_space=pltpu.SMEM)
HB = pl.BlockSpec(memory_space=pltpu.HBM)
AN = pl.BlockSpec(memory_space=pl.ANY)


def params(mib=16):
    return pltpu.CompilerParams(vmem_limit_bytes=mib << 20)


def shape(dims, dtype=BF16):
    return jax.ShapeDtypeStruct(dims, dtype)


def rows(index, count, channels):
    start = index * channels
    if not isinstance(start, int):
        start = pl.multiple_of(start, 16)
    return pl.ds(start, count * channels)


def permutation(height, group, back):
    n = height * group
    out = lax.broadcasted_iota(jnp.int32, (n, n), 0)
    src = lax.broadcasted_iota(jnp.int32, (n, n), 1)
    if back:
        want = (out % height) * group + out // height
    else:
        want = (out % group) * height + out // group
    return jnp.where(src == want, 1.0, 0.0).astype(BF16)


def channel_groups(channels):
    return [(start, min(32, channels - start)) for start in range(0, channels, 32)]


def as_column(row):
    n = row.shape[1]
    here = lax.broadcasted_iota(jnp.int32, (n, n), 0) == lax.broadcasted_iota(jnp.int32, (n, n), 1)
    return jnp.sum(jnp.where(here, jnp.broadcast_to(row, (n, n)), 0.0), axis=1, keepdims=True)


def place_in_plane(span):
    me = lax.axis_index("lat")
    return me % span, (me // span) % 2, me % 2


def pack_tile(k, dst, w_ref, obs_ref, count_ref, slots, channels):
    live = lax.broadcasted_iota(jnp.int32, (slots, BLK_LON), 0) < count_ref[0, k]
    zero = jnp.zeros((slots, BLK_LON), BF16)
    for i in range(BLK_LAT):
        half = w_ref[k, :, i * BLK_LON : (i + 1) * BLK_LON]
        dst[i * slots : (i + 1) * slots, :] = jnp.where(live, half, zero)
    dst[BLK_LAT * slots : BLK_LAT * slots + channels, :] = obs_ref[k]


def edge_pair(src_ref, ha_ref, hb_ref, height, channels):
    me, odd = lax.axis_index("lat"), lax.axis_index("lat") % 2
    last = height - HALO
    ha_ref[...] = src_ref[rows(last * (1 - odd), HALO, channels), :]
    alone = (me == 0) | (me == lax.axis_size("lat") - 1)

    @pl.when(alone)
    def _():
        hb_ref[...] = jnp.zeros_like(hb_ref)

    @pl.when(jnp.logical_not(alone))
    def _():
        hb_ref[...] = src_ref[rows(last * odd, HALO, channels), :]


def pack_kernel(
    channels, span,
    count_hbm, w_hbm, obs_hbm, x_hbm,
    za_ref, zb_ref, own_ref, x_ref,
    count_ref, w_ref, obs_ref, sems,
):
    copies = [
        pltpu.make_async_copy(count_hbm, count_ref, sems.at[0]),
        pltpu.make_async_copy(w_hbm.at[0], w_ref, sems.at[1]),
        pltpu.make_async_copy(obs_hbm.at[0], obs_ref, sems.at[2]),
        pltpu.make_async_copy(x_hbm, x_ref, sems.at[3]),
    ]
    for copy in copies:
        copy.start()
    for copy in copies[:3]:
        copy.wait()
    p, z_odd, _ = place_in_plane(span)
    slots = w_ref.shape[1]
    pack = functools.partial(
        pack_tile, w_ref=w_ref, obs_ref=obs_ref, count_ref=count_ref, slots=slots, channels=channels
    )
    for j in range(span):
        up = jnp.maximum(p - j, 0)
        down = jnp.minimum(2 * span + p - j, 2 * span)
        pack(jnp.where(z_odd == 1, down, up), za_ref.at[j])
        pack(jnp.where(z_odd == 1, up, down), zb_ref.at[j])
        if j == 0:
            pack(span, own_ref.at[0])
        else:
            pack(span + p - lax.bitwise_xor(p, j), own_ref.at[j])
    copies[3].wait()


def prepare_kernel(channels, height, x_ref, after_ref, xt_ref, ha_ref, hb_ref):
    for start, size in channel_groups(channels):
        n = size * height
        moved = jnp.dot(
            permutation(height, size, False),
            x_ref[start * height : start * height + n, :],
            preferred_element_type=F32,
        ).astype(BF16)
        for r in range(height):
            xt_ref[r * channels + start : r * channels + start + size, :] = (
                moved[r * size : (r + 1) * size, :]
            )
    edge_pair(xt_ref, ha_ref, hb_ref, height, channels)


def relay_kernel(span, after_ref, za_ref, zb_ref, own_ref, *outs):
    p, z_odd, _ = place_in_plane(span)
    for m in range(1, span):
        to = lax.bitwise_xor(p, m)
        below = jnp.where(to < p, 1, 0)
        outs[m - 1][0] = own_ref[m]

        @pl.when(below == z_odd)
        def _():
            outs[m - 1][1] = za_ref[to]

        @pl.when(below != z_odd)
        def _():
            outs[m - 1][1] = zb_ref[to]


def stack_forward(raw_ref, dst):
    taps, _, outs, ins = raw_ref.shape
    total = jnp.zeros(dst.shape, F32)
    for a in range(taps):
        block = raw_ref[a].reshape(taps * outs, ins)
        to = lax.broadcasted_iota(jnp.int32, (ins, taps * ins), 1)
        pick = jnp.where(to == lax.broadcasted_iota(jnp.int32, to.shape, 0) + a * ins, 1.0, 0.0)
        total += jnp.dot(block, pick.astype(BF16), preferred_element_type=F32)
    dst[...] = total.astype(BF16)


def stack_backward(raw_ref, dst, shifts):
    taps, _, outs, ins = raw_ref.shape
    n, width = taps * outs, dst.shape[1]
    src = lax.broadcasted_iota(jnp.int32, (n, width), 0)
    to = lax.broadcasted_iota(jnp.int32, (n, width), 1)
    for half, shift in enumerate(shifts):
        pick = jnp.where(src == to + shift * outs, 1.0, 0.0).astype(BF16)
        for b in range(taps):
            block = jnp.concatenate([raw_ref[taps - 1 - a, taps - 1 - b] for a in range(taps)], axis=0)
            start = (half * taps + b) * ins
            dst[start : start + ins, :] = lax.dot_general(
                block, pick, (((0,), (0,)), ((), ())), preferred_element_type=F32
            ).astype(BF16)


def join_taps(taps, channels):
    width = taps.shape[1]
    return (
        pltpu.roll(taps[0:channels], 1, 1)
        + taps[channels : 2 * channels]
        + pltpu.roll(taps[2 * channels : 3 * channels], width - 1, 1)
    )


def conv_row(w_ref, src_ref, index, channels):
    window = src_ref[rows(index, 3, channels), :]
    return join_taps(jnp.dot(w_ref[...], window, preferred_element_type=F32), channels)


def conv_pair(w_ref, window, channels):
    taps = jnp.dot(w_ref[...], window, preferred_element_type=F32)
    return join_taps(taps[: 3 * channels], channels), join_taps(taps[3 * channels :], channels)


def silu_and_slope(act, keep=None):
    gate = 0.5 * jnp.tanh(0.5 * act) + 0.5
    if keep is not None:
        gate = gate * keep
    hidden = act * gate
    return hidden.astype(BF16), gate * (1.0 + act - hidden)


def ext_edges(channels, height, mid_ref, a_ref, b_ref, top, bottom, odd):
    edge = HALO * channels
    top[edge : 2 * edge, :] = mid_ref[0:edge, :]
    bottom[0:edge, :] = mid_ref[(height - HALO) * channels : height * channels, :]

    @pl.when(odd == 1)
    def _():
        top[0:edge, :] = a_ref[...]
        bottom[edge : 2 * edge, :] = b_ref[...]

    @pl.when(odd == 0)
    def _():
        top[0:edge, :] = b_ref[...]
        bottom[edge : 2 * edge, :] = a_ref[...]


def forward_inner_kernel(
    channels, height,
    xt_ref, raw1_ref, raw2_ref,
    hid_ref, slope_ref, res_ref, w1_ref, w2_ref,
):
    stack_forward(raw1_ref, w1_ref)
    stack_forward(raw2_ref, w2_ref)
    for i in range(height - 2):
        act = conv_row(w1_ref, xt_ref, i, channels)
        hid_ref[rows(i, 1, channels), :], slope_ref[rows(i, 1, channels), :] = silu_and_slope(act)
    for i in range(height - 4):
        res_ref[rows(i, 1, channels), :] = conv_row(w2_ref, hid_ref, i, channels)


def on_grid():
    me = lax.axis_index("lat")
    count = lax.axis_size("lat")
    return jnp.where(me == 0, 0.0, 1.0), jnp.where(me == count - 1, 0.0, 1.0)


def forward_edge_kernel(
    channels, height,
    xt_ref, a_ref, b_ref, hid_ref, w1_ref, w2_ref, raw1_ref, raw2_ref,
    slope_ref, res_ref, w1t_ref, w2t_ref, above1_ref, above2_ref, below1_ref, below2_ref,
    top, bottom, hid_top, hid_bottom,
):
    odd = lax.axis_index("lat") % 2
    ext_edges(channels, height, xt_ref, a_ref, b_ref, top, bottom, odd)
    has_above, has_below = on_grid()
    inner = (height - 2 - HALO) * channels
    hid_top[2 * channels : 4 * channels, :] = hid_ref[0 : 2 * channels, :]
    hid_bottom[0 : 2 * channels, :] = hid_ref[inner : inner + 2 * channels, :]
    for i, keep in ((0, has_above), (1, None)):
        act = conv_row(w1_ref, top, i, channels)
        hid_top[rows(i, 1, channels), :], slope_ref[rows(i, 1, channels), :] = silu_and_slope(act, keep)
    for i, keep in ((0, None), (1, has_below)):
        act = conv_row(w1_ref, bottom, i, channels)
        hid_bottom[rows(2 + i, 1, channels), :], slope_ref[rows(2 + i, 1, channels), :] = (
            silu_and_slope(act, keep)
        )
    for i in range(2):
        res_ref[rows(i, 1, channels), :] = conv_row(w2_ref, hid_top, i, channels)
        res_ref[rows(2 + i, 1, channels), :] = conv_row(w2_ref, hid_bottom, i, channels)
    for raw_ref, full, above, below in (
        (raw1_ref, w1t_ref, above1_ref, below1_ref),
        (raw2_ref, w2t_ref, above2_ref, below2_ref),
    ):
        stack_backward(raw_ref, full, (0,))
        stack_backward(raw_ref, above, (0, -1))
        stack_backward(raw_ref, below, (2, 1))


def early_jobs(span, own_ref, za_ref, zb_ref, near_refs):
    p, z_odd, _ = place_in_plane(span)
    jobs = [
        (span, own_ref.at[0]),
        (jnp.where(z_odd == 1, 0, 2 * span), za_ref.at[p]),
        (jnp.where(z_odd == 1, 2 * span, 0), zb_ref.at[p]),
    ]
    return jobs + plane_jobs(span, range(1, 1 + len(near_refs)), near_refs)


def plane_jobs(span, partners, near_refs):
    p, _, _ = place_in_plane(span)
    jobs = []
    for m, ref in zip(partners, near_refs):
        step = lax.bitwise_xor(p, m) - p
        jobs.append((span + step, ref.at[0]))
        jobs.append((jnp.where(step > 0, step, 2 * span + step), ref.at[1]))
    return jobs


def tile_terms(jobs, route_ref, xt_ref, inner_ref, edge_ref, obs_weight, channels, height, columns):
    slots = BLK_LON
    across, down = columns // BLK_LON, height // BLK_LAT
    places, blocks = [], []
    for k, _ in jobs:
        n = route_ref[0, k]
        r, q = n // across, n % across
        inside = (r > 0) & (r < down - 1)
        lanes = pl.ds(pl.multiple_of(q * BLK_LON, BLK_LON), BLK_LON)
        block = []
        for i in range(BLK_LAT):
            row_in = jnp.clip(r * BLK_LAT + i - HALO, 0, height - 2 * HALO - 1)
            row_edge = jnp.where(r == 0, i, HALO + i)
            res = jnp.where(
                inside,
                inner_ref[rows(row_in, 1, channels), lanes],
                edge_ref[rows(row_edge, 1, channels), lanes],
            )
            here = (rows(r * BLK_LAT + i, 1, channels), lanes)
            block.append((xt_ref[here].astype(F32) + res).astype(BF16))
        places.append((r, lanes))
        blocks.append(block)
    misfits = []
    for (_, ref), block in zip(jobs, blocks):
        predicted = jnp.zeros((channels, slots), F32)
        for i in range(BLK_LAT):
            predicted += lax.dot_general(
                block[i],
                ref[i * slots : (i + 1) * slots, :],
                (((1,), (1,)), ((), ())),
                preferred_element_type=F32,
            )
        obs = ref[BLK_LAT * slots : BLK_LAT * slots + channels, :].astype(F32)
        misfits.append(((obs - predicted) * obs_weight).astype(BF16))
    terms = [
        [
            jnp.dot(misfit, ref[i * slots : (i + 1) * slots, :], preferred_element_type=F32).astype(BF16)
            for i in range(BLK_LAT)
        ]
        for (_, ref), misfit in zip(jobs, misfits)
    ]
    return places, terms


def early_tile_kernel(
    channels, height, columns, span,
    route_hbm, xt_ref, inner_ref, edge_ref, ow_ref, own_ref, za_ref, zb_ref, near_ref,
    guide_ref,
    route_ref, sem,
):
    copy = pltpu.make_async_copy(route_hbm, route_ref, sem)
    copy.start()
    guide_ref[...] = jnp.zeros_like(guide_ref)
    copy.wait()
    jobs = early_jobs(span, own_ref, za_ref, zb_ref, [near_ref])
    places, terms = tile_terms(
        jobs, route_ref, xt_ref, inner_ref, edge_ref, as_column(ow_ref[...]), channels, height, columns
    )
    for (r, lanes), term in zip(places, terms):
        for i in range(BLK_LAT):
            guide_ref[rows(r * BLK_LAT + i, 1, channels), lanes] += term[i].astype(F32)


def late_tile_kernel(
    channels, height, columns, span,
    route_ref, xt_ref, inner_ref, edge_ref, ow_ref, guide_ref, *refs,
):
    near_refs, (late_ref, ga_ref, gb_ref, sums, low) = refs[: span - 2], refs[span - 2 :]
    edge = HALO * channels
    last = (height - HALO) * channels
    sums[0:edge, :] = guide_ref[0:edge, :]
    sums[edge : 2 * edge, :] = guide_ref[last : last + edge, :]
    jobs = plane_jobs(span, range(2, span), near_refs)
    places, terms = tile_terms(
        jobs, route_ref, xt_ref, inner_ref, edge_ref, as_column(ow_ref[...]), channels, height, columns
    )
    down = height // BLK_LAT
    for index, ((r, lanes), term) in enumerate(zip(places, terms)):
        part = jnp.where(r == 0, 0, jnp.where(r == down - 1, 1, 2))
        for i in range(BLK_LAT):
            late_ref[index, i] = term[i]
            sums[rows(part * HALO + i, 1, channels), lanes] += term[i].astype(F32)
    low[...] = sums[0 : 2 * edge, :].astype(BF16)
    edge_pair(low, ga_ref, gb_ref, 2 * HALO, channels)


def backward_inner_kernel(
    channels, height, columns, span,
    route_ref, early_ref, late_ref, slope_ref, inner_ref, edge_ref, prior_ref, w2_ref, w1_ref,
    part_adj_ref, part_score_ref, score_ref,
    guide, low, adj,
):
    guide[...] = early_ref[...]
    across = columns // BLK_LON
    jobs = plane_jobs(span, range(2, span), [late_ref] * (span - 2))
    for index, (k, _) in enumerate(jobs):
        n = route_ref[0, k]
        lanes = pl.ds(pl.multiple_of((n % across) * BLK_LON, BLK_LON), BLK_LON)
        for i in range(BLK_LAT):
            here = (rows((n // across) * BLK_LAT + i, 1, channels), lanes)
            guide[here] += late_ref[index, i].astype(F32)
    edge = HALO * channels
    none = jnp.zeros((edge, columns), BF16)
    low[0:edge, :] = none
    low[edge : edge + height * channels, :] = guide[...].astype(BF16)
    low[edge + height * channels :, :] = none
    adj[0:edge, :] = none
    adj[height * channels :, :] = none
    for i in range(height + 2):
        part = conv_row(w2_ref, low, i, channels)
        if HALO <= i < height:
            adj[rows(i, 1, channels), :] = (slope_ref[rows(i - HALO, 1, channels), :] * part).astype(BF16)
        else:
            part_adj_ref[rows(i if i < HALO else i - height + HALO, 1, channels), :] = part
    prior = as_column(prior_ref[...])
    for i in range(height):
        part = conv_row(w1_ref, adj, i, channels) + guide[rows(i, 1, channels), :]
        if HALO <= i < height - HALO:
            here = rows(i - HALO, 1, channels)
            score_ref[here, :] = (prior * inner_ref[here, :] + part).astype(BF16)
        else:
            here = rows(i if i < HALO else i - height + 2 * HALO, 1, channels)
            part_score_ref[here, :] = prior * edge_ref[here, :] + part


def backward_edge_kernel(
    channels, height,
    a_ref, b_ref, slope_ref, part_adj_ref, part_score_ref, score_ref,
    above2_ref, below2_ref, above1_ref, below1_ref,
    out_hbm,
    out_ref, edge_ref, sems,
):
    odd = lax.axis_index("lat") % 2
    first, second = a_ref[...], b_ref[...]
    for at, window, w2_ref, w1_ref in (
        (0, jnp.where(odd == 1, first, second), above2_ref, above1_ref),
        (HALO, jnp.where(odd == 1, second, first), below2_ref, below1_ref),
    ):
        here = [rows(at + i, 1, channels) for i in range(HALO)]
        adj = [
            (slope_ref[place, :] * (part_adj_ref[place, :] + back)).astype(BF16)
            for place, back in zip(here, conv_pair(w2_ref, window, channels))
        ]
        for place, back in zip(here, conv_pair(w1_ref, jnp.concatenate(adj, axis=0), channels)):
            edge_ref[place, :] = (part_score_ref[place, :] + back).astype(BF16)
    copies = []
    for start, size in channel_groups(channels):
        n = size * height
        picked = []
        for r in range(height):
            if r < HALO:
                src, at = edge_ref, r
            elif r < height - HALO:
                src, at = score_ref, r - HALO
            else:
                src, at = edge_ref, r - height + 2 * HALO
            picked.append(src[at * channels + start : at * channels + start + size, :])
        part = pl.ds(start * height, n)
        out_ref[part, :] = jnp.dot(
            permutation(height, size, True), jnp.concatenate(picked, axis=0), preferred_element_type=F32
        ).astype(BF16)
        copies.append(pltpu.make_async_copy(out_ref.at[part], out_hbm.at[part], sems.at[len(copies)]))
        copies[-1].start()
    for copy in copies:
        copy.wait()


def pairs(groups, count, partner):
    found = []
    for g in range(groups):
        for i in range(count):
            other = partner(i)
            if 0 <= other < count:
                found.append((g * count + i, g * count + other))
            elif groups % 2 == 0:
                found.append((g * count + i, (g ^ 1) * count + i))
    return found


def local(
    noisy_state, w_first, w_second, prior_weight, obs_weight, block_route, counts, tile_weights, observations
):
    channels, height, columns = noisy_state.shape
    tile_total = block_route.shape[1]
    span = tile_total // 2
    slots = tile_weights.shape[2]
    count = lax.axis_size("lat")
    pack_rows = BLK_LAT * slots + channels
    taps = w_first.shape[0]

    def field(n, dtype=BF16):
        return shape((n * channels, columns), dtype)

    def buffer(n, dtype=BF16):
        return pltpu.VMEM((n * channels, columns), dtype)

    def exchange(x, partner):
        return lax.ppermute(x, ("grp", "lat"), pairs(lax.axis_size("grp"), count, partner))

    def swap(x, step, parity):
        return exchange(x, lambda i: i + step if (i // step) % 2 == parity else i - step)

    packed = shape((span, pack_rows, BLK_LON))
    def in_hbm(x):
        return pltpu.with_memory_space_constraint(x, pltpu.HBM)

    za_send, zb_send, own, x = pl.pallas_call(
        functools.partial(pack_kernel, channels, span),
        out_shape=(packed, packed, packed, field(height)),
        in_specs=[HB] * 4,
        out_specs=[VM] * 4,
        scratch_shapes=[
            pltpu.SMEM(counts.shape, jnp.int32),
            pltpu.VMEM(tile_weights.shape[1:], BF16),
            pltpu.VMEM(observations.shape[1:], BF16),
            pltpu.SemaphoreType.DMA((4,)),
        ],
        compiler_params=params(),
    )(
        in_hbm(counts),
        in_hbm(tile_weights),
        in_hbm(observations),
        in_hbm(noisy_state.reshape(channels * height, columns)),
    )
    za, zb = swap(za_send, span, 0), swap(zb_send, span, 1)
    xt, ha, hb = pl.pallas_call(
        functools.partial(prepare_kernel, channels, height),
        out_shape=(field(height), field(HALO), field(HALO)),
        in_specs=[VM, AN],
        out_specs=[VM] * 3,
        compiler_params=params(),
    )(x, za_send)
    ha, hb = swap(ha, 1, 0), swap(hb, 1, 1)

    weight = shape((taps * channels, taps * channels))
    pair_weight = shape((HALO * taps * channels, HALO * channels))
    hid, slope_in, res_in, w1, w2 = pl.pallas_call(
        functools.partial(forward_inner_kernel, channels, height),
        out_shape=(field(height - 2), field(height - 2, F32), field(height - 4, F32), weight, weight),
        in_specs=[VM] * 3,
        out_specs=[VM] * 5,
        compiler_params=params(),
    )(xt, w_first, w_second)

    relayed = pl.pallas_call(
        functools.partial(relay_kernel, span),
        out_shape=tuple(shape((2, pack_rows, BLK_LON)) for _ in range(span - 1)),
        in_specs=[AN] + [VM] * 3,
        out_specs=[VM] * (span - 1),
        compiler_params=params(),
    )(w1, za, zb, own)
    arrived = [exchange(relayed[m - 1], lambda i, m=m: i ^ m) for m in range(1, span)]

    slope_ed, res_ed, w1t, w2t, above1, above2, below1, below2 = pl.pallas_call(
        functools.partial(forward_edge_kernel, channels, height),
        out_shape=(field(2 * HALO, F32), field(2 * HALO, F32), weight, weight) + (pair_weight,) * 4,
        in_specs=[VM] * 8,
        out_specs=[VM] * 8,
        scratch_shapes=[buffer(2 * HALO)] * 4,
        compiler_params=params(),
    )(xt, ha, hb, hid, w1, w2, w_first, w_second)

    observed = obs_weight[None, :]
    early = pl.pallas_call(
        functools.partial(early_tile_kernel, channels, height, columns, span),
        out_shape=field(height, F32),
        in_specs=[HB] + [VM] * 8,
        out_specs=VM,
        scratch_shapes=[pltpu.SMEM(block_route.shape, jnp.int32), pltpu.SemaphoreType.DMA],
        compiler_params=params(),
    )(in_hbm(block_route), xt, res_in, res_ed, observed, own, za, zb, arrived[0])

    late, ga, gb = pl.pallas_call(
        functools.partial(late_tile_kernel, channels, height, columns, span),
        out_shape=(
            shape((2 * (span - 2), BLK_LAT, channels, BLK_LON)),
            field(HALO),
            field(HALO),
        ),
        in_specs=[SM] + [VM] * (5 + span - 2),
        out_specs=[VM] * 3,
        scratch_shapes=[buffer(3 * HALO, F32), buffer(2 * HALO)],
        compiler_params=params(),
    )(block_route, xt, res_in, res_ed, observed, early, *arrived[1:])
    ga, gb = swap(ga, 1, 0), swap(gb, 1, 1)

    part_adj, part_score, score = pl.pallas_call(
        functools.partial(backward_inner_kernel, channels, height, columns, span),
        out_shape=(field(2 * HALO, F32), field(2 * HALO, F32), field(height - 2 * HALO)),
        in_specs=[SM] + [VM] * 8,
        out_specs=[VM] * 3,
        scratch_shapes=[buffer(height, F32), buffer(height + 2 * HALO), buffer(height + 2)],
        compiler_params=params(),
    )(block_route, early, late, slope_in, res_in, res_ed, prior_weight[None, :], w2t, w1t)

    out = pl.pallas_call(
        functools.partial(backward_edge_kernel, channels, height),
        out_shape=shape((channels * height, columns)),
        in_specs=[VM] * 10,
        out_specs=HB,
        scratch_shapes=[
            buffer(height),
            buffer(2 * HALO),
            pltpu.SemaphoreType.DMA((len(channel_groups(channels)),)),
        ],
        compiler_params=params(),
    )(ga, gb, slope_ed, part_adj, part_score, score, above2, below2, above1, below1)
    return out.reshape(channels, height, columns)


def solution(mesh):
    in_specs = (
        P("grp", "lat", None),
        P(),
        P(),
        P(),
        P(),
        P(("grp", "lat"), None),
        P(("grp", "lat"), None),
        P(("grp", "lat"), None, None, None),
        P(("grp", "lat"), None, None, None),
    )
    out_specs = P("grp", "lat", None)
    return jax.shard_map(local, mesh=mesh, in_specs=in_specs, out_specs=out_specs, check_vma=False)
```

```python
import functools

import jax
import jax.numpy as jnp
from jax import lax
from jax.experimental import pallas as pl
from jax.experimental.pallas import tpu as pltpu
from jax.sharding import PartitionSpec as P

BLK_LAT = 2
BLK_LON = 128
HALO = 2
F32 = jnp.float32
BF16 = jnp.bfloat16

VM = pl.BlockSpec(memory_space=pltpu.VMEM)
SM = pl.BlockSpec(memory_space=pltpu.SMEM)
HB = pl.BlockSpec(memory_space=pltpu.HBM)
AN = pl.BlockSpec(memory_space=pl.ANY)


def params(mib=16):
    return pltpu.CompilerParams(vmem_limit_bytes=mib << 20)


def shape(dims, dtype=BF16):
    return jax.ShapeDtypeStruct(dims, dtype)


def rows(index, count, channels):
    start = index * channels
    if not isinstance(start, int):
        start = pl.multiple_of(start, 16)
    return pl.ds(start, count * channels)


def permutation(height, group, back):
    n = height * group
    out = lax.broadcasted_iota(jnp.int32, (n, n), 0)
    src = lax.broadcasted_iota(jnp.int32, (n, n), 1)
    if back:
        want = (out % height) * group + out // height
    else:
        want = (out % group) * height + out // group
    return jnp.where(src == want, 1.0, 0.0).astype(BF16)


def channel_groups(channels):
    return [(start, min(32, channels - start)) for start in range(0, channels, 32)]


def as_column(row):
    n = row.shape[1]
    here = lax.broadcasted_iota(jnp.int32, (n, n), 0) == lax.broadcasted_iota(jnp.int32, (n, n), 1)
    return jnp.sum(jnp.where(here, jnp.broadcast_to(row, (n, n)), 0.0), axis=1, keepdims=True)


def place_in_plane(span):
    me = lax.axis_index("lat")
    return me % span, (me // span) % 2, me % 2


def pack_tile(k, dst, w_ref, obs_ref, count_ref, slots, channels):
    live = lax.broadcasted_iota(jnp.int32, (slots, BLK_LON), 0) < count_ref[0, k]
    zero = jnp.zeros((slots, BLK_LON), BF16)
    for i in range(BLK_LAT):
        half = w_ref[k, :, i * BLK_LON : (i + 1) * BLK_LON]
        dst[i * slots : (i + 1) * slots, :] = jnp.where(live, half, zero)
    dst[BLK_LAT * slots : BLK_LAT * slots + channels, :] = obs_ref[k]


def first_rows(src_ref, dst, height, channels):
    odd = lax.axis_index("lat") % 2
    dst[...] = src_ref[rows((height - HALO) * (1 - odd), HALO, channels), :]


def second_rows(src_ref, dst, height, channels):
    me, odd = lax.axis_index("lat"), lax.axis_index("lat") % 2
    alone = (me == 0) | (me == lax.axis_size("lat") - 1)

    @pl.when(alone)
    def _():
        dst[...] = jnp.zeros_like(dst)

    @pl.when(jnp.logical_not(alone))
    def _():
        dst[...] = src_ref[rows((height - HALO) * odd, HALO, channels), :]


def pack_kernel(
    channels, span,
    count_hbm, w_hbm, obs_hbm, x_hbm,
    za_ref, zb_ref, own_ref, near_ref, y2_ref, y3_ref, x_ref,
    count_ref, w_ref, obs_ref, sems,
):
    copies = [
        pltpu.make_async_copy(count_hbm, count_ref, sems.at[0]),
        pltpu.make_async_copy(w_hbm.at[0], w_ref, sems.at[1]),
        pltpu.make_async_copy(obs_hbm.at[0], obs_ref, sems.at[2]),
        pltpu.make_async_copy(x_hbm, x_ref, sems.at[3]),
    ]
    for copy in copies:
        copy.start()
    for copy in copies[:3]:
        copy.wait()
    p, z_odd, _ = place_in_plane(span)
    slots = w_ref.shape[1]
    pack = functools.partial(
        pack_tile, w_ref=w_ref, obs_ref=obs_ref, count_ref=count_ref, slots=slots, channels=channels
    )
    for j in range(span):
        up = jnp.maximum(p - j, 0)
        down = jnp.minimum(2 * span + p - j, 2 * span)
        pack(jnp.where(z_odd == 1, down, up), za_ref.at[j])
        pack(jnp.where(z_odd == 1, up, down), zb_ref.at[j])
    pack(span, own_ref)
    for j, dst in enumerate((near_ref, y2_ref, y3_ref), 1):
        pack(span + p - lax.bitwise_xor(p, j), dst)
    copies[3].wait()


def prepare_kernel(channels, height, x_ref, after_ref, xt_ref, hb_ref):
    for start, size in channel_groups(channels):
        n = size * height
        moved = jnp.dot(
            permutation(height, size, False),
            x_ref[start * height : start * height + n, :],
            preferred_element_type=F32,
        ).astype(BF16)
        for r in range(height):
            xt_ref[r * channels + start : r * channels + start + size, :] = (
                moved[r * size : (r + 1) * size, :]
            )
    second_rows(xt_ref, hb_ref, height, channels)


def relay_kernel(span, za_ref, zb_ref, near_ref, *refs):
    near_out, *far_outs = refs[-span + 1 :]
    p, z_odd, _ = place_in_plane(span)
    near_out[0] = near_ref[...]
    for m, out in enumerate([near_out.at[1]] + far_outs, 1):
        to = lax.bitwise_xor(p, m)
        below = jnp.where(to < p, 1, 0)

        @pl.when(below == z_odd)
        def _():
            out[...] = za_ref[to]

        @pl.when(below != z_odd)
        def _():
            out[...] = zb_ref[to]


def stack_forward(raw_ref, dst):
    taps, _, outs, ins = raw_ref.shape
    total = jnp.zeros(dst.shape, F32)
    for a in range(taps):
        block = raw_ref[a].reshape(taps * outs, ins)
        to = lax.broadcasted_iota(jnp.int32, (ins, taps * ins), 1)
        pick = jnp.where(to == lax.broadcasted_iota(jnp.int32, to.shape, 0) + a * ins, 1.0, 0.0)
        total += jnp.dot(block, pick.astype(BF16), preferred_element_type=F32)
    dst[...] = total.astype(BF16)


def stack_backward(raw_ref, by_row_ref, by_column_ref):
    taps, _, outs, ins = raw_ref.shape
    n = taps * outs
    here = lax.broadcasted_iota(jnp.int32, (n, n), 0) == lax.broadcasted_iota(jnp.int32, (n, n), 1)
    same = jnp.where(here, 1.0, 0.0).astype(BF16)
    end = taps - 1
    for i in range(taps):
        by_row = jnp.concatenate([raw_ref[end - j, end - i] for j in range(taps)], axis=0)
        by_column = jnp.concatenate([raw_ref[i, end - j] for j in range(taps)], axis=0)
        for block, dst in ((by_row, by_row_ref), (by_column, by_column_ref)):
            dst[i * ins : (i + 1) * ins, :] = lax.dot_general(
                block, same, (((0,), (0,)), ((), ())), preferred_element_type=F32
            ).astype(BF16)


def join_taps(taps, channels):
    width = taps.shape[1]
    return (
        pltpu.roll(taps[0:channels], 1, 1)
        + taps[channels : 2 * channels]
        + pltpu.roll(taps[2 * channels : 3 * channels], width - 1, 1)
    )


def conv_row(w_ref, src_ref, index, channels):
    window = src_ref[rows(index, 3, channels), :]
    return join_taps(jnp.dot(w_ref[...], window, preferred_element_type=F32), channels)


def shifted(row):
    return jnp.concatenate([pltpu.roll(row, 1, 1), row, pltpu.roll(row, row.shape[1] - 1, 1)], axis=0)


def halo_share(w_ref, first, second, above, channels):
    near, far = (second, first) if above else (first, second)
    start = channels if above else 0
    near = jnp.dot(w_ref[start : start + 2 * channels, :], shifted(near), preferred_element_type=F32)
    start = 2 * channels if above else 0
    far = jnp.dot(w_ref[start : start + channels, :], shifted(far), preferred_element_type=F32)
    if above:
        return near[:channels] + far, near[channels:]
    return near[:channels], near[channels:] + far


def silu_and_slope(act, keep=None):
    gate = 0.5 * jnp.tanh(0.5 * act) + 0.5
    if keep is not None:
        gate = gate * keep
    hidden = act * gate
    return hidden.astype(BF16), gate * (1.0 + act - hidden)


def ext_edges(channels, height, mid_ref, a_ref, b_ref, top, bottom, odd):
    edge = HALO * channels
    top[edge : 2 * edge, :] = mid_ref[0:edge, :]
    bottom[0:edge, :] = mid_ref[(height - HALO) * channels : height * channels, :]

    @pl.when(odd == 1)
    def _():
        top[0:edge, :] = a_ref[...]
        bottom[edge : 2 * edge, :] = b_ref[...]

    @pl.when(odd == 0)
    def _():
        top[0:edge, :] = b_ref[...]
        bottom[edge : 2 * edge, :] = a_ref[...]


def forward_inner_kernel(
    channels, height,
    xt_ref, raw1_ref, raw2_ref, after2_ref, after3_ref,
    hid_ref, slope_ref, res_ref, w1_ref, w2_ref, ha_ref,
):
    first_rows(xt_ref, ha_ref, height, channels)
    stack_forward(raw1_ref, w1_ref)
    stack_forward(raw2_ref, w2_ref)
    for i in range(height - 2):
        act = conv_row(w1_ref, xt_ref, i, channels)
        hid_ref[rows(i, 1, channels), :], slope_ref[rows(i, 1, channels), :] = silu_and_slope(act)
    for i in range(height - 4):
        res_ref[rows(i, 1, channels), :] = conv_row(w2_ref, hid_ref, i, channels)


def on_grid():
    me = lax.axis_index("lat")
    count = lax.axis_size("lat")
    return jnp.where(me == 0, 0.0, 1.0), jnp.where(me == count - 1, 0.0, 1.0)


def forward_edge_kernel(
    channels, height,
    xt_ref, a_ref, b_ref, hid_ref, w1_ref, w2_ref, raw1_ref, raw2_ref,
    slope_ref, res_ref, w1t_ref, w2t_ref, col1_ref, col2_ref,
    top, bottom, hid_top, hid_bottom,
):
    odd = lax.axis_index("lat") % 2
    ext_edges(channels, height, xt_ref, a_ref, b_ref, top, bottom, odd)
    has_above, has_below = on_grid()
    inner = (height - 2 - HALO) * channels
    hid_top[2 * channels : 4 * channels, :] = hid_ref[0 : 2 * channels, :]
    hid_bottom[0 : 2 * channels, :] = hid_ref[inner : inner + 2 * channels, :]
    for i, keep in ((0, has_above), (1, None)):
        act = conv_row(w1_ref, top, i, channels)
        hid_top[rows(i, 1, channels), :], slope_ref[rows(i, 1, channels), :] = silu_and_slope(act, keep)
    for i, keep in ((0, None), (1, has_below)):
        act = conv_row(w1_ref, bottom, i, channels)
        hid_bottom[rows(2 + i, 1, channels), :], slope_ref[rows(2 + i, 1, channels), :] = (
            silu_and_slope(act, keep)
        )
    for i in range(2):
        res_ref[rows(i, 1, channels), :] = conv_row(w2_ref, hid_top, i, channels)
        res_ref[rows(2 + i, 1, channels), :] = conv_row(w2_ref, hid_bottom, i, channels)
    stack_backward(raw1_ref, w1t_ref, col1_ref)
    stack_backward(raw2_ref, w2t_ref, col2_ref)


def direct_job(span, m, ref):
    p, _, _ = place_in_plane(span)
    return span + lax.bitwise_xor(p, m) - p, ref


def relayed_job(span, m, ref):
    p, _, _ = place_in_plane(span)
    step = lax.bitwise_xor(p, m) - p
    return jnp.where(step > 0, step, 2 * span + step), ref


def early_jobs(span, own_ref, za_ref, zb_ref, near_ref, far_refs):
    p, z_odd, _ = place_in_plane(span)
    jobs = [
        (span, own_ref),
        (jnp.where(z_odd == 1, 0, 2 * span), za_ref.at[p]),
        (jnp.where(z_odd == 1, 2 * span, 0), zb_ref.at[p]),
        direct_job(span, 1, near_ref.at[0]),
        relayed_job(span, 1, near_ref.at[1]),
    ]
    return jobs + [direct_job(span, m, ref) for m, ref in enumerate(far_refs, 2)]


def late_jobs(span, far_refs):
    return [relayed_job(span, m, ref) for m, ref in enumerate(far_refs, 2)]


def tile_terms(jobs, route_ref, xt_ref, inner_ref, edge_ref, obs_weight, channels, height, columns):
    slots = BLK_LON
    across, down = columns // BLK_LON, height // BLK_LAT
    places, blocks = [], []
    for k, _ in jobs:
        n = route_ref[0, k]
        r, q = n // across, n % across
        inside = (r > 0) & (r < down - 1)
        lanes = pl.ds(pl.multiple_of(q * BLK_LON, BLK_LON), BLK_LON)
        block = []
        for i in range(BLK_LAT):
            row_in = jnp.clip(r * BLK_LAT + i - HALO, 0, height - 2 * HALO - 1)
            row_edge = jnp.where(r == 0, i, HALO + i)
            res = jnp.where(
                inside,
                inner_ref[rows(row_in, 1, channels), lanes],
                edge_ref[rows(row_edge, 1, channels), lanes],
            )
            here = (rows(r * BLK_LAT + i, 1, channels), lanes)
            block.append((xt_ref[here].astype(F32) + res).astype(BF16))
        places.append((r, lanes))
        blocks.append(block)
    misfits = []
    for (_, ref), block in zip(jobs, blocks):
        predicted = jnp.zeros((channels, slots), F32)
        for i in range(BLK_LAT):
            predicted += lax.dot_general(
                block[i],
                ref[i * slots : (i + 1) * slots, :],
                (((1,), (1,)), ((), ())),
                preferred_element_type=F32,
            )
        obs = ref[BLK_LAT * slots : BLK_LAT * slots + channels, :].astype(F32)
        misfits.append(((obs - predicted) * obs_weight).astype(BF16))
    terms = [
        [
            jnp.dot(misfit, ref[i * slots : (i + 1) * slots, :], preferred_element_type=F32).astype(BF16)
            for i in range(BLK_LAT)
        ]
        for (_, ref), misfit in zip(jobs, misfits)
    ]
    return places, terms


def early_tile_kernel(
    channels, height, columns, span,
    route_hbm, xt_ref, inner_ref, edge_ref, ow_ref, own_ref, za_ref, zb_ref, near_ref, *refs,
):
    far_refs, (guide_ref, route_ref, sem) = refs[: span - 2], refs[span - 2 :]
    copy = pltpu.make_async_copy(route_hbm, route_ref, sem)
    copy.start()
    guide_ref[...] = jnp.zeros_like(guide_ref)
    copy.wait()
    jobs = early_jobs(span, own_ref, za_ref, zb_ref, near_ref, far_refs)
    places, terms = tile_terms(
        jobs, route_ref, xt_ref, inner_ref, edge_ref, as_column(ow_ref[...]), channels, height, columns
    )
    for (r, lanes), term in zip(places, terms):
        for i in range(BLK_LAT):
            guide_ref[rows(r * BLK_LAT + i, 1, channels), lanes] += term[i].astype(F32)


def late_tile_kernel(
    channels, height, columns, span,
    route_ref, xt_ref, inner_ref, edge_ref, ow_ref, guide_ref, *refs,
):
    far_refs, (late_ref, ga_ref, gb_ref, sums, low) = refs[: span - 2], refs[span - 2 :]
    edge = HALO * channels
    last = (height - HALO) * channels
    sums[0:edge, :] = guide_ref[0:edge, :]
    sums[edge : 2 * edge, :] = guide_ref[last : last + edge, :]
    jobs = late_jobs(span, far_refs)
    places, terms = tile_terms(
        jobs, route_ref, xt_ref, inner_ref, edge_ref, as_column(ow_ref[...]), channels, height, columns
    )
    down = height // BLK_LAT
    for index, ((r, lanes), term) in enumerate(zip(places, terms)):
        part = jnp.where(r == 0, 0, jnp.where(r == down - 1, 1, 2))
        for i in range(BLK_LAT):
            late_ref[index, i] = term[i]
            sums[rows(part * HALO + i, 1, channels), lanes] += term[i].astype(F32)
    low[...] = sums[0 : 2 * edge, :].astype(BF16)
    second_rows(low, gb_ref, 2 * HALO, channels)
    first_rows(low, ga_ref, 2 * HALO, channels)


def backward_inner_kernel(
    channels, height, columns, span,
    route_ref, early_ref, late_ref, slope_ref, inner_ref, edge_ref, prior_ref, w2_ref, w1_ref,
    part_adj_ref, part_score_ref, score_ref,
    guide, low, adj,
):
    guide[...] = early_ref[...]
    across = columns // BLK_LON
    jobs = late_jobs(span, [late_ref] * (span - 2))
    for index, (k, _) in enumerate(jobs):
        n = route_ref[0, k]
        lanes = pl.ds(pl.multiple_of((n % across) * BLK_LON, BLK_LON), BLK_LON)
        for i in range(BLK_LAT):
            here = (rows((n // across) * BLK_LAT + i, 1, channels), lanes)
            guide[here] += late_ref[index, i].astype(F32)
    edge = HALO * channels
    none = jnp.zeros((edge, columns), BF16)
    low[0:edge, :] = none
    low[edge : edge + height * channels, :] = guide[...].astype(BF16)
    low[edge + height * channels :, :] = none
    adj[0:edge, :] = none
    adj[height * channels :, :] = none
    for i in range(height + 2):
        part = conv_row(w2_ref, low, i, channels)
        if HALO <= i < height:
            adj[rows(i, 1, channels), :] = (slope_ref[rows(i - HALO, 1, channels), :] * part).astype(BF16)
        else:
            part_adj_ref[rows(i if i < HALO else i - height + HALO, 1, channels), :] = part
    prior = as_column(prior_ref[...])
    for i in range(height):
        part = conv_row(w1_ref, adj, i, channels) + guide[rows(i, 1, channels), :]
        if HALO <= i < height - HALO:
            here = rows(i - HALO, 1, channels)
            score_ref[here, :] = (prior * inner_ref[here, :] + part).astype(BF16)
        else:
            here = rows(i if i < HALO else i - height + 2 * HALO, 1, channels)
            part_score_ref[here, :] = prior * edge_ref[here, :] + part


def backward_edge_kernel(
    channels, height,
    a_ref, b_ref, slope_ref, part_adj_ref, part_score_ref, score_ref,
    w2_ref, w1_ref,
    out_hbm,
    out_ref, edge_ref, sems,
):
    odd = lax.axis_index("lat") % 2
    a, b = a_ref[...], b_ref[...]
    for at, window, above in ((0, jnp.where(odd == 1, a, b), True), (HALO, jnp.where(odd == 1, b, a), False)):
        here = [rows(at + i, 1, channels) for i in range(HALO)]
        share = halo_share(w2_ref, window[:channels], window[channels:], above, channels)
        adj = [
            (slope_ref[place, :] * (part_adj_ref[place, :] + back)).astype(BF16)
            for place, back in zip(here, share)
        ]
        for place, back in zip(here, halo_share(w1_ref, adj[0], adj[1], above, channels)):
            edge_ref[place, :] = (part_score_ref[place, :] + back).astype(BF16)
    copies = []
    for start, size in channel_groups(channels):
        n = size * height
        picked = []
        for r in range(height):
            if r < HALO:
                src, at = edge_ref, r
            elif r < height - HALO:
                src, at = score_ref, r - HALO
            else:
                src, at = edge_ref, r - height + 2 * HALO
            picked.append(src[at * channels + start : at * channels + start + size, :])
        part = pl.ds(start * height, n)
        out_ref[part, :] = jnp.dot(
            permutation(height, size, True), jnp.concatenate(picked, axis=0), preferred_element_type=F32
        ).astype(BF16)
        copies.append(pltpu.make_async_copy(out_ref.at[part], out_hbm.at[part], sems.at[len(copies)]))
        copies[-1].start()
    for copy in copies:
        copy.wait()


def pairs(groups, count, partner):
    found = []
    for g in range(groups):
        for i in range(count):
            other = partner(i)
            if 0 <= other < count:
                found.append((g * count + i, g * count + other))
            elif groups % 2 == 0:
                found.append((g * count + i, (g ^ 1) * count + i))
    return found


def local(
    noisy_state, w_first, w_second, prior_weight, obs_weight, block_route, counts, tile_weights, observations
):
    channels, height, columns = noisy_state.shape
    tile_total = block_route.shape[1]
    span = tile_total // 2
    slots = tile_weights.shape[2]
    count = lax.axis_size("lat")
    pack_rows = BLK_LAT * slots + channels
    taps = w_first.shape[0]

    def field(n, dtype=BF16):
        return shape((n * channels, columns), dtype)

    def buffer(n, dtype=BF16):
        return pltpu.VMEM((n * channels, columns), dtype)

    def exchange(x, partner):
        return lax.ppermute(x, ("grp", "lat"), pairs(lax.axis_size("grp"), count, partner))

    def swap(x, step, parity):
        return exchange(x, lambda i: i + step if (i // step) % 2 == parity else i - step)

    packed = shape((span, pack_rows, BLK_LON))
    def in_hbm(x):
        return pltpu.with_memory_space_constraint(x, pltpu.HBM)

    tile = shape((pack_rows, BLK_LON))
    za_send, zb_send, own, near, *far, x = pl.pallas_call(
        functools.partial(pack_kernel, channels, span),
        out_shape=(packed, packed) + (tile,) * span + (field(height),),
        in_specs=[HB] * 4,
        out_specs=[VM] * (3 + span),
        scratch_shapes=[
            pltpu.SMEM(counts.shape, jnp.int32),
            pltpu.VMEM(tile_weights.shape[1:], BF16),
            pltpu.VMEM(observations.shape[1:], BF16),
            pltpu.SemaphoreType.DMA((4,)),
        ],
        compiler_params=params(),
    )(
        in_hbm(counts),
        in_hbm(tile_weights),
        in_hbm(observations),
        in_hbm(noisy_state.reshape(channels * height, columns)),
    )
    za, zb = swap(za_send, span, 0), swap(zb_send, span, 1)
    far = [exchange(buf, lambda i, m=m: i ^ m) for m, buf in enumerate(far, 2)]
    xt, hb = pl.pallas_call(
        functools.partial(prepare_kernel, channels, height),
        out_shape=(field(height), field(HALO)),
        in_specs=[VM, AN],
        out_specs=[VM] * 2,
        compiler_params=params(),
    )(x, za_send)
    hb = swap(hb, 1, 1)

    weight = shape((taps * channels, taps * channels))
    hid, slope_in, res_in, w1, w2, ha = pl.pallas_call(
        functools.partial(forward_inner_kernel, channels, height),
        out_shape=(
            field(height - 2),
            field(height - 2, F32),
            field(height - 4, F32),
            weight,
            weight,
            field(HALO),
        ),
        in_specs=[VM] * 3 + [AN] * len(far),
        out_specs=[VM] * 6,
        compiler_params=params(),
    )(xt, w_first, w_second, *far)
    ha = swap(ha, 1, 0)

    relayed = pl.pallas_call(
        functools.partial(relay_kernel, span),
        out_shape=(shape((2, pack_rows, BLK_LON)),) + (tile,) * (span - 2),
        in_specs=[VM] * 3 + [AN],
        out_specs=[VM] * (span - 1),
        compiler_params=params(),
    )(za, zb, near, w1)
    near, *last = [exchange(buf, lambda i, m=m: i ^ m) for m, buf in enumerate(relayed, 1)]

    slope_ed, res_ed, w1t, w2t, col1, col2 = pl.pallas_call(
        functools.partial(forward_edge_kernel, channels, height),
        out_shape=(field(2 * HALO, F32), field(2 * HALO, F32)) + (weight,) * 4,
        in_specs=[VM] * 8,
        out_specs=[VM] * 6,
        scratch_shapes=[buffer(2 * HALO)] * 4,
        compiler_params=params(),
    )(xt, ha, hb, hid, w1, w2, w_first, w_second)

    observed = obs_weight[None, :]
    early = pl.pallas_call(
        functools.partial(early_tile_kernel, channels, height, columns, span),
        out_shape=field(height, F32),
        in_specs=[HB] + [VM] * (8 + span - 2),
        out_specs=VM,
        scratch_shapes=[pltpu.SMEM(block_route.shape, jnp.int32), pltpu.SemaphoreType.DMA],
        compiler_params=params(),
    )(in_hbm(block_route), xt, res_in, res_ed, observed, own, za, zb, near, *far)

    late, ga, gb = pl.pallas_call(
        functools.partial(late_tile_kernel, channels, height, columns, span),
        out_shape=(
            shape((span - 2, BLK_LAT, channels, BLK_LON)),
            field(HALO),
            field(HALO),
        ),
        in_specs=[SM] + [VM] * (5 + span - 2),
        out_specs=[VM] * 3,
        scratch_shapes=[buffer(3 * HALO, F32), buffer(2 * HALO)],
        compiler_params=params(),
    )(block_route, xt, res_in, res_ed, observed, early, *last)
    ga, gb = swap(ga, 1, 0), swap(gb, 1, 1)

    part_adj, part_score, score = pl.pallas_call(
        functools.partial(backward_inner_kernel, channels, height, columns, span),
        out_shape=(field(2 * HALO, F32), field(2 * HALO, F32), field(height - 2 * HALO)),
        in_specs=[SM] + [VM] * 8,
        out_specs=[VM] * 3,
        scratch_shapes=[buffer(height, F32), buffer(height + 2 * HALO), buffer(height + 2)],
        compiler_params=params(),
    )(block_route, early, late, slope_in, res_in, res_ed, prior_weight[None, :], w2t, w1t)

    out = pl.pallas_call(
        functools.partial(backward_edge_kernel, channels, height),
        out_shape=shape((channels * height, columns)),
        in_specs=[VM] * 8,
        out_specs=HB,
        scratch_shapes=[
            buffer(height),
            buffer(2 * HALO),
            pltpu.SemaphoreType.DMA((len(channel_groups(channels)),)),
        ],
        compiler_params=params(),
    )(ga, gb, slope_ed, part_adj, part_score, score, col2, col1)
    return out.reshape(channels, height, columns)


def solution(mesh):
    in_specs = (
        P("grp", "lat", None),
        P(),
        P(),
        P(),
        P(),
        P(("grp", "lat"), None),
        P(("grp", "lat"), None),
        P(("grp", "lat"), None, None, None),
        P(("grp", "lat"), None, None, None),
    )
    out_specs = P("grp", "lat", None)
    return jax.shard_map(local, mesh=mesh, in_specs=in_specs, out_specs=out_specs, check_vma=False)
```

```python
import functools

import jax
import jax.numpy as jnp
from jax import lax
from jax.experimental import pallas as pl
from jax.experimental.pallas import tpu as pltpu
from jax.sharding import PartitionSpec as P

BLK_LAT = 2
BLK_LON = 128
HALO = 2
F32 = jnp.float32
BF16 = jnp.bfloat16

VM = pl.BlockSpec(memory_space=pltpu.VMEM)
SM = pl.BlockSpec(memory_space=pltpu.SMEM)
HB = pl.BlockSpec(memory_space=pltpu.HBM)
AN = pl.BlockSpec(memory_space=pl.ANY)


def params(mib=16):
    return pltpu.CompilerParams(vmem_limit_bytes=mib << 20)


def shape(dims, dtype=BF16):
    return jax.ShapeDtypeStruct(dims, dtype)


def rows(index, count, channels):
    start = index * channels
    if not isinstance(start, int):
        start = pl.multiple_of(start, 16)
    return pl.ds(start, count * channels)


def permutation(height, group, back):
    n = height * group
    out = lax.broadcasted_iota(jnp.int32, (n, n), 0)
    src = lax.broadcasted_iota(jnp.int32, (n, n), 1)
    if back:
        want = (out % height) * group + out // height
    else:
        want = (out % group) * height + out // group
    return jnp.where(src == want, 1.0, 0.0).astype(BF16)


def channel_groups(channels):
    return [(start, min(32, channels - start)) for start in range(0, channels, 32)]


def as_column(row):
    n = row.shape[1]
    here = lax.broadcasted_iota(jnp.int32, (n, n), 0) == lax.broadcasted_iota(jnp.int32, (n, n), 1)
    return jnp.sum(jnp.where(here, jnp.broadcast_to(row, (n, n)), 0.0), axis=1, keepdims=True)


def place_in_plane(span):
    me = lax.axis_index("lat")
    return me % span, (me // span) % 2, me % 2


def pack_tile(k, dst, w_ref, obs_ref, count_ref, channels):
    slots = w_ref.shape[1]
    live = lax.broadcasted_iota(jnp.int32, (slots, BLK_LON), 0) < count_ref[0, k]
    zero = jnp.zeros((slots, BLK_LON), BF16)
    for i in range(BLK_LAT):
        half = w_ref[k, :, i * BLK_LON : (i + 1) * BLK_LON]
        dst[i * slots : (i + 1) * slots, :] = jnp.where(live, half, zero)
    dst[BLK_LAT * slots : BLK_LAT * slots + channels, :] = obs_ref[k]


def first_rows(src_ref, dst, height, channels):
    odd = lax.axis_index("lat") % 2
    dst[...] = src_ref[rows((height - HALO) * (1 - odd), HALO, channels), :]


def second_rows(src_ref, dst, height, channels):
    me, odd = lax.axis_index("lat"), lax.axis_index("lat") % 2
    alone = (me == 0) | (me == lax.axis_size("lat") - 1)

    @pl.when(alone)
    def _():
        dst[...] = jnp.zeros_like(dst)

    @pl.when(jnp.logical_not(alone))
    def _():
        dst[...] = src_ref[rows((height - HALO) * odd, HALO, channels), :]


def pack_near_kernel(
    channels, span,
    count_hbm, w_hbm, obs_hbm, x_hbm,
    own_ref, near_ref, y2_ref, y3_ref, x_ref, w_ref, obs_ref,
    count_ref, sems,
):
    copies = [
        pltpu.make_async_copy(count_hbm, count_ref, sems.at[0]),
        pltpu.make_async_copy(w_hbm.at[0], w_ref, sems.at[1]),
        pltpu.make_async_copy(obs_hbm.at[0], obs_ref, sems.at[2]),
        pltpu.make_async_copy(x_hbm, x_ref, sems.at[3]),
    ]
    for copy in copies:
        copy.start()
    for copy in copies[:3]:
        copy.wait()
    p, _, _ = place_in_plane(span)
    pack_tile(span, own_ref, w_ref, obs_ref, count_ref, channels)
    for j, dst in enumerate((near_ref, y2_ref, y3_ref), 1):
        pack_tile(span + p - lax.bitwise_xor(p, j), dst, w_ref, obs_ref, count_ref, channels)
    copies[3].wait()


def prepare_kernel(
    channels, height, span,
    count_hbm, w_ref, obs_ref, x_ref,
    za_ref, zb_ref, xt_ref, hb_ref,
    count_ref, sem,
):
    copy = pltpu.make_async_copy(count_hbm, count_ref, sem)
    copy.start()
    for start, size in channel_groups(channels):
        n = size * height
        moved = jnp.dot(
            permutation(height, size, False),
            x_ref[start * height : start * height + n, :],
            preferred_element_type=F32,
        ).astype(BF16)
        for r in range(height):
            xt_ref[r * channels + start : r * channels + start + size, :] = (
                moved[r * size : (r + 1) * size, :]
            )
    second_rows(xt_ref, hb_ref, height, channels)
    copy.wait()
    p, z_odd, _ = place_in_plane(span)
    for j in range(span):
        up = jnp.maximum(p - j, 0)
        down = jnp.minimum(2 * span + p - j, 2 * span)
        for k, dst in ((jnp.where(z_odd == 1, down, up), za_ref), (jnp.where(z_odd == 1, up, down), zb_ref)):
            pack_tile(k, dst.at[j], w_ref, obs_ref, count_ref, channels)


def relay_kernel(channels, height, span, za_ref, zb_ref, near_ref, xt_ref, *refs):
    ha_ref, near_out, *far_outs = refs[-span:]
    first_rows(xt_ref, ha_ref, height, channels)
    p, z_odd, _ = place_in_plane(span)
    near_out[0] = near_ref[...]
    for m, out in enumerate([near_out.at[1]] + far_outs, 1):
        to = lax.bitwise_xor(p, m)
        below = jnp.where(to < p, 1, 0)

        @pl.when(below == z_odd)
        def _():
            out[...] = za_ref[to]

        @pl.when(below != z_odd)
        def _():
            out[...] = zb_ref[to]


def stack_forward(raw_ref, dst):
    taps, _, outs, ins = raw_ref.shape
    total = jnp.zeros(dst.shape, F32)
    for a in range(taps):
        block = raw_ref[a].reshape(taps * outs, ins)
        to = lax.broadcasted_iota(jnp.int32, (ins, taps * ins), 1)
        pick = jnp.where(to == lax.broadcasted_iota(jnp.int32, to.shape, 0) + a * ins, 1.0, 0.0)
        total += jnp.dot(block, pick.astype(BF16), preferred_element_type=F32)
    dst[...] = total.astype(BF16)


def stack_backward(raw_ref, by_row_ref, by_column_ref):
    taps, _, outs, ins = raw_ref.shape
    n = taps * outs
    here = lax.broadcasted_iota(jnp.int32, (n, n), 0) == lax.broadcasted_iota(jnp.int32, (n, n), 1)
    same = jnp.where(here, 1.0, 0.0).astype(BF16)
    end = taps - 1
    for i in range(taps):
        by_row = jnp.concatenate([raw_ref[end - j, end - i] for j in range(taps)], axis=0)
        by_column = jnp.concatenate([raw_ref[i, end - j] for j in range(taps)], axis=0)
        for block, dst in ((by_row, by_row_ref), (by_column, by_column_ref)):
            dst[i * ins : (i + 1) * ins, :] = lax.dot_general(
                block, same, (((0,), (0,)), ((), ())), preferred_element_type=F32
            ).astype(BF16)


def join_taps(taps, channels):
    width = taps.shape[1]
    return (
        pltpu.roll(taps[0:channels], 1, 1)
        + taps[channels : 2 * channels]
        + pltpu.roll(taps[2 * channels : 3 * channels], width - 1, 1)
    )


def conv_row(w_ref, src_ref, index, channels):
    window = src_ref[rows(index, 3, channels), :]
    return join_taps(jnp.dot(w_ref[...], window, preferred_element_type=F32), channels)


def shifted(row):
    return jnp.concatenate([pltpu.roll(row, 1, 1), row, pltpu.roll(row, row.shape[1] - 1, 1)], axis=0)


def halo_share(w_ref, first, second, above, channels):
    near, far = (second, first) if above else (first, second)
    start = channels if above else 0
    near = jnp.dot(w_ref[start : start + 2 * channels, :], shifted(near), preferred_element_type=F32)
    start = 2 * channels if above else 0
    far = jnp.dot(w_ref[start : start + channels, :], shifted(far), preferred_element_type=F32)
    if above:
        return near[:channels] + far, near[channels:]
    return near[:channels], near[channels:] + far


def silu_and_slope(act, keep=None):
    gate = 0.5 * jnp.tanh(0.5 * act) + 0.5
    if keep is not None:
        gate = gate * keep
    hidden = act * gate
    return hidden.astype(BF16), gate * (1.0 + act - hidden)


def ext_edges(channels, height, mid_ref, a_ref, b_ref, top, bottom, odd):
    edge = HALO * channels
    top[edge : 2 * edge, :] = mid_ref[0:edge, :]
    bottom[0:edge, :] = mid_ref[(height - HALO) * channels : height * channels, :]

    @pl.when(odd == 1)
    def _():
        top[0:edge, :] = a_ref[...]
        bottom[edge : 2 * edge, :] = b_ref[...]

    @pl.when(odd == 0)
    def _():
        top[0:edge, :] = b_ref[...]
        bottom[edge : 2 * edge, :] = a_ref[...]


def hidden_inner_kernel(channels, height, xt_ref, raw1_ref, hid_ref, slope_ref, w1_ref):
    stack_forward(raw1_ref, w1_ref)
    for i in range(height - 2):
        act = conv_row(w1_ref, xt_ref, i, channels)
        hid_ref[rows(i, 1, channels), :], slope_ref[rows(i, 1, channels), :] = silu_and_slope(act)


def residual_inner_kernel(channels, height, hid_ref, raw2_ref, *refs):
    res_ref, w2_ref = refs[-2:]
    stack_forward(raw2_ref, w2_ref)
    for i in range(height - 4):
        res_ref[rows(i, 1, channels), :] = conv_row(w2_ref, hid_ref, i, channels)


def on_grid():
    me = lax.axis_index("lat")
    count = lax.axis_size("lat")
    return jnp.where(me == 0, 0.0, 1.0), jnp.where(me == count - 1, 0.0, 1.0)


def forward_edge_kernel(
    channels, height,
    xt_ref, a_ref, b_ref, hid_ref, w1_ref, w2_ref, raw1_ref, raw2_ref,
    slope_ref, res_ref, w1t_ref, w2t_ref, col1_ref, col2_ref,
    top, bottom, hid_top, hid_bottom,
):
    odd = lax.axis_index("lat") % 2
    ext_edges(channels, height, xt_ref, a_ref, b_ref, top, bottom, odd)
    has_above, has_below = on_grid()
    inner = (height - 2 - HALO) * channels
    hid_top[2 * channels : 4 * channels, :] = hid_ref[0 : 2 * channels, :]
    hid_bottom[0 : 2 * channels, :] = hid_ref[inner : inner + 2 * channels, :]
    for i, keep in ((0, has_above), (1, None)):
        act = conv_row(w1_ref, top, i, channels)
        hid_top[rows(i, 1, channels), :], slope_ref[rows(i, 1, channels), :] = silu_and_slope(act, keep)
    for i, keep in ((0, None), (1, has_below)):
        act = conv_row(w1_ref, bottom, i, channels)
        hid_bottom[rows(2 + i, 1, channels), :], slope_ref[rows(2 + i, 1, channels), :] = (
            silu_and_slope(act, keep)
        )
    for i in range(2):
        res_ref[rows(i, 1, channels), :] = conv_row(w2_ref, hid_top, i, channels)
        res_ref[rows(2 + i, 1, channels), :] = conv_row(w2_ref, hid_bottom, i, channels)
    stack_backward(raw1_ref, w1t_ref, col1_ref)
    stack_backward(raw2_ref, w2t_ref, col2_ref)


def direct_job(span, m, ref):
    p, _, _ = place_in_plane(span)
    return span + lax.bitwise_xor(p, m) - p, ref


def relayed_job(span, m, ref):
    p, _, _ = place_in_plane(span)
    step = lax.bitwise_xor(p, m) - p
    return jnp.where(step > 0, step, 2 * span + step), ref


def early_jobs(span, own_ref, za_ref, zb_ref, near_ref, far_refs):
    p, z_odd, _ = place_in_plane(span)
    jobs = [
        (span, own_ref),
        (jnp.where(z_odd == 1, 0, 2 * span), za_ref.at[p]),
        (jnp.where(z_odd == 1, 2 * span, 0), zb_ref.at[p]),
        direct_job(span, 1, near_ref.at[0]),
        relayed_job(span, 1, near_ref.at[1]),
    ]
    return jobs + [direct_job(span, m, ref) for m, ref in enumerate(far_refs, 2)]


def late_jobs(span, far_refs):
    return [relayed_job(span, m, ref) for m, ref in enumerate(far_refs, 2)]


def tile_terms(jobs, route_ref, xt_ref, inner_ref, edge_ref, obs_weight, channels, height, columns):
    slots = BLK_LON
    across, down = columns // BLK_LON, height // BLK_LAT
    places, blocks = [], []
    for k, _ in jobs:
        n = route_ref[0, k]
        r, q = n // across, n % across
        inside = (r > 0) & (r < down - 1)
        lanes = pl.ds(pl.multiple_of(q * BLK_LON, BLK_LON), BLK_LON)
        block = []
        for i in range(BLK_LAT):
            row_in = jnp.clip(r * BLK_LAT + i - HALO, 0, height - 2 * HALO - 1)
            row_edge = jnp.where(r == 0, i, HALO + i)
            res = jnp.where(
                inside,
                inner_ref[rows(row_in, 1, channels), lanes],
                edge_ref[rows(row_edge, 1, channels), lanes],
            )
            here = (rows(r * BLK_LAT + i, 1, channels), lanes)
            block.append((xt_ref[here].astype(F32) + res).astype(BF16))
        places.append((r, lanes))
        blocks.append(block)
    misfits = []
    for (_, ref), block in zip(jobs, blocks):
        predicted = jnp.zeros((channels, slots), F32)
        for i in range(BLK_LAT):
            predicted += lax.dot_general(
                block[i],
                ref[i * slots : (i + 1) * slots, :],
                (((1,), (1,)), ((), ())),
                preferred_element_type=F32,
            )
        obs = ref[BLK_LAT * slots : BLK_LAT * slots + channels, :].astype(F32)
        misfits.append(((obs - predicted) * obs_weight).astype(BF16))
    terms = [
        [
            jnp.dot(misfit, ref[i * slots : (i + 1) * slots, :], preferred_element_type=F32).astype(BF16)
            for i in range(BLK_LAT)
        ]
        for (_, ref), misfit in zip(jobs, misfits)
    ]
    return places, terms


def early_tile_kernel(
    channels, height, columns, span,
    route_hbm, xt_ref, inner_ref, edge_ref, ow_ref, own_ref, za_ref, zb_ref, near_ref, *refs,
):
    far_refs, (guide_ref, route_ref, sem) = refs[: span - 2], refs[span - 2 :]
    copy = pltpu.make_async_copy(route_hbm, route_ref, sem)
    copy.start()
    guide_ref[...] = jnp.zeros_like(guide_ref)
    copy.wait()
    jobs = early_jobs(span, own_ref, za_ref, zb_ref, near_ref, far_refs)
    places, terms = tile_terms(
        jobs, route_ref, xt_ref, inner_ref, edge_ref, as_column(ow_ref[...]), channels, height, columns
    )
    for (r, lanes), term in zip(places, terms):
        for i in range(BLK_LAT):
            guide_ref[rows(r * BLK_LAT + i, 1, channels), lanes] += term[i].astype(F32)


def late_tile_kernel(
    channels, height, columns, span,
    route_ref, xt_ref, inner_ref, edge_ref, ow_ref, guide_ref, *refs,
):
    far_refs, (late_ref, ga_ref, gb_ref, sums, low) = refs[: span - 2], refs[span - 2 :]
    edge = HALO * channels
    last = (height - HALO) * channels
    sums[0:edge, :] = guide_ref[0:edge, :]
    sums[edge : 2 * edge, :] = guide_ref[last : last + edge, :]
    jobs = late_jobs(span, far_refs)
    places, terms = tile_terms(
        jobs, route_ref, xt_ref, inner_ref, edge_ref, as_column(ow_ref[...]), channels, height, columns
    )
    down = height // BLK_LAT
    for index, ((r, lanes), term) in enumerate(zip(places, terms)):
        part = jnp.where(r == 0, 0, jnp.where(r == down - 1, 1, 2))
        for i in range(BLK_LAT):
            late_ref[index, i] = term[i]
            sums[rows(part * HALO + i, 1, channels), lanes] += term[i].astype(F32)
    low[...] = sums[0 : 2 * edge, :].astype(BF16)
    second_rows(low, gb_ref, 2 * HALO, channels)
    first_rows(low, ga_ref, 2 * HALO, channels)


def backward_inner_kernel(
    channels, height, columns, span,
    route_ref, early_ref, late_ref, slope_ref, inner_ref, edge_ref, prior_ref, w2_ref, w1_ref,
    part_adj_ref, part_score_ref, score_ref,
    guide, low, adj,
):
    guide[...] = early_ref[...]
    across = columns // BLK_LON
    jobs = late_jobs(span, [late_ref] * (span - 2))
    for index, (k, _) in enumerate(jobs):
        n = route_ref[0, k]
        lanes = pl.ds(pl.multiple_of((n % across) * BLK_LON, BLK_LON), BLK_LON)
        for i in range(BLK_LAT):
            here = (rows((n // across) * BLK_LAT + i, 1, channels), lanes)
            guide[here] += late_ref[index, i].astype(F32)
    edge = HALO * channels
    none = jnp.zeros((edge, columns), BF16)
    low[0:edge, :] = none
    low[edge : edge + height * channels, :] = guide[...].astype(BF16)
    low[edge + height * channels :, :] = none
    adj[0:edge, :] = none
    adj[height * channels :, :] = none
    for i in range(height + 2):
        part = conv_row(w2_ref, low, i, channels)
        if HALO <= i < height:
            adj[rows(i, 1, channels), :] = (slope_ref[rows(i - HALO, 1, channels), :] * part).astype(BF16)
        else:
            part_adj_ref[rows(i if i < HALO else i - height + HALO, 1, channels), :] = part
    prior = as_column(prior_ref[...])
    for i in range(height):
        part = conv_row(w1_ref, adj, i, channels) + guide[rows(i, 1, channels), :]
        if HALO <= i < height - HALO:
            here = rows(i - HALO, 1, channels)
            score_ref[here, :] = (prior * inner_ref[here, :] + part).astype(BF16)
        else:
            here = rows(i if i < HALO else i - height + 2 * HALO, 1, channels)
            part_score_ref[here, :] = prior * edge_ref[here, :] + part


def backward_edge_kernel(
    channels, height,
    a_ref, b_ref, slope_ref, part_adj_ref, part_score_ref, score_ref,
    w2_ref, w1_ref,
    out_hbm,
    out_ref, edge_ref, sems,
):
    odd = lax.axis_index("lat") % 2
    a, b = a_ref[...], b_ref[...]
    for at, window, above in ((0, jnp.where(odd == 1, a, b), True), (HALO, jnp.where(odd == 1, b, a), False)):
        here = [rows(at + i, 1, channels) for i in range(HALO)]
        share = halo_share(w2_ref, window[:channels], window[channels:], above, channels)
        adj = [
            (slope_ref[place, :] * (part_adj_ref[place, :] + back)).astype(BF16)
            for place, back in zip(here, share)
        ]
        for place, back in zip(here, halo_share(w1_ref, adj[0], adj[1], above, channels)):
            edge_ref[place, :] = (part_score_ref[place, :] + back).astype(BF16)
    copies = []
    for start, size in channel_groups(channels):
        n = size * height
        picked = []
        for r in range(height):
            if r < HALO:
                src, at = edge_ref, r
            elif r < height - HALO:
                src, at = score_ref, r - HALO
            else:
                src, at = edge_ref, r - height + 2 * HALO
            picked.append(src[at * channels + start : at * channels + start + size, :])
        part = pl.ds(start * height, n)
        out_ref[part, :] = jnp.dot(
            permutation(height, size, True), jnp.concatenate(picked, axis=0), preferred_element_type=F32
        ).astype(BF16)
        copies.append(pltpu.make_async_copy(out_ref.at[part], out_hbm.at[part], sems.at[len(copies)]))
        copies[-1].start()
    for copy in copies:
        copy.wait()


def pairs(groups, count, partner):
    found = []
    for g in range(groups):
        for i in range(count):
            other = partner(i)
            if 0 <= other < count:
                found.append((g * count + i, g * count + other))
            elif groups % 2 == 0:
                found.append((g * count + i, (g ^ 1) * count + i))
    return found


def local(
    noisy_state, w_first, w_second, prior_weight, obs_weight, block_route, counts, tile_weights, observations
):
    channels, height, columns = noisy_state.shape
    tile_total = block_route.shape[1]
    span = tile_total // 2
    slots = tile_weights.shape[2]
    count = lax.axis_size("lat")
    pack_rows = BLK_LAT * slots + channels
    taps = w_first.shape[0]

    def field(n, dtype=BF16):
        return shape((n * channels, columns), dtype)

    def buffer(n, dtype=BF16):
        return pltpu.VMEM((n * channels, columns), dtype)

    def exchange(x, partner):
        return lax.ppermute(x, ("grp", "lat"), pairs(lax.axis_size("grp"), count, partner))

    def swap(x, step, parity):
        return exchange(x, lambda i: i + step if (i // step) % 2 == parity else i - step)

    packed = shape((span, pack_rows, BLK_LON))
    def in_hbm(x):
        return pltpu.with_memory_space_constraint(x, pltpu.HBM)

    tile = shape((pack_rows, BLK_LON))
    own, near, *far, x, tw, ob = pl.pallas_call(
        functools.partial(pack_near_kernel, channels, span),
        out_shape=(tile,) * span + (field(height), shape(tile_weights.shape[1:]), shape(observations.shape[1:])),
        in_specs=[HB] * 4,
        out_specs=[VM] * (span + 3),
        scratch_shapes=[pltpu.SMEM(counts.shape, jnp.int32), pltpu.SemaphoreType.DMA((4,))],
        compiler_params=params(),
    )(
        in_hbm(counts),
        in_hbm(tile_weights),
        in_hbm(observations),
        in_hbm(noisy_state.reshape(channels * height, columns)),
    )
    far = [exchange(buf, lambda i, m=m: i ^ m) for m, buf in enumerate(far, 2)]
    za, zb, xt, hb = pl.pallas_call(
        functools.partial(prepare_kernel, channels, height, span),
        out_shape=(packed, packed, field(height), field(HALO)),
        in_specs=[HB] + [VM] * 3,
        out_specs=[VM] * 4,
        scratch_shapes=[pltpu.SMEM(counts.shape, jnp.int32), pltpu.SemaphoreType.DMA],
        compiler_params=params(),
    )(in_hbm(counts), tw, ob, x)
    za, zb, hb = swap(za, span, 0), swap(zb, span, 1), swap(hb, 1, 1)

    weight = shape((taps * channels, taps * channels))
    hid, slope_in, w1 = pl.pallas_call(
        functools.partial(hidden_inner_kernel, channels, height),
        out_shape=(field(height - 2), field(height - 2, F32), weight),
        in_specs=[VM] * 2,
        out_specs=[VM] * 3,
        compiler_params=params(),
    )(xt, w_first)
    res_in, w2 = pl.pallas_call(
        functools.partial(residual_inner_kernel, channels, height),
        out_shape=(field(height - 4, F32), weight),
        in_specs=[VM] * 2 + [AN] * len(far),
        out_specs=[VM] * 2,
        compiler_params=params(),
        cost_estimate=pl.CostEstimate(flops=20_000_000_000, bytes_accessed=1 << 22, transcendentals=0),
    )(hid, w_second, *far)

    ha, *relayed = pl.pallas_call(
        functools.partial(relay_kernel, channels, height, span),
        out_shape=(field(HALO), shape((2, pack_rows, BLK_LON))) + (tile,) * (span - 2),
        in_specs=[VM] * 4 + [AN],
        out_specs=[VM] * span,
        compiler_params=params(),
    )(za, zb, near, xt, w2)
    ha = swap(ha, 1, 0)
    near, *last = [exchange(buf, lambda i, m=m: i ^ m) for m, buf in enumerate(relayed, 1)]

    slope_ed, res_ed, w1t, w2t, col1, col2 = pl.pallas_call(
        functools.partial(forward_edge_kernel, channels, height),
        out_shape=(field(2 * HALO, F32), field(2 * HALO, F32)) + (weight,) * 4,
        in_specs=[VM] * 8,
        out_specs=[VM] * 6,
        scratch_shapes=[buffer(2 * HALO)] * 4,
        compiler_params=params(),
    )(xt, ha, hb, hid, w1, w2, w_first, w_second)

    observed = obs_weight[None, :]
    early = pl.pallas_call(
        functools.partial(early_tile_kernel, channels, height, columns, span),
        out_shape=field(height, F32),
        in_specs=[HB] + [VM] * (8 + span - 2),
        out_specs=VM,
        scratch_shapes=[pltpu.SMEM(block_route.shape, jnp.int32), pltpu.SemaphoreType.DMA],
        compiler_params=params(),
    )(in_hbm(block_route), xt, res_in, res_ed, observed, own, za, zb, near, *far)

    late, ga, gb = pl.pallas_call(
        functools.partial(late_tile_kernel, channels, height, columns, span),
        out_shape=(
            shape((span - 2, BLK_LAT, channels, BLK_LON)),
            field(HALO),
            field(HALO),
        ),
        in_specs=[SM] + [VM] * (5 + span - 2),
        out_specs=[VM] * 3,
        scratch_shapes=[buffer(3 * HALO, F32), buffer(2 * HALO)],
        compiler_params=params(),
    )(block_route, xt, res_in, res_ed, observed, early, *last)
    ga, gb = swap(ga, 1, 0), swap(gb, 1, 1)

    part_adj, part_score, score = pl.pallas_call(
        functools.partial(backward_inner_kernel, channels, height, columns, span),
        out_shape=(field(2 * HALO, F32), field(2 * HALO, F32), field(height - 2 * HALO)),
        in_specs=[SM] + [VM] * 8,
        out_specs=[VM] * 3,
        scratch_shapes=[buffer(height, F32), buffer(height + 2 * HALO), buffer(height + 2)],
        compiler_params=params(),
    )(block_route, early, late, slope_in, res_in, res_ed, prior_weight[None, :], w2t, w1t)

    out = pl.pallas_call(
        functools.partial(backward_edge_kernel, channels, height),
        out_shape=shape((channels * height, columns)),
        in_specs=[VM] * 8,
        out_specs=HB,
        scratch_shapes=[
            buffer(height),
            buffer(2 * HALO),
            pltpu.SemaphoreType.DMA((len(channel_groups(channels)),)),
        ],
        compiler_params=params(),
    )(ga, gb, slope_ed, part_adj, part_score, score, col2, col1)
    return out.reshape(channels, height, columns)


def solution(mesh):
    in_specs = (
        P("grp", "lat", None),
        P(),
        P(),
        P(),
        P(),
        P(("grp", "lat"), None),
        P(("grp", "lat"), None),
        P(("grp", "lat"), None, None, None),
        P(("grp", "lat"), None, None, None),
    )
    out_specs = P("grp", "lat", None)
    return jax.shard_map(local, mesh=mesh, in_specs=in_specs, out_specs=out_specs, check_vma=False)
```

```python
import functools

import jax
import jax.numpy as jnp
from jax import lax
from jax.experimental import pallas as pl
from jax.experimental.pallas import tpu as pltpu
from jax.sharding import PartitionSpec as P

BLK_LAT = 2
BLK_LON = 128
HALO = 2
F32 = jnp.float32
BF16 = jnp.bfloat16

VM = pl.BlockSpec(memory_space=pltpu.VMEM)
SM = pl.BlockSpec(memory_space=pltpu.SMEM)
HB = pl.BlockSpec(memory_space=pltpu.HBM)
AN = pl.BlockSpec(memory_space=pl.ANY)


def params(mib=16):
    return pltpu.CompilerParams(vmem_limit_bytes=mib << 20)


def shape(dims, dtype=BF16):
    return jax.ShapeDtypeStruct(dims, dtype)


def rows(index, count, channels):
    start = index * channels
    if not isinstance(start, int):
        start = pl.multiple_of(start, 16)
    return pl.ds(start, count * channels)


def permutation(height, group, back):
    n = height * group
    out = lax.broadcasted_iota(jnp.int32, (n, n), 0)
    src = lax.broadcasted_iota(jnp.int32, (n, n), 1)
    if back:
        want = (out % height) * group + out // height
    else:
        want = (out % group) * height + out // group
    return jnp.where(src == want, 1.0, 0.0).astype(BF16)


def channel_groups(channels):
    return [(start, min(32, channels - start)) for start in range(0, channels, 32)]


def as_column(row):
    n = row.shape[1]
    here = lax.broadcasted_iota(jnp.int32, (n, n), 0) == lax.broadcasted_iota(jnp.int32, (n, n), 1)
    return jnp.sum(jnp.where(here, jnp.broadcast_to(row, (n, n)), 0.0), axis=1, keepdims=True)


def place_in_plane(span):
    me = lax.axis_index("lat")
    return me % span, (me // span) % 2, me % 2


def pack_tile(k, dst, w_ref, obs_ref, count_ref, slots, channels):
    live = lax.broadcasted_iota(jnp.int32, (slots, BLK_LON), 0) < count_ref[0, k]
    zero = jnp.zeros((slots, BLK_LON), BF16)
    for i in range(BLK_LAT):
        half = w_ref[k, :, i * BLK_LON : (i + 1) * BLK_LON]
        dst[i * slots : (i + 1) * slots, :] = jnp.where(live, half, zero)
    dst[BLK_LAT * slots : BLK_LAT * slots + channels, :] = obs_ref[k]


def first_rows(src_ref, dst, height, channels):
    odd = lax.axis_index("lat") % 2
    dst[...] = src_ref[rows((height - HALO) * (1 - odd), HALO, channels), :]


def second_rows(src_ref, dst, height, channels):
    me, odd = lax.axis_index("lat"), lax.axis_index("lat") % 2
    alone = (me == 0) | (me == lax.axis_size("lat") - 1)

    @pl.when(alone)
    def _():
        dst[...] = jnp.zeros_like(dst)

    @pl.when(jnp.logical_not(alone))
    def _():
        dst[...] = src_ref[rows((height - HALO) * odd, HALO, channels), :]


def pack_kernel(
    channels, span,
    count_hbm, w_hbm, obs_hbm, x_hbm,
    za_ref, zb_ref, own_ref, near_ref, y2_ref, y3_ref, x_ref,
    count_ref, w_ref, obs_ref, sems,
):
    copies = [
        pltpu.make_async_copy(count_hbm, count_ref, sems.at[0]),
        pltpu.make_async_copy(w_hbm.at[0], w_ref, sems.at[1]),
        pltpu.make_async_copy(obs_hbm.at[0], obs_ref, sems.at[2]),
        pltpu.make_async_copy(x_hbm, x_ref, sems.at[3]),
    ]
    for copy in copies:
        copy.start()
    for copy in copies[:3]:
        copy.wait()
    p, z_odd, _ = place_in_plane(span)
    slots = w_ref.shape[1]
    pack = functools.partial(
        pack_tile, w_ref=w_ref, obs_ref=obs_ref, count_ref=count_ref, slots=slots, channels=channels
    )
    for j in range(span):
        up = jnp.maximum(p - j, 0)
        down = jnp.minimum(2 * span + p - j, 2 * span)
        pack(jnp.where(z_odd == 1, down, up), za_ref.at[j])
        pack(jnp.where(z_odd == 1, up, down), zb_ref.at[j])
    pack(span, own_ref)
    for j, dst in enumerate((near_ref, y2_ref, y3_ref), 1):
        pack(span + p - lax.bitwise_xor(p, j), dst)
    copies[3].wait()


def prepare_kernel(channels, height, x_ref, after_ref, xt_ref, hb_ref):
    for start, size in channel_groups(channels):
        n = size * height
        moved = jnp.dot(
            permutation(height, size, False),
            x_ref[start * height : start * height + n, :],
            preferred_element_type=F32,
        ).astype(BF16)
        for r in range(height):
            xt_ref[r * channels + start : r * channels + start + size, :] = (
                moved[r * size : (r + 1) * size, :]
            )
    second_rows(xt_ref, hb_ref, height, channels)


def relay_kernel(span, za_ref, zb_ref, near_ref, *refs):
    near_out, *far_outs = refs[-span + 1 :]
    p, z_odd, _ = place_in_plane(span)
    near_out[0] = near_ref[...]
    for m, out in enumerate([near_out.at[1]] + far_outs, 1):
        to = lax.bitwise_xor(p, m)
        below = jnp.where(to < p, 1, 0)

        @pl.when(below == z_odd)
        def _():
            out[...] = za_ref[to]

        @pl.when(below != z_odd)
        def _():
            out[...] = zb_ref[to]


def stack_forward(raw_ref, dst):
    taps, _, outs, ins = raw_ref.shape
    total = jnp.zeros(dst.shape, F32)
    for a in range(taps):
        block = raw_ref[a].reshape(taps * outs, ins)
        to = lax.broadcasted_iota(jnp.int32, (ins, taps * ins), 1)
        pick = jnp.where(to == lax.broadcasted_iota(jnp.int32, to.shape, 0) + a * ins, 1.0, 0.0)
        total += jnp.dot(block, pick.astype(BF16), preferred_element_type=F32)
    dst[...] = total.astype(BF16)


def stack_backward(raw_ref, by_row_ref, by_column_ref):
    taps, _, outs, ins = raw_ref.shape
    n = taps * outs
    here = lax.broadcasted_iota(jnp.int32, (n, n), 0) == lax.broadcasted_iota(jnp.int32, (n, n), 1)
    same = jnp.where(here, 1.0, 0.0).astype(BF16)
    end = taps - 1
    for i in range(taps):
        by_row = jnp.concatenate([raw_ref[end - j, end - i] for j in range(taps)], axis=0)
        by_column = jnp.concatenate([raw_ref[i, end - j] for j in range(taps)], axis=0)
        for block, dst in ((by_row, by_row_ref), (by_column, by_column_ref)):
            dst[i * ins : (i + 1) * ins, :] = lax.dot_general(
                block, same, (((0,), (0,)), ((), ())), preferred_element_type=F32
            ).astype(BF16)


def join_taps(taps, channels):
    width = taps.shape[1]
    return (
        pltpu.roll(taps[0:channels], 1, 1)
        + taps[channels : 2 * channels]
        + pltpu.roll(taps[2 * channels : 3 * channels], width - 1, 1)
    )


def conv_row(w_ref, src_ref, index, channels):
    window = src_ref[rows(index, 3, channels), :]
    return join_taps(jnp.dot(w_ref[...], window, preferred_element_type=F32), channels)


def shifted(row):
    return jnp.concatenate([pltpu.roll(row, 1, 1), row, pltpu.roll(row, row.shape[1] - 1, 1)], axis=0)


def halo_share(w_ref, first, second, above, channels):
    near, far = (second, first) if above else (first, second)
    start = channels if above else 0
    near = jnp.dot(w_ref[start : start + 2 * channels, :], shifted(near), preferred_element_type=F32)
    start = 2 * channels if above else 0
    far = jnp.dot(w_ref[start : start + channels, :], shifted(far), preferred_element_type=F32)
    if above:
        return near[:channels] + far, near[channels:]
    return near[:channels], near[channels:] + far


def silu_and_slope(act, keep=None):
    gate = 0.5 * jnp.tanh(0.5 * act) + 0.5
    if keep is not None:
        gate = gate * keep
    hidden = act * gate
    return hidden.astype(BF16), gate * (1.0 + act - hidden)


def ext_edges(channels, height, mid_ref, a_ref, b_ref, top, bottom, odd):
    edge = HALO * channels
    top[edge : 2 * edge, :] = mid_ref[0:edge, :]
    bottom[0:edge, :] = mid_ref[(height - HALO) * channels : height * channels, :]

    @pl.when(odd == 1)
    def _():
        top[0:edge, :] = a_ref[...]
        bottom[edge : 2 * edge, :] = b_ref[...]

    @pl.when(odd == 0)
    def _():
        top[0:edge, :] = b_ref[...]
        bottom[edge : 2 * edge, :] = a_ref[...]


def forward_inner_kernel(
    channels, height,
    xt_ref, raw1_ref, raw2_ref, after2_ref, after3_ref,
    hid_ref, slope_ref, res_ref, w1_ref, w2_ref, ha_ref,
):
    first_rows(xt_ref, ha_ref, height, channels)
    stack_forward(raw1_ref, w1_ref)
    stack_forward(raw2_ref, w2_ref)
    for i in range(height - 2):
        act = conv_row(w1_ref, xt_ref, i, channels)
        hid_ref[rows(i, 1, channels), :], slope_ref[rows(i, 1, channels), :] = silu_and_slope(act)
    for i in range(height - 4):
        res_ref[rows(i, 1, channels), :] = conv_row(w2_ref, hid_ref, i, channels)


def on_grid():
    me = lax.axis_index("lat")
    count = lax.axis_size("lat")
    return jnp.where(me == 0, 0.0, 1.0), jnp.where(me == count - 1, 0.0, 1.0)


def forward_edge_kernel(
    channels, height,
    xt_ref, a_ref, b_ref, hid_ref, w1_ref, w2_ref, raw1_ref, raw2_ref,
    slope_ref, res_ref, w1t_ref, w2t_ref, col1_ref, col2_ref,
    top, bottom, hid_top, hid_bottom,
):
    odd = lax.axis_index("lat") % 2
    ext_edges(channels, height, xt_ref, a_ref, b_ref, top, bottom, odd)
    has_above, has_below = on_grid()
    inner = (height - 2 - HALO) * channels
    hid_top[2 * channels : 4 * channels, :] = hid_ref[0 : 2 * channels, :]
    hid_bottom[0 : 2 * channels, :] = hid_ref[inner : inner + 2 * channels, :]
    for i, keep in ((0, has_above), (1, None)):
        act = conv_row(w1_ref, top, i, channels)
        hid_top[rows(i, 1, channels), :], slope_ref[rows(i, 1, channels), :] = silu_and_slope(act, keep)
    for i, keep in ((0, None), (1, has_below)):
        act = conv_row(w1_ref, bottom, i, channels)
        hid_bottom[rows(2 + i, 1, channels), :], slope_ref[rows(2 + i, 1, channels), :] = (
            silu_and_slope(act, keep)
        )
    for i in range(2):
        res_ref[rows(i, 1, channels), :] = conv_row(w2_ref, hid_top, i, channels)
        res_ref[rows(2 + i, 1, channels), :] = conv_row(w2_ref, hid_bottom, i, channels)
    stack_backward(raw1_ref, w1t_ref, col1_ref)
    stack_backward(raw2_ref, w2t_ref, col2_ref)


def direct_job(span, m, ref):
    p, _, _ = place_in_plane(span)
    return span + lax.bitwise_xor(p, m) - p, ref


def relayed_job(span, m, ref):
    p, _, _ = place_in_plane(span)
    step = lax.bitwise_xor(p, m) - p
    return jnp.where(step > 0, step, 2 * span + step), ref


def early_jobs(span, own_ref, za_ref, zb_ref, near_ref, far_refs):
    p, z_odd, _ = place_in_plane(span)
    jobs = [
        (span, own_ref),
        (jnp.where(z_odd == 1, 0, 2 * span), za_ref.at[p]),
        (jnp.where(z_odd == 1, 2 * span, 0), zb_ref.at[p]),
        direct_job(span, 1, near_ref.at[0]),
        relayed_job(span, 1, near_ref.at[1]),
    ]
    return jobs + [direct_job(span, m, ref) for m, ref in enumerate(far_refs, 2)]


def late_jobs(span, far_refs):
    return [relayed_job(span, m, ref) for m, ref in enumerate(far_refs, 2)]


def tile_terms(jobs, route_ref, xt_ref, inner_ref, edge_ref, obs_weight, channels, height, columns):
    slots = BLK_LON
    across, down = columns // BLK_LON, height // BLK_LAT
    places, blocks = [], []
    for k, _ in jobs:
        n = route_ref[0, k]
        r, q = n // across, n % across
        inside = (r > 0) & (r < down - 1)
        lanes = pl.ds(pl.multiple_of(q * BLK_LON, BLK_LON), BLK_LON)
        block = []
        for i in range(BLK_LAT):
            row_in = jnp.clip(r * BLK_LAT + i - HALO, 0, height - 2 * HALO - 1)
            row_edge = jnp.where(r == 0, i, HALO + i)
            res = jnp.where(
                inside,
                inner_ref[rows(row_in, 1, channels), lanes],
                edge_ref[rows(row_edge, 1, channels), lanes],
            )
            here = (rows(r * BLK_LAT + i, 1, channels), lanes)
            block.append((xt_ref[here].astype(F32) + res).astype(BF16))
        places.append((r, lanes))
        blocks.append(block)
    misfits = []
    for (_, ref), block in zip(jobs, blocks):
        predicted = jnp.zeros((channels, slots), F32)
        for i in range(BLK_LAT):
            predicted += lax.dot_general(
                block[i],
                ref[i * slots : (i + 1) * slots, :],
                (((1,), (1,)), ((), ())),
                preferred_element_type=F32,
            )
        obs = ref[BLK_LAT * slots : BLK_LAT * slots + channels, :].astype(F32)
        misfits.append(((obs - predicted) * obs_weight).astype(BF16))
    terms = [
        [
            jnp.dot(misfit, ref[i * slots : (i + 1) * slots, :], preferred_element_type=F32).astype(BF16)
            for i in range(BLK_LAT)
        ]
        for (_, ref), misfit in zip(jobs, misfits)
    ]
    return places, terms


def early_tile_kernel(
    channels, height, columns, span,
    route_hbm, xt_ref, inner_ref, edge_ref, ow_ref, own_ref, za_ref, zb_ref, near_ref, *refs,
):
    far_refs, (guide_ref, route_ref, sem) = refs[: span - 2], refs[span - 2 :]
    copy = pltpu.make_async_copy(route_hbm, route_ref, sem)
    copy.start()
    guide_ref[...] = jnp.zeros_like(guide_ref)
    copy.wait()
    jobs = early_jobs(span, own_ref, za_ref, zb_ref, near_ref, far_refs)
    places, terms = tile_terms(
        jobs, route_ref, xt_ref, inner_ref, edge_ref, as_column(ow_ref[...]), channels, height, columns
    )
    for (r, lanes), term in zip(places, terms):
        for i in range(BLK_LAT):
            guide_ref[rows(r * BLK_LAT + i, 1, channels), lanes] += term[i].astype(F32)


def late_tile_kernel(
    channels, height, columns, span,
    route_ref, xt_ref, inner_ref, edge_ref, ow_ref, guide_ref, *refs,
):
    far_refs, (late_ref, ga_ref, gb_ref, sums, low) = refs[: span - 2], refs[span - 2 :]
    edge = HALO * channels
    last = (height - HALO) * channels
    sums[0:edge, :] = guide_ref[0:edge, :]
    sums[edge : 2 * edge, :] = guide_ref[last : last + edge, :]
    jobs = late_jobs(span, far_refs)
    places, terms = tile_terms(
        jobs, route_ref, xt_ref, inner_ref, edge_ref, as_column(ow_ref[...]), channels, height, columns
    )
    down = height // BLK_LAT
    for index, ((r, lanes), term) in enumerate(zip(places, terms)):
        part = jnp.where(r == 0, 0, jnp.where(r == down - 1, 1, 2))
        for i in range(BLK_LAT):
            late_ref[index, i] = term[i]
            sums[rows(part * HALO + i, 1, channels), lanes] += term[i].astype(F32)
    low[...] = sums[0 : 2 * edge, :].astype(BF16)
    second_rows(low, gb_ref, 2 * HALO, channels)
    first_rows(low, ga_ref, 2 * HALO, channels)


def backward_inner_kernel(
    channels, height, columns, span,
    route_ref, early_ref, late_ref, slope_ref, inner_ref, edge_ref, prior_ref, w2_ref, w1_ref,
    part_adj_ref, part_score_ref, score_ref,
    guide, low, adj,
):
    guide[...] = early_ref[...]
    across = columns // BLK_LON
    jobs = late_jobs(span, [late_ref] * (span - 2))
    for index, (k, _) in enumerate(jobs):
        n = route_ref[0, k]
        lanes = pl.ds(pl.multiple_of((n % across) * BLK_LON, BLK_LON), BLK_LON)
        for i in range(BLK_LAT):
            here = (rows((n // across) * BLK_LAT + i, 1, channels), lanes)
            guide[here] += late_ref[index, i].astype(F32)
    edge = HALO * channels
    none = jnp.zeros((edge, columns), BF16)
    low[0:edge, :] = none
    low[edge : edge + height * channels, :] = guide[...].astype(BF16)
    low[edge + height * channels :, :] = none
    adj[0:edge, :] = none
    adj[height * channels :, :] = none
    for i in range(height + 2):
        part = conv_row(w2_ref, low, i, channels)
        if HALO <= i < height:
            adj[rows(i, 1, channels), :] = (slope_ref[rows(i - HALO, 1, channels), :] * part).astype(BF16)
        else:
            part_adj_ref[rows(i if i < HALO else i - height + HALO, 1, channels), :] = part
    prior = as_column(prior_ref[...])
    for i in range(height):
        part = conv_row(w1_ref, adj, i, channels) + guide[rows(i, 1, channels), :]
        if HALO <= i < height - HALO:
            here = rows(i - HALO, 1, channels)
            score_ref[here, :] = (prior * inner_ref[here, :] + part).astype(BF16)
        else:
            here = rows(i if i < HALO else i - height + 2 * HALO, 1, channels)
            part_score_ref[here, :] = prior * edge_ref[here, :] + part


def backward_edge_kernel(
    channels, height,
    a_ref, b_ref, slope_ref, part_adj_ref, part_score_ref, score_ref,
    w2_ref, w1_ref,
    out_hbm,
    out_ref, edge_ref, sems,
):
    odd = lax.axis_index("lat") % 2
    a, b = a_ref[...], b_ref[...]
    adjoint = []
    for at, window, above in ((0, jnp.where(odd == 1, a, b), True), (HALO, jnp.where(odd == 1, b, a), False)):
        here = [rows(at + i, 1, channels) for i in range(HALO)]
        share = halo_share(w2_ref, window[:channels], window[channels:], above, channels)
        rows_here = [
            (slope_ref[place, :] * (part_adj_ref[place, :] + back)).astype(BF16)
            for place, back in zip(here, share)
        ]
        adjoint.append((here, rows_here, above))
    for here, adj, above in adjoint:
        for place, back in zip(here, halo_share(w1_ref, adj[0], adj[1], above, channels)):
            edge_ref[place, :] = (part_score_ref[place, :] + back).astype(BF16)
    copies = []
    for start, size in channel_groups(channels):
        n = size * height
        picked = []
        for r in range(height):
            if r < HALO:
                src, at = edge_ref, r
            elif r < height - HALO:
                src, at = score_ref, r - HALO
            else:
                src, at = edge_ref, r - height + 2 * HALO
            picked.append(src[at * channels + start : at * channels + start + size, :])
        part = pl.ds(start * height, n)
        out_ref[part, :] = jnp.dot(
            permutation(height, size, True), jnp.concatenate(picked, axis=0), preferred_element_type=F32
        ).astype(BF16)
        copies.append(pltpu.make_async_copy(out_ref.at[part], out_hbm.at[part], sems.at[len(copies)]))
        copies[-1].start()
    for copy in copies:
        copy.wait()


def pairs(groups, count, partner):
    found = []
    for g in range(groups):
        for i in range(count):
            other = partner(i)
            if 0 <= other < count:
                found.append((g * count + i, g * count + other))
            elif groups % 2 == 0:
                found.append((g * count + i, (g ^ 1) * count + i))
    return found


def local(
    noisy_state, w_first, w_second, prior_weight, obs_weight, block_route, counts, tile_weights, observations
):
    channels, height, columns = noisy_state.shape
    tile_total = block_route.shape[1]
    span = tile_total // 2
    slots = tile_weights.shape[2]
    count = lax.axis_size("lat")
    pack_rows = BLK_LAT * slots + channels
    taps = w_first.shape[0]

    def field(n, dtype=BF16):
        return shape((n * channels, columns), dtype)

    def buffer(n, dtype=BF16):
        return pltpu.VMEM((n * channels, columns), dtype)

    def exchange(x, partner):
        return lax.ppermute(x, ("grp", "lat"), pairs(lax.axis_size("grp"), count, partner))

    def swap(x, step, parity):
        return exchange(x, lambda i: i + step if (i // step) % 2 == parity else i - step)

    packed = shape((span, pack_rows, BLK_LON))
    def in_hbm(x):
        return pltpu.with_memory_space_constraint(x, pltpu.HBM)

    tile = shape((pack_rows, BLK_LON))
    za_send, zb_send, own, near, *far, x = pl.pallas_call(
        functools.partial(pack_kernel, channels, span),
        out_shape=(packed, packed) + (tile,) * span + (field(height),),
        in_specs=[HB] * 4,
        out_specs=[VM] * (3 + span),
        scratch_shapes=[
            pltpu.SMEM(counts.shape, jnp.int32),
            pltpu.VMEM(tile_weights.shape[1:], BF16),
            pltpu.VMEM(observations.shape[1:], BF16),
            pltpu.SemaphoreType.DMA((4,)),
        ],
        compiler_params=params(),
    )(
        in_hbm(counts),
        in_hbm(tile_weights),
        in_hbm(observations),
        in_hbm(noisy_state.reshape(channels * height, columns)),
    )
    za, zb = swap(za_send, span, 0), swap(zb_send, span, 1)
    far = [exchange(buf, lambda i, m=m: i ^ m) for m, buf in enumerate(far, 2)]
    xt, hb = pl.pallas_call(
        functools.partial(prepare_kernel, channels, height),
        out_shape=(field(height), field(HALO)),
        in_specs=[VM, AN],
        out_specs=[VM] * 2,
        compiler_params=params(),
    )(x, za_send)
    hb = swap(hb, 1, 1)

    weight = shape((taps * channels, taps * channels))
    hid, slope_in, res_in, w1, w2, ha = pl.pallas_call(
        functools.partial(forward_inner_kernel, channels, height),
        out_shape=(
            field(height - 2),
            field(height - 2, F32),
            field(height - 4, F32),
            weight,
            weight,
            field(HALO),
        ),
        in_specs=[VM] * 3 + [AN] * len(far),
        out_specs=[VM] * 6,
        compiler_params=params(),
    )(xt, w_first, w_second, *far)
    ha = swap(ha, 1, 0)

    relayed = pl.pallas_call(
        functools.partial(relay_kernel, span),
        out_shape=(shape((2, pack_rows, BLK_LON)),) + (tile,) * (span - 2),
        in_specs=[VM] * 3 + [AN],
        out_specs=[VM] * (span - 1),
        compiler_params=params(),
    )(za, zb, near, w1)
    near, *last = [exchange(buf, lambda i, m=m: i ^ m) for m, buf in enumerate(relayed, 1)]

    slope_ed, res_ed, w1t, w2t, col1, col2 = pl.pallas_call(
        functools.partial(forward_edge_kernel, channels, height),
        out_shape=(field(2 * HALO, F32), field(2 * HALO, F32)) + (weight,) * 4,
        in_specs=[VM] * 8,
        out_specs=[VM] * 6,
        scratch_shapes=[buffer(2 * HALO)] * 4,
        compiler_params=params(),
    )(xt, ha, hb, hid, w1, w2, w_first, w_second)

    observed = obs_weight[None, :]
    early = pl.pallas_call(
        functools.partial(early_tile_kernel, channels, height, columns, span),
        out_shape=field(height, F32),
        in_specs=[HB] + [VM] * (8 + span - 2),
        out_specs=VM,
        scratch_shapes=[pltpu.SMEM(block_route.shape, jnp.int32), pltpu.SemaphoreType.DMA],
        compiler_params=params(),
    )(in_hbm(block_route), xt, res_in, res_ed, observed, own, za, zb, near, *far)

    late, ga, gb = pl.pallas_call(
        functools.partial(late_tile_kernel, channels, height, columns, span),
        out_shape=(
            shape((span - 2, BLK_LAT, channels, BLK_LON)),
            field(HALO),
            field(HALO),
        ),
        in_specs=[SM] + [VM] * (5 + span - 2),
        out_specs=[VM] * 3,
        scratch_shapes=[buffer(3 * HALO, F32), buffer(2 * HALO)],
        compiler_params=params(),
    )(block_route, xt, res_in, res_ed, observed, early, *last)
    gb, ga = swap(gb, 1, 1), swap(ga, 1, 0)

    part_adj, part_score, score = pl.pallas_call(
        functools.partial(backward_inner_kernel, channels, height, columns, span),
        out_shape=(field(2 * HALO, F32), field(2 * HALO, F32), field(height - 2 * HALO)),
        in_specs=[SM] + [VM] * 8,
        out_specs=[VM] * 3,
        scratch_shapes=[buffer(height, F32), buffer(height + 2 * HALO), buffer(height + 2)],
        compiler_params=params(),
    )(block_route, early, late, slope_in, res_in, res_ed, prior_weight[None, :], w2t, w1t)

    out = pl.pallas_call(
        functools.partial(backward_edge_kernel, channels, height),
        out_shape=shape((channels * height, columns)),
        in_specs=[VM] * 8,
        out_specs=HB,
        scratch_shapes=[
            buffer(height),
            buffer(2 * HALO),
            pltpu.SemaphoreType.DMA((len(channel_groups(channels)),)),
        ],
        compiler_params=params(),
    )(ga, gb, slope_ed, part_adj, part_score, score, col2, col1)
    return out.reshape(channels, height, columns)


def solution(mesh):
    in_specs = (
        P("grp", "lat", None),
        P(),
        P(),
        P(),
        P(),
        P(("grp", "lat"), None),
        P(("grp", "lat"), None),
        P(("grp", "lat"), None, None, None),
        P(("grp", "lat"), None, None, None),
    )
    out_specs = P("grp", "lat", None)
    return jax.shard_map(local, mesh=mesh, in_specs=in_specs, out_specs=out_specs, check_vma=False)
```

```python
import functools

import jax
import jax.numpy as jnp
from jax import lax
from jax.experimental import pallas as pl
from jax.experimental.pallas import tpu as pltpu
from jax.sharding import PartitionSpec as P

BLK_LAT = 2
BLK_LON = 128
HALO = 2
F32 = jnp.float32
BF16 = jnp.bfloat16

VM = pl.BlockSpec(memory_space=pltpu.VMEM)
SM = pl.BlockSpec(memory_space=pltpu.SMEM)
HB = pl.BlockSpec(memory_space=pltpu.HBM)
AN = pl.BlockSpec(memory_space=pl.ANY)


def params(mib=16):
    return pltpu.CompilerParams(vmem_limit_bytes=mib << 20)


def shape(dims, dtype=BF16):
    return jax.ShapeDtypeStruct(dims, dtype)


def rows(index, count, channels):
    start = index * channels
    if not isinstance(start, int):
        start = pl.multiple_of(start, 16)
    return pl.ds(start, count * channels)


def permutation(height, group, back):
    n = height * group
    out = lax.broadcasted_iota(jnp.int32, (n, n), 0)
    src = lax.broadcasted_iota(jnp.int32, (n, n), 1)
    if back:
        want = (out % height) * group + out // height
    else:
        want = (out % group) * height + out // group
    return jnp.where(src == want, 1.0, 0.0).astype(BF16)


def channel_groups(channels):
    return [(start, min(32, channels - start)) for start in range(0, channels, 32)]


def as_column(row):
    n = row.shape[1]
    here = lax.broadcasted_iota(jnp.int32, (n, n), 0) == lax.broadcasted_iota(jnp.int32, (n, n), 1)
    return jnp.sum(jnp.where(here, jnp.broadcast_to(row, (n, n)), 0.0), axis=1, keepdims=True)


def place_in_plane(span):
    me = lax.axis_index("lat")
    return me % span, (me // span) % 2, me % 2


def pack_tile(k, dst, w_ref, obs_ref, count_ref, slots, channels):
    live = lax.broadcasted_iota(jnp.int32, (slots, BLK_LON), 0) < count_ref[0, k]
    zero = jnp.zeros((slots, BLK_LON), BF16)
    for i in range(BLK_LAT):
        half = w_ref[k, :, i * BLK_LON : (i + 1) * BLK_LON]
        dst[i * slots : (i + 1) * slots, :] = jnp.where(live, half, zero)
    dst[BLK_LAT * slots : BLK_LAT * slots + channels, :] = obs_ref[k]


def first_rows(src_ref, dst, height, channels):
    odd = lax.axis_index("lat") % 2
    dst[...] = src_ref[rows((height - HALO) * (1 - odd), HALO, channels), :]


def second_rows(src_ref, dst, height, channels):
    me, odd = lax.axis_index("lat"), lax.axis_index("lat") % 2
    alone = (me == 0) | (me == lax.axis_size("lat") - 1)

    @pl.when(alone)
    def _():
        dst[...] = jnp.zeros_like(dst)

    @pl.when(jnp.logical_not(alone))
    def _():
        dst[...] = src_ref[rows((height - HALO) * odd, HALO, channels), :]


def pack_kernel(
    channels, span,
    count_hbm, w_hbm, obs_hbm, x_hbm,
    za_ref, zb_ref, own_ref, near_ref, y2_ref, y3_ref, x_ref,
    count_ref, w_ref, obs_ref, sems,
):
    copies = [
        pltpu.make_async_copy(count_hbm, count_ref, sems.at[0]),
        pltpu.make_async_copy(w_hbm.at[0], w_ref, sems.at[1]),
        pltpu.make_async_copy(obs_hbm.at[0], obs_ref, sems.at[2]),
        pltpu.make_async_copy(x_hbm, x_ref, sems.at[3]),
    ]
    for copy in copies:
        copy.start()
    for copy in copies[:3]:
        copy.wait()
    p, z_odd, _ = place_in_plane(span)
    slots = w_ref.shape[1]
    pack = functools.partial(
        pack_tile, w_ref=w_ref, obs_ref=obs_ref, count_ref=count_ref, slots=slots, channels=channels
    )
    for j in range(span):
        up = jnp.maximum(p - j, 0)
        down = jnp.minimum(2 * span + p - j, 2 * span)
        pack(jnp.where(z_odd == 1, down, up), za_ref.at[j])
        pack(jnp.where(z_odd == 1, up, down), zb_ref.at[j])
    pack(span, own_ref)
    for j, dst in enumerate((near_ref, y2_ref, y3_ref), 1):
        pack(span + p - lax.bitwise_xor(p, j), dst)
    copies[3].wait()


def prepare_kernel(channels, height, x_ref, after_ref, xt_ref, hb_ref):
    for start, size in channel_groups(channels):
        n = size * height
        moved = jnp.dot(
            permutation(height, size, False),
            x_ref[start * height : start * height + n, :],
            preferred_element_type=F32,
        ).astype(BF16)
        for r in range(height):
            xt_ref[r * channels + start : r * channels + start + size, :] = (
                moved[r * size : (r + 1) * size, :]
            )
    second_rows(xt_ref, hb_ref, height, channels)


def relay_kernel(span, za_ref, zb_ref, near_ref, *refs):
    near_out, *far_outs = refs[-span + 1 :]
    p, z_odd, _ = place_in_plane(span)
    near_out[0] = near_ref[...]
    for m, out in enumerate([near_out.at[1]] + far_outs, 1):
        to = lax.bitwise_xor(p, m)
        below = jnp.where(to < p, 1, 0)

        @pl.when(below == z_odd)
        def _():
            out[...] = za_ref[to]

        @pl.when(below != z_odd)
        def _():
            out[...] = zb_ref[to]


def stack_forward(raw_ref, dst):
    taps, _, outs, ins = raw_ref.shape
    total = jnp.zeros(dst.shape, F32)
    for a in range(taps):
        block = raw_ref[a].reshape(taps * outs, ins)
        to = lax.broadcasted_iota(jnp.int32, (ins, taps * ins), 1)
        pick = jnp.where(to == lax.broadcasted_iota(jnp.int32, to.shape, 0) + a * ins, 1.0, 0.0)
        total += jnp.dot(block, pick.astype(BF16), preferred_element_type=F32)
    dst[...] = total.astype(BF16)


def stack_backward(raw_ref, by_row_ref, by_column_ref):
    taps, _, outs, ins = raw_ref.shape
    n = taps * outs
    here = lax.broadcasted_iota(jnp.int32, (n, n), 0) == lax.broadcasted_iota(jnp.int32, (n, n), 1)
    same = jnp.where(here, 1.0, 0.0).astype(BF16)
    end = taps - 1
    for i in range(taps):
        by_row = jnp.concatenate([raw_ref[end - j, end - i] for j in range(taps)], axis=0)
        by_column = jnp.concatenate([raw_ref[i, end - j] for j in range(taps)], axis=0)
        for block, dst in ((by_row, by_row_ref), (by_column, by_column_ref)):
            dst[i * ins : (i + 1) * ins, :] = lax.dot_general(
                block, same, (((0,), (0,)), ((), ())), preferred_element_type=F32
            ).astype(BF16)


def join_taps(taps, channels):
    width = taps.shape[1]
    return (
        pltpu.roll(taps[0:channels], 1, 1)
        + taps[channels : 2 * channels]
        + pltpu.roll(taps[2 * channels : 3 * channels], width - 1, 1)
    )


def conv_row(w_ref, src_ref, index, channels):
    window = src_ref[rows(index, 3, channels), :]
    return join_taps(jnp.dot(w_ref[...], window, preferred_element_type=F32), channels)


def shifted(row):
    return jnp.concatenate([pltpu.roll(row, 1, 1), row, pltpu.roll(row, row.shape[1] - 1, 1)], axis=0)


def halo_share(w_ref, first, second, above, channels):
    near, far = (second, first) if above else (first, second)
    start = channels if above else 0
    near = jnp.dot(w_ref[start : start + 2 * channels, :], shifted(near), preferred_element_type=F32)
    start = 2 * channels if above else 0
    far = jnp.dot(w_ref[start : start + channels, :], shifted(far), preferred_element_type=F32)
    if above:
        return near[:channels] + far, near[channels:]
    return near[:channels], near[channels:] + far


def silu_and_slope(act, keep=None):
    gate = 0.5 * jnp.tanh(0.5 * act) + 0.5
    if keep is not None:
        gate = gate * keep
    hidden = act * gate
    return hidden.astype(BF16), gate * (1.0 + act - hidden)


def ext_edges(channels, height, mid_ref, a_ref, b_ref, top, bottom, odd):
    edge = HALO * channels
    top[edge : 2 * edge, :] = mid_ref[0:edge, :]
    bottom[0:edge, :] = mid_ref[(height - HALO) * channels : height * channels, :]

    @pl.when(odd == 1)
    def _():
        top[0:edge, :] = a_ref[...]
        bottom[edge : 2 * edge, :] = b_ref[...]

    @pl.when(odd == 0)
    def _():
        top[0:edge, :] = b_ref[...]
        bottom[edge : 2 * edge, :] = a_ref[...]


def forward_inner_kernel(
    channels, height,
    xt_ref, raw1_ref, raw2_ref, after2_ref, after3_ref,
    hid_ref, slope_ref, res_ref, w1_ref, w2_ref, ha_ref,
):
    first_rows(xt_ref, ha_ref, height, channels)
    stack_forward(raw1_ref, w1_ref)
    stack_forward(raw2_ref, w2_ref)
    for i in range(height - 2):
        act = conv_row(w1_ref, xt_ref, i, channels)
        hid_ref[rows(i, 1, channels), :], slope_ref[rows(i, 1, channels), :] = silu_and_slope(act)
    for i in range(height - 4):
        res_ref[rows(i, 1, channels), :] = conv_row(w2_ref, hid_ref, i, channels)


def on_grid():
    me = lax.axis_index("lat")
    count = lax.axis_size("lat")
    return jnp.where(me == 0, 0.0, 1.0), jnp.where(me == count - 1, 0.0, 1.0)


def forward_edge_kernel(
    channels, height,
    xt_ref, a_ref, b_ref, hid_ref, w1_ref, w2_ref, raw1_ref, raw2_ref,
    slope_ref, res_ref, w1t_ref, w2t_ref, col1_ref, col2_ref,
    top, bottom, hid_top, hid_bottom,
):
    odd = lax.axis_index("lat") % 2
    ext_edges(channels, height, xt_ref, a_ref, b_ref, top, bottom, odd)
    has_above, has_below = on_grid()
    inner = (height - 2 - HALO) * channels
    hid_top[2 * channels : 4 * channels, :] = hid_ref[0 : 2 * channels, :]
    hid_bottom[0 : 2 * channels, :] = hid_ref[inner : inner + 2 * channels, :]
    for i, keep in ((0, has_above), (1, None)):
        act = conv_row(w1_ref, top, i, channels)
        hid_top[rows(i, 1, channels), :], slope_ref[rows(i, 1, channels), :] = silu_and_slope(act, keep)
    for i, keep in ((0, None), (1, has_below)):
        act = conv_row(w1_ref, bottom, i, channels)
        hid_bottom[rows(2 + i, 1, channels), :], slope_ref[rows(2 + i, 1, channels), :] = (
            silu_and_slope(act, keep)
        )
    for i in range(2):
        res_ref[rows(i, 1, channels), :] = conv_row(w2_ref, hid_top, i, channels)
        res_ref[rows(2 + i, 1, channels), :] = conv_row(w2_ref, hid_bottom, i, channels)
    stack_backward(raw1_ref, w1t_ref, col1_ref)
    stack_backward(raw2_ref, w2t_ref, col2_ref)


def direct_job(span, m, ref):
    p, _, _ = place_in_plane(span)
    return span + lax.bitwise_xor(p, m) - p, ref


def relayed_job(span, m, ref):
    p, _, _ = place_in_plane(span)
    step = lax.bitwise_xor(p, m) - p
    return jnp.where(step > 0, step, 2 * span + step), ref


def early_jobs(span, own_ref, za_ref, zb_ref, far_refs):
    p, z_odd, _ = place_in_plane(span)
    jobs = [
        (span, own_ref),
        (jnp.where(z_odd == 1, 0, 2 * span), za_ref.at[p]),
        (jnp.where(z_odd == 1, 2 * span, 0), zb_ref.at[p]),
    ]
    return jobs + [direct_job(span, m, ref) for m, ref in enumerate(far_refs, 2)]


def late_jobs(span, near_ref, far_refs):
    near = [direct_job(span, 1, near_ref.at[0]), relayed_job(span, 1, near_ref.at[1])]
    return near + [relayed_job(span, m, ref) for m, ref in enumerate(far_refs, 2)]


def tile_terms(jobs, route_ref, xt_ref, inner_ref, edge_ref, obs_weight, channels, height, columns):
    slots = BLK_LON
    across, down = columns // BLK_LON, height // BLK_LAT
    places, blocks = [], []
    for k, _ in jobs:
        n = route_ref[0, k]
        r, q = n // across, n % across
        inside = (r > 0) & (r < down - 1)
        lanes = pl.ds(pl.multiple_of(q * BLK_LON, BLK_LON), BLK_LON)
        block = []
        for i in range(BLK_LAT):
            row_in = jnp.clip(r * BLK_LAT + i - HALO, 0, height - 2 * HALO - 1)
            row_edge = jnp.where(r == 0, i, HALO + i)
            res = jnp.where(
                inside,
                inner_ref[rows(row_in, 1, channels), lanes],
                edge_ref[rows(row_edge, 1, channels), lanes],
            )
            here = (rows(r * BLK_LAT + i, 1, channels), lanes)
            block.append((xt_ref[here].astype(F32) + res).astype(BF16))
        places.append((r, lanes))
        blocks.append(block)
    misfits = []
    for (_, ref), block in zip(jobs, blocks):
        predicted = jnp.zeros((channels, slots), F32)
        for i in range(BLK_LAT):
            predicted += lax.dot_general(
                block[i],
                ref[i * slots : (i + 1) * slots, :],
                (((1,), (1,)), ((), ())),
                preferred_element_type=F32,
            )
        obs = ref[BLK_LAT * slots : BLK_LAT * slots + channels, :].astype(F32)
        misfits.append(((obs - predicted) * obs_weight).astype(BF16))
    terms = [
        [
            jnp.dot(misfit, ref[i * slots : (i + 1) * slots, :], preferred_element_type=F32).astype(BF16)
            for i in range(BLK_LAT)
        ]
        for (_, ref), misfit in zip(jobs, misfits)
    ]
    return places, terms


def early_tile_kernel(
    channels, height, columns, span,
    route_hbm, xt_ref, inner_ref, edge_ref, ow_ref, own_ref, za_ref, zb_ref, *refs,
):
    far_refs, (guide_ref, route_ref, sem) = refs[: span - 2], refs[span - 2 :]
    copy = pltpu.make_async_copy(route_hbm, route_ref, sem)
    copy.start()
    guide_ref[...] = jnp.zeros_like(guide_ref)
    copy.wait()
    jobs = early_jobs(span, own_ref, za_ref, zb_ref, far_refs)
    places, terms = tile_terms(
        jobs, route_ref, xt_ref, inner_ref, edge_ref, as_column(ow_ref[...]), channels, height, columns
    )
    for (r, lanes), term in zip(places, terms):
        for i in range(BLK_LAT):
            guide_ref[rows(r * BLK_LAT + i, 1, channels), lanes] += term[i].astype(F32)


def late_tile_kernel(
    channels, height, columns, span,
    route_ref, xt_ref, inner_ref, edge_ref, ow_ref, guide_ref, *refs,
):
    near_ref, *far_refs = refs[: span - 1]
    late_ref, ga_ref, gb_ref, sums, low = refs[span - 1 :]
    edge = HALO * channels
    last = (height - HALO) * channels
    sums[0:edge, :] = guide_ref[0:edge, :]
    sums[edge : 2 * edge, :] = guide_ref[last : last + edge, :]
    jobs = late_jobs(span, near_ref, far_refs)
    places, terms = tile_terms(
        jobs, route_ref, xt_ref, inner_ref, edge_ref, as_column(ow_ref[...]), channels, height, columns
    )
    down = height // BLK_LAT
    for index, ((r, lanes), term) in enumerate(zip(places, terms)):
        part = jnp.where(r == 0, 0, jnp.where(r == down - 1, 1, 2))
        for i in range(BLK_LAT):
            late_ref[index, i] = term[i]
            sums[rows(part * HALO + i, 1, channels), lanes] += term[i].astype(F32)
    low[...] = sums[0 : 2 * edge, :].astype(BF16)
    second_rows(low, gb_ref, 2 * HALO, channels)
    first_rows(low, ga_ref, 2 * HALO, channels)


def backward_inner_kernel(
    channels, height, columns, span,
    route_ref, early_ref, late_ref, slope_ref, inner_ref, edge_ref, prior_ref, w2_ref, w1_ref,
    part_adj_ref, part_score_ref, score_ref,
    guide, low, adj,
):
    guide[...] = early_ref[...]
    across = columns // BLK_LON
    jobs = late_jobs(span, late_ref, [late_ref] * (span - 2))
    for index, (k, _) in enumerate(jobs):
        n = route_ref[0, k]
        lanes = pl.ds(pl.multiple_of((n % across) * BLK_LON, BLK_LON), BLK_LON)
        for i in range(BLK_LAT):
            here = (rows((n // across) * BLK_LAT + i, 1, channels), lanes)
            guide[here] += late_ref[index, i].astype(F32)
    edge = HALO * channels
    none = jnp.zeros((edge, columns), BF16)
    low[0:edge, :] = none
    low[edge : edge + height * channels, :] = guide[...].astype(BF16)
    low[edge + height * channels :, :] = none
    adj[0:edge, :] = none
    adj[height * channels :, :] = none
    for i in range(height + 2):
        part = conv_row(w2_ref, low, i, channels)
        if HALO <= i < height:
            adj[rows(i, 1, channels), :] = (slope_ref[rows(i - HALO, 1, channels), :] * part).astype(BF16)
        else:
            part_adj_ref[rows(i if i < HALO else i - height + HALO, 1, channels), :] = part
    prior = as_column(prior_ref[...])
    for i in range(height):
        part = conv_row(w1_ref, adj, i, channels) + guide[rows(i, 1, channels), :]
        if HALO <= i < height - HALO:
            here = rows(i - HALO, 1, channels)
            score_ref[here, :] = (prior * inner_ref[here, :] + part).astype(BF16)
        else:
            here = rows(i if i < HALO else i - height + 2 * HALO, 1, channels)
            part_score_ref[here, :] = prior * edge_ref[here, :] + part


def backward_edge_kernel(
    channels, height,
    a_ref, b_ref, slope_ref, part_adj_ref, part_score_ref, score_ref,
    w2_ref, w1_ref,
    out_hbm,
    out_ref, edge_ref, sems,
):
    odd = lax.axis_index("lat") % 2
    a, b = a_ref[...], b_ref[...]
    adjoint = []
    for at, window, above in ((0, jnp.where(odd == 1, a, b), True), (HALO, jnp.where(odd == 1, b, a), False)):
        here = [rows(at + i, 1, channels) for i in range(HALO)]
        share = halo_share(w2_ref, window[:channels], window[channels:], above, channels)
        rows_here = [
            (slope_ref[place, :] * (part_adj_ref[place, :] + back)).astype(BF16)
            for place, back in zip(here, share)
        ]
        adjoint.append((here, rows_here, above))
    for here, adj, above in adjoint:
        for place, back in zip(here, halo_share(w1_ref, adj[0], adj[1], above, channels)):
            edge_ref[place, :] = (part_score_ref[place, :] + back).astype(BF16)
    copies = []
    for start, size in channel_groups(channels):
        n = size * height
        picked = []
        for r in range(height):
            if r < HALO:
                src, at = edge_ref, r
            elif r < height - HALO:
                src, at = score_ref, r - HALO
            else:
                src, at = edge_ref, r - height + 2 * HALO
            picked.append(src[at * channels + start : at * channels + start + size, :])
        part = pl.ds(start * height, n)
        out_ref[part, :] = jnp.dot(
            permutation(height, size, True), jnp.concatenate(picked, axis=0), preferred_element_type=F32
        ).astype(BF16)
        copies.append(pltpu.make_async_copy(out_ref.at[part], out_hbm.at[part], sems.at[len(copies)]))
        copies[-1].start()
    for copy in copies:
        copy.wait()


def pairs(groups, count, partner):
    found = []
    for g in range(groups):
        for i in range(count):
            other = partner(i)
            if 0 <= other < count:
                found.append((g * count + i, g * count + other))
            elif groups % 2 == 0:
                found.append((g * count + i, (g ^ 1) * count + i))
    return found


def local(
    noisy_state, w_first, w_second, prior_weight, obs_weight, block_route, counts, tile_weights, observations
):
    channels, height, columns = noisy_state.shape
    tile_total = block_route.shape[1]
    span = tile_total // 2
    slots = tile_weights.shape[2]
    count = lax.axis_size("lat")
    pack_rows = BLK_LAT * slots + channels
    taps = w_first.shape[0]

    def field(n, dtype=BF16):
        return shape((n * channels, columns), dtype)

    def buffer(n, dtype=BF16):
        return pltpu.VMEM((n * channels, columns), dtype)

    def exchange(x, partner):
        return lax.ppermute(x, ("grp", "lat"), pairs(lax.axis_size("grp"), count, partner))

    def swap(x, step, parity):
        return exchange(x, lambda i: i + step if (i // step) % 2 == parity else i - step)

    packed = shape((span, pack_rows, BLK_LON))
    def in_hbm(x):
        return pltpu.with_memory_space_constraint(x, pltpu.HBM)

    tile = shape((pack_rows, BLK_LON))
    za_send, zb_send, own, near, *far, x = pl.pallas_call(
        functools.partial(pack_kernel, channels, span),
        out_shape=(packed, packed) + (tile,) * span + (field(height),),
        in_specs=[HB] * 4,
        out_specs=[VM] * (3 + span),
        scratch_shapes=[
            pltpu.SMEM(counts.shape, jnp.int32),
            pltpu.VMEM(tile_weights.shape[1:], BF16),
            pltpu.VMEM(observations.shape[1:], BF16),
            pltpu.SemaphoreType.DMA((4,)),
        ],
        compiler_params=params(),
    )(
        in_hbm(counts),
        in_hbm(tile_weights),
        in_hbm(observations),
        in_hbm(noisy_state.reshape(channels * height, columns)),
    )
    za, zb = swap(za_send, span, 0), swap(zb_send, span, 1)
    far = [exchange(buf, lambda i, m=m: i ^ m) for m, buf in enumerate(far, 2)]
    xt, hb = pl.pallas_call(
        functools.partial(prepare_kernel, channels, height),
        out_shape=(field(height), field(HALO)),
        in_specs=[VM, AN],
        out_specs=[VM] * 2,
        compiler_params=params(),
    )(x, za_send)
    hb = swap(hb, 1, 1)

    weight = shape((taps * channels, taps * channels))
    hid, slope_in, res_in, w1, w2, ha = pl.pallas_call(
        functools.partial(forward_inner_kernel, channels, height),
        out_shape=(
            field(height - 2),
            field(height - 2, F32),
            field(height - 4, F32),
            weight,
            weight,
            field(HALO),
        ),
        in_specs=[VM] * 3 + [AN] * len(far),
        out_specs=[VM] * 6,
        compiler_params=params(),
    )(xt, w_first, w_second, *far)
    ha = swap(ha, 1, 0)

    relayed = pl.pallas_call(
        functools.partial(relay_kernel, span),
        out_shape=(shape((2, pack_rows, BLK_LON)),) + (tile,) * (span - 2),
        in_specs=[VM] * 3 + [AN],
        out_specs=[VM] * (span - 1),
        compiler_params=params(),
    )(za, zb, near, w1)
    last = [exchange(relayed[m - 1], lambda i, m=m: i ^ m) for m in range(span - 1, 0, -1)][::-1]

    slope_ed, res_ed, w1t, w2t, col1, col2 = pl.pallas_call(
        functools.partial(forward_edge_kernel, channels, height),
        out_shape=(field(2 * HALO, F32), field(2 * HALO, F32)) + (weight,) * 4,
        in_specs=[VM] * 8,
        out_specs=[VM] * 6,
        scratch_shapes=[buffer(2 * HALO)] * 4,
        compiler_params=params(),
    )(xt, ha, hb, hid, w1, w2, w_first, w_second)

    observed = obs_weight[None, :]
    early = pl.pallas_call(
        functools.partial(early_tile_kernel, channels, height, columns, span),
        out_shape=field(height, F32),
        in_specs=[HB] + [VM] * (7 + span - 2),
        out_specs=VM,
        scratch_shapes=[pltpu.SMEM(block_route.shape, jnp.int32), pltpu.SemaphoreType.DMA],
        compiler_params=params(),
    )(in_hbm(block_route), xt, res_in, res_ed, observed, own, za, zb, *far)

    late, ga, gb = pl.pallas_call(
        functools.partial(late_tile_kernel, channels, height, columns, span),
        out_shape=(
            shape((span, BLK_LAT, channels, BLK_LON)),
            field(HALO),
            field(HALO),
        ),
        in_specs=[SM] + [VM] * (5 + span - 1),
        out_specs=[VM] * 3,
        scratch_shapes=[buffer(3 * HALO, F32), buffer(2 * HALO)],
        compiler_params=params(),
    )(block_route, xt, res_in, res_ed, observed, early, *last)
    gb, ga = swap(gb, 1, 1), swap(ga, 1, 0)

    part_adj, part_score, score = pl.pallas_call(
        functools.partial(backward_inner_kernel, channels, height, columns, span),
        out_shape=(field(2 * HALO, F32), field(2 * HALO, F32), field(height - 2 * HALO)),
        in_specs=[SM] + [VM] * 8,
        out_specs=[VM] * 3,
        scratch_shapes=[buffer(height, F32), buffer(height + 2 * HALO), buffer(height + 2)],
        compiler_params=params(),
    )(block_route, early, late, slope_in, res_in, res_ed, prior_weight[None, :], w2t, w1t)

    out = pl.pallas_call(
        functools.partial(backward_edge_kernel, channels, height),
        out_shape=shape((channels * height, columns)),
        in_specs=[VM] * 8,
        out_specs=HB,
        scratch_shapes=[
            buffer(height),
            buffer(2 * HALO),
            pltpu.SemaphoreType.DMA((len(channel_groups(channels)),)),
        ],
        compiler_params=params(),
    )(ga, gb, slope_ed, part_adj, part_score, score, col2, col1)
    return out.reshape(channels, height, columns)


def solution(mesh):
    in_specs = (
        P("grp", "lat", None),
        P(),
        P(),
        P(),
        P(),
        P(("grp", "lat"), None),
        P(("grp", "lat"), None),
        P(("grp", "lat"), None, None, None),
        P(("grp", "lat"), None, None, None),
    )
    out_specs = P("grp", "lat", None)
    return jax.shard_map(local, mesh=mesh, in_specs=in_specs, out_specs=out_specs, check_vma=False)
```
